32 devices in a mesh: gx: 4 (over x, core), gy: 4 (over z), gz: 2 (over y).
Axes of the slice: x: 2, y: 2, z: 4, core: 2. Of those that a mesh axis runs over, the one named last changes fastest.
Arguments:
- flow_adjoint: float32 [19, 64, 64, 256], P(None, 'gx', 'gy', 'gz'), may hold values from -6 to 6
- solute_adjoint: float32 [7, 64, 64, 256], P(None, 'gx', 'gy', 'gz'), may hold values from -6 to 6
- flow_density: bfloat16 [4, 64, 64, 256], P(None, 'gx', 'gy', 'gz'), may hold values from 0.796875 to 1.25
- flow_velocity: bfloat16 [4, 3, 64, 64, 256], P(None, None, 'gx', 'gy', 'gz'), may hold values from -0.119628906 to 0.119628906
- solute_level: bfloat16 [4, 64, 64, 256], P(None, 'gx', 'gy', 'gz'), may hold values from 0.099609375 to 3
- solid: int32 [64, 64, 256], P('gx', 'gy', 'gz'), may hold values 0 or 1
- owner: int32 [8], replicated, may hold values from 0 to 1, as said below
Outputs:
- flow_result: float32 [19, 64, 64, 256], P(None, 'gx', 'gy', 'gz')
- solute_result: float32 [7, 64, 64, 256], P(None, 'gx', 'gy', 'gz')
The draws below stay inside these ranges and needn't reach their ends.
Inputs may be any that keep to these rules, and one draw needn't show every extreme that they name: owner never falls along the list; every gz device holds 1 to 7 blocks.
All inputs are finite; a program needn't handle non-finite values. No bound on the sum of `solid` on one device may be relied on, other than what follows from the above.
Results may differ from the reference program's by a relative error of at most 0.0003.
Values sent between devices are 32-bit elements; how exact they have to be, the bound alone decides.
No kernel may reach another device: no remote copies, remote signals or barrier semaphores. Data moves between devices by JAX's collectives and lax.ppermute only.
A program may use at most 128 MiB of HBM per device.

```python
import math
import jax
import jax.numpy as jnp

BZC = 16
SLOTS = 8
STEPS = 4
LBLK = 8
NX = 64
NY = 64
NZ = 256
N_GZ = 2


def draw_owner(key, part):
    first_key, second_key = jax.random.split(jax.random.fold_in(key, 7))
    order = jax.random.permutation(first_key, N_GZ)
    moves = jax.random.randint(second_key, (N_GZ // 2,), 1, SLOTS).astype(jnp.int32)
    counts = jnp.zeros((N_GZ,), jnp.int32)
    counts = counts.at[order[0::2]].set(moves)
    counts = counts.at[order[1::2]].set(SLOTS - moves)
    ends = jnp.cumsum(counts)
    positions = jnp.arange(LBLK, dtype=jnp.int32)
    return jnp.sum((positions[:, None] >= ends[None, :]).astype(jnp.int32), axis=1).astype(jnp.int32)


def with_ends(result, own_key, smallest, top_value):
    longest = result.shape.index(max(result.shape))
    spots = []
    for shift in (0, 1):
        where = [jax.random.randint(jax.random.fold_in(own_key, axis), (), 0, length) for axis, length in enumerate(result.shape)]
        where[longest] = (where[longest] + shift) % result.shape[longest]
        spots.append(tuple(where))
    return result.at[spots[0]].set(smallest).at[spots[1]].set(top_value)


def block_scale(own_key, extent, cuts, least, top_value):
    level = 1.0
    for axis_at, blocks in cuts:
        steps = jax.random.uniform(jax.random.fold_in(jax.random.fold_in(own_key, 6), axis_at), (blocks,), jnp.float32, least / len(cuts), top_value / len(cuts))
        level = level * jnp.repeat(jnp.exp(steps), extent[axis_at] // blocks).reshape((-1,) + (1,) * (len(extent) - 1 - axis_at))
    return level


def bell_draw(key, dims, scale, most, cuts=(), kind=jnp.bfloat16):
    entries = scale * jax.random.normal(key, dims, jnp.float32)
    if cuts:
        entries = entries * block_scale(key, dims, cuts, -0.22, 0.18)
    return jnp.clip(entries, -most, most).astype(kind)


def setup_inputs(seed: int = 0) -> dict:
    key_list = jax.random.split(jax.random.key(seed), 8)
    flow_adjoint = bell_draw(key_list[0], (19, NX, NY, NZ), 1.0, 6.0, ((1, 4), (2, 4), (3, 2)), jnp.float32)
    solute_adjoint = bell_draw(key_list[1], (7, NX, NY, NZ), 1.0, 6.0, ((1, 4), (2, 4), (3, 2)), jnp.float32)
    flow_density = jnp.clip(0.796875 + 0.453125 * jax.random.uniform(key_list[2], (STEPS, NX, NY, NZ), jnp.float32) ** block_scale(key_list[2], (STEPS, NX, NY, NZ), ((1, 4), (2, 4), (3, 2)), -0.2, 0.2), 0.796875, 1.25).astype(jnp.bfloat16)
    flow_velocity = jnp.clip(jax.random.uniform(key_list[3], (STEPS, 3, NX, NY, NZ), jnp.float32, -0.119628906, 0.119628906) * block_scale(key_list[3], (STEPS, 3, NX, NY, NZ), ((2, 4), (3, 4), (4, 2)), -0.4, 0.0), -0.119628906, 0.119628906).astype(jnp.bfloat16)
    solute_level = jnp.clip(jnp.exp(math.log(3.0) - 3.4051113 * jax.random.uniform(key_list[4], (STEPS, NX, NY, NZ), jnp.float32) ** block_scale(key_list[4], (STEPS, NX, NY, NZ), ((1, 4), (2, 4), (3, 2)), -0.2, 0.2)), 0.099609375, 3.0).astype(jnp.bfloat16)
    solid = with_ends((jax.random.randint(key_list[5], (NX, NY, NZ), 0, 4) < 1).astype(jnp.int32), jax.random.fold_in(key_list[5], 1), 0, 1)
    owner = draw_owner(jax.random.fold_in(key_list[7], 71), 0)
    return dict(flow_adjoint=flow_adjoint, solute_adjoint=solute_adjoint, flow_density=flow_density, flow_velocity=flow_velocity, solute_level=solute_level, solid=solid, owner=owner)


FLOW_DIRS = [(0, 0, 0), (1, 0, 0), (-1, 0, 0), (0, 1, 0), (0, -1, 0), (0, 0, 1), (0, 0, -1),
             (1, 1, 0), (-1, -1, 0), (1, -1, 0), (-1, 1, 0), (1, 0, 1), (-1, 0, -1),
             (1, 0, -1), (-1, 0, 1), (0, 1, 1), (0, -1, -1), (0, 1, -1), (0, -1, 1)]
FLOW_WEIGHTS = [1.0 / 3.0] + [1.0 / 18.0] * 6 + [1.0 / 36.0] * 12
SOLUTE_DIRS = FLOW_DIRS[:7]
SOLUTE_WEIGHTS = [0.25] + [0.125] * 6
flow_omega = 1.25
solute_omega = 1.6
langmuir_rate = 0.05


def opposite(table):
    return [table.index((-entry[0], -entry[1], -entry[2])) for entry in table]


def reverse_stream(field, solid_pad, table):
    reverse = opposite(table)
    width_x, width_y, width_z = field.shape[1], field.shape[2], field.shape[3]
    padded = jnp.pad(field, ((0, 0), (1, 1), (1, 1), (1, 1)))
    result_rows = []
    for number, (step_x, step_y, step_z) in enumerate(table):
        near = padded[number, 1 + step_x:1 + step_x + width_x, 1 + step_y:1 + step_y + width_y, 1 + step_z:1 + step_z + width_z]
        blocked = solid_pad[1 + step_x:1 + step_x + width_x, 1 + step_y:1 + step_y + width_y, 1 + step_z:1 + step_z + width_z]
        result_rows.append(jnp.where(blocked == 0, near, field[reverse[number]]))
    return jnp.stack(result_rows)


def solute_update(read, level, velocity):
    vel_x = velocity[0].astype(jnp.float32)
    vel_y = velocity[1].astype(jnp.float32)
    vel_z = velocity[2].astype(jnp.float32)
    level = level.astype(jnp.float32)
    moment_zero = 0.0
    moment_x = 0.0
    moment_y = 0.0
    moment_z = 0.0
    for number, (step_x, step_y, step_z) in enumerate(SOLUTE_DIRS):
        weighted = SOLUTE_WEIGHTS[number] * read[number]
        moment_zero = moment_zero + weighted
        moment_x = moment_x + step_x * weighted
        moment_y = moment_y + step_y * weighted
        moment_z = moment_z + step_z * weighted
    uptake = langmuir_rate / ((1.0 + level) * (1.0 + level))
    common = solute_omega * (moment_zero + 4.0 * (moment_x * vel_x + moment_y * vel_y + moment_z * vel_z)) - uptake * moment_zero
    updated = jnp.stack([(1.0 - solute_omega) * read[number] + common for number in range(len(SOLUTE_DIRS))])
    factor = 4.0 * solute_omega * level
    pull = jnp.stack([factor * moment_x, factor * moment_y, factor * moment_z])
    return updated, pull


def flow_update(read, density, velocity, pull):
    vel_x = velocity[0].astype(jnp.float32)
    vel_y = velocity[1].astype(jnp.float32)
    vel_z = velocity[2].astype(jnp.float32)
    speed_sq = vel_x * vel_x + vel_y * vel_y + vel_z * vel_z
    moment_zero = 0.0
    moment_x = 0.0
    moment_y = 0.0
    moment_z = 0.0
    for number, (step_x, step_y, step_z) in enumerate(FLOW_DIRS):
        weighted = FLOW_WEIGHTS[number] * read[number]
        along = step_x * vel_x + step_y * vel_y + step_z * vel_z
        moment_zero = moment_zero + weighted * (1.0 - 4.5 * along * along + 1.5 * speed_sq)
        shared = 9.0 * weighted * along
        moment_x = moment_x + weighted * (3.0 * step_x - 3.0 * vel_x) + shared * step_x
        moment_y = moment_y + weighted * (3.0 * step_y - 3.0 * vel_y) + shared * step_y
        moment_z = moment_z + weighted * (3.0 * step_z - 3.0 * vel_z) + shared * step_z
    inverse_density = 1.0 / density.astype(jnp.float32)
    result_rows = []
    for number, (step_x, step_y, step_z) in enumerate(FLOW_DIRS):
        relax = moment_zero + step_x * moment_x + step_y * moment_y + step_z * moment_z
        source = (pull[0] * (step_x - vel_x) + pull[1] * (step_y - vel_y) + pull[2] * (step_z - vel_z)) * inverse_density
        result_rows.append((1.0 - flow_omega) * read[number] + flow_omega * relax + source)
    return jnp.stack(result_rows)


def reference(flow_adjoint, solute_adjoint, flow_density, flow_velocity, solute_level, solid, owner):
    blocks = owner.shape[0]
    slot_start = jnp.sum((owner[None, :] < owner[:, None]).astype(jnp.int32), axis=1)
    slot_number = jnp.arange(blocks, dtype=jnp.int32) - slot_start
    offsets = (owner * SLOTS + slot_number) * BZC
    zmap = (offsets[:, None] + jnp.arange(BZC, dtype=jnp.int32)[None, :]).reshape(-1).astype(jnp.int32)
    flow = jnp.take(flow_adjoint, zmap, axis=-1)
    solute = jnp.take(solute_adjoint, zmap, axis=-1)
    density = jnp.take(flow_density, zmap, axis=-1)
    velocity = jnp.take(flow_velocity, zmap, axis=-1)
    level = jnp.take(solute_level, zmap, axis=-1)
    solid_column = jnp.take(solid, zmap, axis=-1)
    valid = jnp.where(solid_column == 0, 1.0, 0.0).astype(jnp.float32)
    solid_pad = jnp.pad(solid_column, 1)
    pulls = [None] * STEPS
    for step in reversed(range(STEPS)):
        read = reverse_stream(solute, solid_pad, SOLUTE_DIRS)
        solute, pulls[step] = solute_update(read, level[step], velocity[step])
        solute = solute * valid
    for step in reversed(range(STEPS)):
        read = reverse_stream(flow, solid_pad, FLOW_DIRS)
        flow = flow_update(read, density[step], velocity[step], pulls[step]) * valid
    flow_result = jnp.zeros(flow_adjoint.shape, jnp.float32).at[..., zmap].set(flow)
    solute_result = jnp.zeros(solute_adjoint.shape, jnp.float32).at[..., zmap].set(solute)
    return flow_result, solute_result
```

```python
import functools

import jax
import jax.numpy as jnp
from jax import lax
from jax.experimental import pallas as pl
from jax.experimental.pallas import tpu as pltpu
from jax.sharding import PartitionSpec as P

BZC = 16

FLOW_DIRS = [
    (0, 0, 0),
    (1, 0, 0),
    (-1, 0, 0),
    (0, 1, 0),
    (0, -1, 0),
    (0, 0, 1),
    (0, 0, -1),
    (1, 1, 0),
    (-1, -1, 0),
    (1, -1, 0),
    (-1, 1, 0),
    (1, 0, 1),
    (-1, 0, -1),
    (1, 0, -1),
    (-1, 0, 1),
    (0, 1, 1),
    (0, -1, -1),
    (0, 1, -1),
    (0, -1, 1),
]
NF = 19
NS = 7
OPPOSITE = [FLOW_DIRS.index((-a, -b, -c)) for a, b, c in FLOW_DIRS]
SOLID = NF + NS
AUX = SOLID + 1
NA = 5
flow_omega = 1.25
solute_omega = 1.6
langmuir_rate = 0.05
VMEM_LIMIT = 50 * 1024 * 1024
F32 = jnp.float32


class Plan:
    def __init__(self, steps, nx, ny, depth):
        self.steps, self.nx, self.ny, self.depth = steps, nx, ny, depth
        self.halo = w = steps
        self.chan = AUX + NA * steps
        self.sent = AUX + NA * (steps - 1)
        self.pitch = -(-(ny + 2 * w) // 8) * 8
        self.wide = nx + 2 * w
        self.count = {k: AUX + NA * (steps - k) for k in range(1, w)}
        self.base, at = {}, 0
        for k in range(1, w):
            self.base[k] = at
            at += self.count[k]
        self.base[w] = at
        self.slab = at + 7

    def last(self, axis, sign):
        flow = [i for i, c in enumerate(FLOW_DIRS) if c[axis] == sign]
        solute = [NF + i for i, c in enumerate(FLOW_DIRS[:NS]) if c[axis] == sign]
        return flow + solute + [SOLID]


def lanes(depth):
    return lax.broadcasted_iota(jnp.int32, (8, depth), 1)


def occupied(owner_ref):
    me = lax.axis_index("gz")
    count = jnp.int32(0)
    for j in range(owner_ref.shape[0]):
        count = count + jnp.where(owner_ref[j] == me, 1, 0).astype(jnp.int32)
    return count * BZC


def z_places(plan, length, ring):
    w, depth = plan.halo, plan.depth
    if ring == 2:
        first = lax.axis_index("gz") == 0
        return [(jnp.where(first, length - w, 0), jnp.where(first, length, depth - w))]
    return [(length - w, jnp.int32(depth - w)), (jnp.int32(0), length)]


def for_channels(plan, sources, body, steps):
    flow, solute, density, velocity, level, solid = sources
    body(0, NF, lambda i, x: flow[i, x])
    body(NF, NS, lambda i, x: solute[i, x])
    body(SOLID, 1, lambda i, x: solid[x].astype(F32))
    for s in steps:
        t = plan.steps - 1 - s
        at = AUX + NA * s
        body(at, 1, lambda i, x, t=t: density[t, x].astype(F32))
        body(at + 1, 1, lambda i, x, t=t: level[t, x].astype(F32))
        body(at + 2, 3, lambda i, x, t=t: velocity[t, i, x].astype(F32))


def each(number, body):
    if number == 1:
        body(0)
    else:
        lax.fori_loop(0, number, lambda i, c: (body(i), c)[1], 0)


def pack_kernel(plan, ring, owner, flow, solute, density, velocity, level, solid, *outs):
    w, depth = plan.halo, plan.depth
    length = occupied(owner)
    lane = lanes(depth)
    places = z_places(plan, length, ring)
    tall = plan.ny // 8
    for (start, _), out in zip(places, outs):
        place = (lane - start) & (depth - 1)

        def body(at, number, read):
            def one(i):
                def merge(lo, count):
                    if count == 1:
                        x, h = divmod(lo, tall)
                        return read(i, x)[8 * h : 8 * h + 8]
                    half = count // 2
                    first, second = merge(lo, half), merge(lo + half, half)
                    return jnp.where(place < w * half, first, pltpu.roll(second, w * half, 1))

                packed = merge(0, plan.nx * tall)
                out[at + i] = pltpu.roll(packed, (depth - start) & (depth - 1), 1)

            each(number, one)

        for_channels(plan, (flow, solute, density, velocity, level, solid), body, range(plan.steps - 1))


def unpack(plan, ring, owner, sources, received, write, steps):
    w, depth = plan.halo, plan.depth
    length = occupied(owner)
    lane = lanes(depth)
    live = lane < length
    places = z_places(plan, length, ring)
    halos = [((lane - to) & (depth - 1)) < w for _, to in places]
    tall = plan.ny // 8

    def body(at, number, read):
        def one(i):
            slabs = []
            if not isinstance(at, int) or at < plan.sent:
                slabs = [pltpu.roll(r[at + i], to, 1) for r, (_, to) in zip(received, places)]
            for x in range(plan.nx):
                row = read(i, x)
                for h in range(tall):
                    tile = jnp.where(live, row[8 * h : 8 * h + 8], 0.0)
                    back = (depth - w * (x * tall + h)) % depth
                    for slab, halo in zip(slabs, halos):
                        tile = jnp.where(halo, pltpu.roll(slab, back, 1) if back else slab, tile)
                    write(at + i, x, h, tile)

        each(number, one)

    for_channels(plan, sources, body, steps)


def faces_kernel(plan, ring, parts, owner, flow, solute, density, velocity, level, solid, *rest):
    received, (y_low, y_high, x_low, x_high, cells) = rest[:parts], rest[parts:]
    w, nx, ny = plan.halo, plan.nx, plan.ny

    def write(c, x, h, tile):
        cells[c, x * ny + 8 * h : x * ny + 8 * h + 8, :] = tile

    unpack(plan, ring, owner, (flow, solute, density, velocity, level, solid), received, write, range(plan.steps - 1))

    def y_row(c, y):
        return cells[c, pl.ds(y, nx, stride=ny), :]

    def x_row(c, x):
        return cells[c, x * ny : (x + 1) * ny, :]

    for k in range(1, w):
        base = plan.base[k]

        def one(c, base=base, k=k):
            y_low[base + c] = y_row(c, k - 1)
            y_high[base + c] = y_row(c, ny - k)
            x_low[base + c] = x_row(c, k - 1)
            x_high[base + c] = x_row(c, nx - k)

        each(plan.count[k], one)
    for j in range(7):
        at = plan.base[w] + j
        y_low[at] = y_row(plan.last(1, 1)[j], w - 1)
        y_high[at] = y_row(plan.last(1, -1)[j], ny - w)
        x_low[at] = x_row(plan.last(0, 1)[j], w - 1)
        x_high[at] = x_row(plan.last(0, -1)[j], nx - w)


def inner_kernel(plan, ring, parts, owner, flow, solute, density, velocity, level, solid, *rest):
    received, out = rest[:parts], rest[parts]
    w, pitch = plan.halo, plan.pitch

    def write(c, x, h, tile):
        row = x * pitch + w + 8 * h
        out[c, row : row + 8, :] = tile

    unpack(plan, ring, owner, (flow, solute, density, velocity, level, solid), received, write, range(plan.steps))


def corners_kernel(plan, from_low, from_high, low, high):
    w, nx, ny = plan.halo, plan.nx, plan.ny
    low[...] = jnp.zeros(low.shape, F32)
    high[...] = jnp.zeros(high.shape, F32)
    tall = 2 * w
    for out, sign in ((low, 1), (high, -1)):
        x_last = plan.last(0, sign)
        for k in range(1, w + 1):
            x = k - 1 if sign == 1 else nx - k
            for m in range(1, w + 1):
                for source, row, y_sign in ((from_low, w - m, -1), (from_high, w - 1 + m, 1)):
                    y_last = plan.last(1, y_sign)
                    if k < w and m < w:
                        number = min(plan.count[k], plan.count[m])
                        out[pl.ds(plan.base[k] * tall + row, number, stride=tall), :] = source[
                            pl.ds(plan.base[m] * nx + x, number, stride=nx), :
                        ]
                        continue
                    for c in range(AUX):
                        if (k == w and c not in x_last) or (m == w and c not in y_last):
                            continue
                        to = plan.base[k] + (x_last.index(c) if k == w else c)
                        at = plan.base[m] + (y_last.index(c) if m == w else c)
                        out[to * tall + row : to * tall + row + 1, :] = source[at * nx + x : at * nx + x + 1, :]


PAD = 8


def steps_kernel(plan, owner, inner, y_low, y_high, x_low, x_high, c_low, c_high, flow_out, solute_out, cells, other, masks, sem):
    w, nx, ny, depth, pitch = plan.halo, plan.nx, plan.ny, plan.depth, plan.pitch
    copy = pltpu.make_async_copy(inner, cells.at[:, pl.ds(PAD + w * pitch, nx * pitch), :], sem)
    copy.start()
    for k in range(1, w + 1):
        for x_part, c_part, x, sign in ((x_low, c_low, w - k, -1), (x_high, c_high, w + nx - 1 + k, 1)):
            row = PAD + x * pitch

            def one(c, j, row=row, x_part=x_part, c_part=c_part):
                cells[c, row : row + w, :] = c_part[j, 0:w, :]
                cells[c, row + w : row + w + ny, :] = x_part[j]
                cells[c, row + w + ny : row + w + ny + w, :] = c_part[j, w : 2 * w, :]

            if k < w:
                each(plan.count[k], lambda c, one=one, k=k: one(c, plan.base[k] + c))
            else:
                for j, c in enumerate(plan.last(0, sign)):
                    one(c, plan.base[w] + j)
    copy.wait()
    for m in range(1, w + 1):
        for part, y, sign in ((y_low, w - m, -1), (y_high, w + ny - 1 + m, 1)):
            row = PAD + w * pitch + y

            def one(c, j, row=row, part=part):
                cells[c, pl.ds(row, nx, stride=pitch), :] = part[j]

            if m < w:
                each(plan.count[m], lambda c, one=one, m=m: one(c, plan.base[m] + c))
            else:
                for j, c in enumerate(plan.last(1, sign)):
                    one(c, plan.base[w] + j)

    length = occupied(owner)
    lane = lanes(depth)
    gx, gy, gz = (lax.axis_index(a) for a in ("gx", "gy", "gz"))
    last_x, last_y, last_z = (lax.axis_size(a) - 1 for a in ("gx", "gy", "gz"))
    above = jnp.where(gz < last_z, w, 0)
    below = jnp.where(gz > 0, w, 0)
    in_z = (lane < length + above) | (lane >= depth - below)
    y_first = jnp.where(gy > 0, 0, w)
    y_end = jnp.where(gy < last_y, ny + 2 * w, w + ny)
    x_first = jnp.where(gx > 0, 0, w)
    x_end = jnp.where(gx < last_x, nx + 2 * w, w + nx)
    sub = lax.broadcasted_iota(jnp.int32, (8, depth), 0)

    def prepare(x, carry):
        in_x = ((x >= x_first) & (x < x_end)).astype(F32)
        for h in range(pitch // 8):
            row = pl.multiple_of(PAD + x * pitch + 8 * h, 8)
            flags = cells[SOLID, pl.ds(row, 8), :]
            y = sub + 8 * h
            masks[0, pl.ds(row, 8), :] = pltpu.roll(flags, depth - 1, 1)
            masks[1, pl.ds(row, 8), :] = pltpu.roll(flags, 1, 1)
            inside = in_z & (y >= y_first) & (y < y_end) & (flags == 0.0)
            masks[2, pl.ds(row, 8), :] = jnp.where(inside, in_x, 0.0)
        return carry

    lax.fori_loop(0, plan.wide, prepare, 0)

    live = lane < length

    def tile(source, s, row, write):
        def field(ref, c, move=0):
            return ref[c, pl.ds(row + move, 8), :]

        blocked = {}

        def reads(first, number):
            result = []
            for i in range(number):
                sx, sy, sz = FLOW_DIRS[i]
                if i == 0:
                    result.append(field(source, first))
                    continue
                move = sx * pitch + sy
                near = field(source, first + i, move)
                if sz:
                    near = pltpu.roll(near, (depth - sz) % depth, 1)
                if i not in blocked:
                    flags = field(cells, SOLID, move) if sz == 0 else field(masks, 0 if sz == 1 else 1, move)
                    blocked[i] = flags != 0.0
                result.append(jnp.where(blocked[i], field(source, first + OPPOSITE[i]), near))
            return result

        valid = field(masks, 2)
        if s == plan.steps - 1:
            valid = jnp.where(live, valid, 0.0)
        aux = AUX + NA * s
        density, level, ux, uy, uz = (field(cells, aux + n) for n in range(NA))

        h = reads(NF, NS)
        px, py, pz = h[1] - h[2], h[3] - h[4], h[5] - h[6]
        p0 = 0.25 * h[0] + 0.125 * ((h[1] + h[2]) + (h[3] + h[4]) + (h[5] + h[6]))
        grown = 1.0 + level
        uptake = langmuir_rate / (grown * grown)
        common = valid * (
            (solute_omega - uptake) * p0 + (solute_omega * 0.5) * (px * ux + py * uy + pz * uz)
        )
        keep = (1.0 - solute_omega) * valid
        for i in range(NS):
            write(NF + i, keep * h[i] + common)
        factor = (0.5 * solute_omega) * level / jnp.maximum(density, 0.5)
        fx, fy, fz = factor * px, factor * py, factor * pz

        g = reads(0, NF)
        a = {i: g[i] + g[i + 1] for i in range(1, NF, 2)}
        d = {i: g[i] - g[i + 1] for i in range(1, NF, 2)}
        m1x = (d[1] + d[1]) + (d[7] + d[9]) + (d[11] + d[13])
        m1y = (d[3] + d[3]) + (d[7] - d[9]) + (d[15] + d[17])
        m1z = (d[5] + d[5]) + (d[11] - d[13]) + (d[15] - d[17])
        exy, exz, eyz = a[7] + a[9], a[11] + a[13], a[15] + a[17]
        tx, ty, tz = a[1] + a[1], a[3] + a[3], a[5] + a[5]
        mxx, myy, mzz = tx + exy + exz, ty + exy + eyz, tz + exz + eyz
        mxy, mxz, myz = a[7] - a[9], a[11] - a[13], a[15] - a[17]
        m0 = 12.0 * g[0] + (tx + ty + tz) + (exy + exz + eyz)
        qx = mxx * ux + mxy * uy + mxz * uz
        qy = mxy * ux + myy * uy + myz * uz
        qz = mxz * ux + myz * uy + mzz * uz
        square = ux * ux + uy * uy + uz * uz
        scaled = flow_omega / 36.0
        zero = m0 * (scaled + (1.5 * scaled) * square) - (4.5 * scaled) * (qx * ux + qy * uy + qz * uz)
        zero = valid * (zero - (fx * ux + fy * uy + fz * uz))
        bx = valid * ((3.0 * scaled) * (m1x + 3.0 * qx - m0 * ux) + fx)
        by = valid * ((3.0 * scaled) * (m1y + 3.0 * qy - m0 * uy) + fy)
        bz = valid * ((3.0 * scaled) * (m1z + 3.0 * qz - m0 * uz) + fz)
        keep = (1.0 - flow_omega) * valid
        write(0, keep * g[0] + zero)
        moves = {1: bx, 3: by, 5: bz, 7: bx + by, 9: bx - by, 11: bx + bz, 13: bx - bz, 15: by + bz, 17: by - bz}
        for i, move in moves.items():
            write(i, keep * g[i] + (zero + move))
            write(i + 1, keep * g[i + 1] + (zero - move))

    buffers = [cells, other]
    for s in range(plan.steps - 1):
        source, target = buffers[s % 2], buffers[(s + 1) % 2]
        first = PAD + (1 + s) * pitch
        tiles = (plan.wide - 2 - 2 * s) * (pitch // 8)

        def body(n, carry, source=source, target=target, first=first, s=s):
            row = pl.multiple_of(first + 8 * n, 8)

            def write(c, value):
                target[c, pl.ds(row, 8), :] = value

            tile(source, s, row, write)
            return carry

        lax.fori_loop(0, tiles, body, 0)

    s = plan.steps - 1
    source = buffers[s % 2]

    def last(x, carry):
        for h in range(ny // 8):
            row = PAD + (x + w) * pitch + w + 8 * h

            def write(c, value, h=h):
                if c < NF:
                    flow_out[c, x, 8 * h : 8 * h + 8, :] = value
                else:
                    solute_out[c - NF, x, 8 * h : 8 * h + 8, :] = value

            tile(source, s, row, write)
        return carry

    lax.fori_loop(0, nx, last, 0)


VMEM = pl.BlockSpec(memory_space=pltpu.VMEM)
SMEM = pl.BlockSpec(memory_space=pltpu.SMEM)
ANY = pl.BlockSpec(memory_space=pl.ANY)


def call(kernel, ins, outs, name, cost, scratch=()):
    return pl.pallas_call(
        kernel,
        in_specs=ins,
        out_shape=outs,
        out_specs=[VMEM] * len(outs),
        scratch_shapes=list(scratch),
        name=name,
        cost_estimate=pl.CostEstimate(flops=cost, bytes_accessed=1 << 23, transcendentals=0),
        compiler_params=pltpu.CompilerParams(vmem_limit_bytes=VMEM_LIMIT),
    )


def per_device(flow_adjoint, solute_adjoint, flow_density, flow_velocity, solute_level, solid, owner):
    steps = flow_density.shape[0]
    nx, ny, depth = solid.shape
    plan = Plan(steps, nx, ny, depth)
    ring = lax.axis_size("gz")
    w = plan.halo
    fields = (flow_adjoint, solute_adjoint, flow_density, flow_velocity, solute_level, solid)

    def move(value, axis, by):
        size = lax.axis_size(axis)
        return lax.ppermute(value, axis, [(i, i + by) for i in range(size) if 0 <= i + by < size])

    parts = 1 if ring == 2 else 2
    packed_shape = jax.ShapeDtypeStruct((plan.sent, 8, depth), F32)
    packed = call(
        functools.partial(pack_kernel, plan, ring), [SMEM] + [VMEM] * 6, [packed_shape] * parts, "pack_column", 1 << 22
    )(owner, *fields)
    if ring == 2:
        received = [lax.ppermute(packed[0], "gz", [(0, 1), (1, 0)])]
    else:
        received = [move(packed[0], "gz", 1), move(packed[1], "gz", -1)]

    def slab(rows):
        return jax.ShapeDtypeStruct((plan.slab, rows, depth), F32)

    y_low, y_high, x_low, x_high = call(
        functools.partial(faces_kernel, plan, ring, parts),
        [SMEM] + [VMEM] * (6 + parts),
        [slab(nx), slab(nx), slab(ny), slab(ny)],
        "faces",
        1 << 22,
        [pltpu.VMEM((plan.sent, nx * ny, depth), F32)],
    )(owner, *fields, *received)
    from_y_low = move(y_high, "gy", 1)
    from_y_high = move(y_low, "gy", -1)
    from_x_low = move(x_high, "gx", 1)
    from_x_high = move(x_low, "gx", -1)
    inner = call(
        functools.partial(inner_kernel, plan, ring, parts),
        [SMEM] + [VMEM] * (6 + parts),
        [jax.ShapeDtypeStruct((plan.chan, nx * plan.pitch, depth), F32)],
        "inner",
        1 << 22,
    )(owner, *fields, *received)[0]

    def rows(value):
        return value.reshape(-1, depth)

    corner = jax.ShapeDtypeStruct((plan.slab * 2 * w, depth), F32)
    c_low, c_high = call(
        functools.partial(corners_kernel, plan), [VMEM] * 2, [corner, corner], "corners", 1 << 20
    )(rows(from_y_low), rows(from_y_high))
    shape = (plan.slab, 2 * w, depth)
    from_c_low = move(c_high, "gx", 1).reshape(shape)
    from_c_high = move(c_low, "gx", -1).reshape(shape)
    height = plan.wide * plan.pitch + 2 * PAD
    flow, solute = call(
        functools.partial(steps_kernel, plan),
        [SMEM, ANY] + [VMEM] * 6,
        [jax.ShapeDtypeStruct(flow_adjoint.shape, F32), jax.ShapeDtypeStruct(solute_adjoint.shape, F32)],
        "steps",
        1 << 28,
        [
            pltpu.VMEM((plan.chan, height, depth), F32),
            pltpu.VMEM((NF + NS, height, depth), F32),
            pltpu.VMEM((3, height, depth), F32),
            pltpu.SemaphoreType.DMA,
        ],
    )(owner, inner, from_y_low, from_y_high, from_x_low, from_x_high, from_c_low, from_c_high)
    return (flow, solute)


def solution(mesh):
    in_specs = (
        P(None, "gx", "gy", "gz"),
        P(None, "gx", "gy", "gz"),
        P(None, "gx", "gy", "gz"),
        P(None, None, "gx", "gy", "gz"),
        P(None, "gx", "gy", "gz"),
        P("gx", "gy", "gz"),
        P(),
    )
    out_specs = (P(None, "gx", "gy", "gz"), P(None, "gx", "gy", "gz"))
    return jax.shard_map(
        per_device, mesh=mesh, in_specs=in_specs, out_specs=out_specs, check_vma=False
    )
```

```python
import functools

import jax
import jax.numpy as jnp
from jax import lax
from jax.experimental import pallas as pl
from jax.experimental.pallas import tpu as pltpu
from jax.sharding import PartitionSpec as P

BZC = 16

FLOW_DIRS = [
    (0, 0, 0),
    (1, 0, 0),
    (-1, 0, 0),
    (0, 1, 0),
    (0, -1, 0),
    (0, 0, 1),
    (0, 0, -1),
    (1, 1, 0),
    (-1, -1, 0),
    (1, -1, 0),
    (-1, 1, 0),
    (1, 0, 1),
    (-1, 0, -1),
    (1, 0, -1),
    (-1, 0, 1),
    (0, 1, 1),
    (0, -1, -1),
    (0, 1, -1),
    (0, -1, 1),
]
NF = 19
NS = 7
OPPOSITE = [FLOW_DIRS.index((-a, -b, -c)) for a, b, c in FLOW_DIRS]
SOLID = NF + NS
AUX = SOLID + 1
NA = 5
flow_omega = 1.25
solute_omega = 1.6
langmuir_rate = 0.05
VMEM_LIMIT = 50 * 1024 * 1024
F32 = jnp.float32


class Plan:
    def __init__(self, steps, nx, ny, depth):
        self.steps, self.nx, self.ny, self.depth = steps, nx, ny, depth
        self.halo = w = steps
        self.chan = AUX + NA * steps
        self.sent = AUX + NA * (steps - 1)
        self.pitch = -(-(ny + 2 * w) // 8) * 8
        self.wide = nx + 2 * w
        self.count = {k: AUX + NA * (steps - k) for k in range(1, w)}
        self.base, at = {}, 0
        for k in range(1, w):
            self.base[k] = at
            at += self.count[k]
        self.base[w] = at
        self.slab = at + 7

    def last(self, axis, sign):
        flow = [i for i, c in enumerate(FLOW_DIRS) if c[axis] == sign]
        solute = [NF + i for i, c in enumerate(FLOW_DIRS[:NS]) if c[axis] == sign]
        return flow + solute + [SOLID]


def lanes(depth):
    return lax.broadcasted_iota(jnp.int32, (8, depth), 1)


def occupied(owner_ref):
    me = lax.axis_index("gz")
    count = jnp.int32(0)
    for j in range(owner_ref.shape[0]):
        count = count + jnp.where(owner_ref[j] == me, 1, 0).astype(jnp.int32)
    return count * BZC


def z_places(plan, length, ring):
    w, depth = plan.halo, plan.depth
    if ring == 2:
        first = lax.axis_index("gz") == 0
        return [(jnp.where(first, length - w, 0), jnp.where(first, length, depth - w))]
    return [(length - w, jnp.int32(depth - w)), (jnp.int32(0), length)]


def for_channels(plan, arrays, held, sems, body, steps):
    copies = fetch(arrays, held, sems)
    flow, solute, density, velocity, level, solid = held
    copies[0].wait()
    body(0, NF, lambda i, x: flow[i, x])
    for copy in copies[1:]:
        copy.wait()
    body(NF, NS, lambda i, x: solute[i, x])
    body(SOLID, 1, lambda i, x: solid[x].astype(F32))
    for s in steps:
        t = plan.steps - 1 - s
        at = AUX + NA * s
        body(at, 1, lambda i, x, t=t: density[t, x].astype(F32))
        body(at + 1, 1, lambda i, x, t=t: level[t, x].astype(F32))
        body(at + 2, 3, lambda i, x, t=t: velocity[t, i, x].astype(F32))


def each(number, body, unroll=4):
    def several(i, carry):
        for u in range(unroll):
            body(i * unroll + u)
        return carry

    turns = number // unroll
    if turns > 1:
        lax.fori_loop(0, turns, several, 0)
    else:
        turns = 0
    for i in range(turns * unroll, number):
        body(i)


def fetch(arrays, held, sems):
    copies = [pltpu.make_async_copy(a, b, sems.at[i]) for i, (a, b) in enumerate(zip(arrays, held))]
    for copy in copies:
        copy.start()
    return copies


def pack_kernel(plan, ring, parts, *refs):
    owner, arrays, outs, held, sems = refs[0], refs[1:7], refs[7 : 7 + parts], refs[7 + parts : 13 + parts], refs[-1]
    w, depth = plan.halo, plan.depth
    length = occupied(owner)
    group = lanes(depth) // w
    places = z_places(plan, length, ring)
    tall = plan.ny // 8
    shifts = [[(w * n + depth - start) & (depth - 1) for n in range(plan.nx * tall)] for start, _ in places]

    def body(at, number, read):
        def one(i):
            packed = [None] * parts
            for x in range(plan.nx):
                row = read(i, x)
                for h in range(tall):
                    n = x * tall + h
                    for p in range(parts):
                        moved = pltpu.roll(row[8 * h : 8 * h + 8], shifts[p][n], 1)
                        packed[p] = moved if n == 0 else jnp.where(group == n, moved, packed[p])
            for p in range(parts):
                outs[p][at + i] = packed[p]

        each(number, one, 3)

    for_channels(plan, arrays, held, sems, body, range(plan.steps - 1))


def unpack(plan, ring, owner, arrays, held, sems, received, write, steps):
    w, depth = plan.halo, plan.depth
    length = occupied(owner)
    lane = lanes(depth)
    live = lane < length
    places = z_places(plan, length, ring)
    halos = [((lane - to) & (depth - 1)) < w for _, to in places]
    tall = plan.ny // 8

    def body(at, number, read):
        def one(i):
            slabs = []
            if not isinstance(at, int) or at < plan.sent:
                slabs = [pltpu.roll(r[at + i], to, 1) for r, (_, to) in zip(received, places)]
            for x in range(plan.nx):
                row = read(i, x)
                for h in range(tall):
                    tile = jnp.where(live, row[8 * h : 8 * h + 8], 0.0)
                    back = (depth - w * (x * tall + h)) % depth
                    for slab, halo in zip(slabs, halos):
                        tile = jnp.where(halo, pltpu.roll(slab, back, 1) if back else slab, tile)
                    write(at + i, x, h, tile)

        each(number, one, 3)

    for_channels(plan, arrays, held, sems, body, steps)


def faces_kernel(plan, ring, parts, *refs):
    owner, arrays, received, rest = refs[0], refs[1:7], refs[7 : 7 + parts], refs[7 + parts :]
    (y_low, y_high, x_low, x_high, cells), held, sems = rest[:5], rest[5:11], rest[11]
    w, nx, ny = plan.halo, plan.nx, plan.ny

    def write(c, x, h, tile):
        cells[c, x * ny + 8 * h : x * ny + 8 * h + 8, :] = tile

    unpack(plan, ring, owner, arrays, held, sems, received, write, range(plan.steps - 1))

    def y_row(c, y):
        return cells[c, pl.ds(y, nx, stride=ny), :]

    def x_row(c, x):
        return cells[c, x * ny : (x + 1) * ny, :]

    for k in range(1, w):
        base = plan.base[k]

        def one(c, base=base, k=k):
            y_low[base + c] = y_row(c, k - 1)
            y_high[base + c] = y_row(c, ny - k)
            x_low[base + c] = x_row(c, k - 1)
            x_high[base + c] = x_row(c, nx - k)

        each(plan.count[k], one)
    for j in range(7):
        at = plan.base[w] + j
        y_low[at] = y_row(plan.last(1, 1)[j], w - 1)
        y_high[at] = y_row(plan.last(1, -1)[j], ny - w)
        x_low[at] = x_row(plan.last(0, 1)[j], w - 1)
        x_high[at] = x_row(plan.last(0, -1)[j], nx - w)


def inner_kernel(plan, ring, parts, *refs):
    owner, arrays, received, rest = refs[0], refs[1:7], refs[7 : 7 + parts], refs[7 + parts :]
    out, held, sems = rest[0], rest[1:7], rest[7]
    w, pitch = plan.halo, plan.pitch

    def write(c, x, h, tile):
        row = x * pitch + w + 8 * h
        out[c, row : row + 8, :] = tile

    unpack(plan, ring, owner, arrays, held, sems, received, write, range(plan.steps))


def corners_kernel(plan, from_low, from_high, inner, low, high):
    w, nx, ny = plan.halo, plan.nx, plan.ny
    low[...] = jnp.zeros(low.shape, F32)
    high[...] = jnp.zeros(high.shape, F32)
    tall = 2 * w
    for out, sign in ((low, 1), (high, -1)):
        x_last = plan.last(0, sign)
        for k in range(1, w + 1):
            x = k - 1 if sign == 1 else nx - k
            for m in range(1, w + 1):
                for source, row, y_sign in ((from_low, w - m, -1), (from_high, w - 1 + m, 1)):
                    y_last = plan.last(1, y_sign)
                    if k < w and m < w:
                        number = min(plan.count[k], plan.count[m])
                        out[pl.ds(plan.base[k] * tall + row, number, stride=tall), :] = source[
                            pl.ds(plan.base[m] * nx + x, number, stride=nx), :
                        ]
                        continue
                    for c in range(AUX):
                        if (k == w and c not in x_last) or (m == w and c not in y_last):
                            continue
                        to = plan.base[k] + (x_last.index(c) if k == w else c)
                        at = plan.base[m] + (y_last.index(c) if m == w else c)
                        out[to * tall + row : to * tall + row + 1, :] = source[at * nx + x : at * nx + x + 1, :]


PAD = 8


def steps_kernel(plan, owner, inner, y_low, y_high, x_low, x_high, c_low, c_high, flow_out, solute_out, cells, other, fields, masks, sems):
    w, nx, ny, depth, pitch = plan.halo, plan.nx, plan.ny, plan.depth, plan.pitch
    middle = pl.ds(PAD + w * pitch, nx * pitch)
    copies = [
        pltpu.make_async_copy(inner.at[pl.ds(0, SOLID)], cells.at[:, middle, :], sems.at[0]),
        pltpu.make_async_copy(inner.at[pl.ds(SOLID, plan.chan - SOLID)], fields.at[:, middle, :], sems.at[1]),
    ]
    for copy in copies:
        copy.start()

    def channels(number, body):
        each(SOLID, lambda c: body(cells, c, c))
        each(number - SOLID, lambda c: body(fields, c, SOLID + c))

    def channel(c):
        return (cells, c) if c < SOLID else (fields, c - SOLID)

    for k in range(1, w + 1):
        for x_part, c_part, x, sign in ((x_low, c_low, w - k, -1), (x_high, c_high, w + nx - 1 + k, 1)):
            row = PAD + x * pitch

            def one(ref, c, j, row=row, x_part=x_part, c_part=c_part):
                ref[c, row : row + w, :] = c_part[j, 0:w, :]
                ref[c, row + w : row + w + ny, :] = x_part[j]
                ref[c, row + w + ny : row + w + ny + w, :] = c_part[j, w : 2 * w, :]

            if k < w:
                channels(plan.count[k], lambda ref, c, j, one=one, k=k: one(ref, c, plan.base[k] + j))
            else:
                for j, c in enumerate(plan.last(0, sign)):
                    one(*channel(c), plan.base[w] + j)
    for copy in copies:
        copy.wait()
    for m in range(1, w + 1):
        for part, y, sign in ((y_low, w - m, -1), (y_high, w + ny - 1 + m, 1)):
            row = PAD + w * pitch + y

            def one(ref, c, j, row=row, part=part):
                ref[c, pl.ds(row, nx, stride=pitch), :] = part[j]

            if m < w:
                channels(plan.count[m], lambda ref, c, j, one=one, m=m: one(ref, c, plan.base[m] + j))
            else:
                for j, c in enumerate(plan.last(1, sign)):
                    one(*channel(c), plan.base[w] + j)

    length = occupied(owner)
    lane = lanes(depth)
    gx, gy, gz = (lax.axis_index(a) for a in ("gx", "gy", "gz"))
    last_x, last_y, last_z = (lax.axis_size(a) - 1 for a in ("gx", "gy", "gz"))
    above = jnp.where(gz < last_z, w, 0)
    below = jnp.where(gz > 0, w, 0)
    in_z = (lane < length + above) | (lane >= depth - below)
    y_first = jnp.where(gy > 0, 0, w)
    y_end = jnp.where(gy < last_y, ny + 2 * w, w + ny)
    x_first = jnp.where(gx > 0, 0, w)
    x_end = jnp.where(gx < last_x, nx + 2 * w, w + nx)
    sub = lax.broadcasted_iota(jnp.int32, (8, depth), 0)

    def prepare(x, carry):
        in_x = ((x >= x_first) & (x < x_end)).astype(F32)
        for h in range(pitch // 8):
            row = pl.multiple_of(PAD + x * pitch + 8 * h, 8)
            flags = fields[0, pl.ds(row, 8), :]
            y = sub + 8 * h
            masks[0, pl.ds(row, 8), :] = pltpu.roll(flags, depth - 1, 1)
            masks[1, pl.ds(row, 8), :] = pltpu.roll(flags, 1, 1)
            inside = in_z & (y >= y_first) & (y < y_end) & (flags == 0.0)
            masks[2, pl.ds(row, 8), :] = jnp.where(inside, in_x, 0.0)
        return carry

    lax.fori_loop(0, plan.wide, prepare, 0)

    live = lane < length

    def tile(source, s, row, write):
        def field(ref, c, move=0):
            return ref[c, pl.ds(row + move, 8), :]

        blocked = {}

        def reads(first, number):
            result = []
            for i in range(number):
                sx, sy, sz = FLOW_DIRS[i]
                if i == 0:
                    result.append(field(source, first))
                    continue
                move = sx * pitch + sy
                near = field(source, first + i, move)
                if sz:
                    near = pltpu.roll(near, (depth - sz) % depth, 1)
                if i not in blocked:
                    flags = field(fields, 0, move) if sz == 0 else field(masks, 0 if sz == 1 else 1, move)
                    blocked[i] = flags != 0.0
                result.append(jnp.where(blocked[i], field(source, first + OPPOSITE[i]), near))
            return result

        valid = field(masks, 2)
        if s == plan.steps - 1:
            valid = jnp.where(live, valid, 0.0)
        aux = AUX - SOLID + NA * s
        density, level, ux, uy, uz = (field(fields, aux + n) for n in range(NA))

        h = reads(NF, NS)
        px, py, pz = h[1] - h[2], h[3] - h[4], h[5] - h[6]
        p0 = 0.25 * h[0] + 0.125 * ((h[1] + h[2]) + (h[3] + h[4]) + (h[5] + h[6]))
        grown = 1.0 + level
        uptake = langmuir_rate / (grown * grown)
        common = valid * (
            (solute_omega - uptake) * p0 + (solute_omega * 0.5) * (px * ux + py * uy + pz * uz)
        )
        keep = (1.0 - solute_omega) * valid
        for i in range(NS):
            write(NF + i, keep * h[i] + common)
        factor = (0.5 * solute_omega) * level / jnp.maximum(density, 0.5)
        fx, fy, fz = factor * px, factor * py, factor * pz

        g = reads(0, NF)
        a = {i: g[i] + g[i + 1] for i in range(1, NF, 2)}
        d = {i: g[i] - g[i + 1] for i in range(1, NF, 2)}
        m1x = (d[1] + d[1]) + (d[7] + d[9]) + (d[11] + d[13])
        m1y = (d[3] + d[3]) + (d[7] - d[9]) + (d[15] + d[17])
        m1z = (d[5] + d[5]) + (d[11] - d[13]) + (d[15] - d[17])
        exy, exz, eyz = a[7] + a[9], a[11] + a[13], a[15] + a[17]
        tx, ty, tz = a[1] + a[1], a[3] + a[3], a[5] + a[5]
        mxx, myy, mzz = tx + exy + exz, ty + exy + eyz, tz + exz + eyz
        mxy, mxz, myz = a[7] - a[9], a[11] - a[13], a[15] - a[17]
        m0 = 12.0 * g[0] + (tx + ty + tz) + (exy + exz + eyz)
        qx = mxx * ux + mxy * uy + mxz * uz
        qy = mxy * ux + myy * uy + myz * uz
        qz = mxz * ux + myz * uy + mzz * uz
        square = ux * ux + uy * uy + uz * uz
        scaled = flow_omega / 36.0
        zero = m0 * (scaled + (1.5 * scaled) * square) - (4.5 * scaled) * (qx * ux + qy * uy + qz * uz)
        zero = valid * (zero - (fx * ux + fy * uy + fz * uz))
        bx = valid * ((3.0 * scaled) * (m1x + 3.0 * qx - m0 * ux) + fx)
        by = valid * ((3.0 * scaled) * (m1y + 3.0 * qy - m0 * uy) + fy)
        bz = valid * ((3.0 * scaled) * (m1z + 3.0 * qz - m0 * uz) + fz)
        keep = (1.0 - flow_omega) * valid
        write(0, keep * g[0] + zero)
        moves = {1: bx, 3: by, 5: bz, 7: bx + by, 9: bx - by, 11: bx + bz, 13: bx - bz, 15: by + bz, 17: by - bz}
        for i, move in moves.items():
            write(i, keep * g[i] + (zero + move))
            write(i + 1, keep * g[i + 1] + (zero - move))

    buffers = [cells, other]
    for s in range(plan.steps - 1):
        source, target = buffers[s % 2], buffers[(s + 1) % 2]
        first = PAD + (1 + s) * pitch

        def body(n, carry, source=source, target=target, first=first, s=s):
            for h in range(pitch // 8):
                row = pl.multiple_of(first + pitch * n + 8 * h, 8)

                def write(c, value, row=row):
                    target[c, pl.ds(row, 8), :] = value

                tile(source, s, row, write)
            return carry

        lax.fori_loop(0, plan.wide - 2 - 2 * s, body, 0)

    s = plan.steps - 1
    source = buffers[s % 2]

    def last(x, carry):
        for h in range(ny // 8):
            row = PAD + (x + w) * pitch + w + 8 * h

            def write(c, value, h=h):
                if c < NF:
                    flow_out[c, x, 8 * h : 8 * h + 8, :] = value
                else:
                    solute_out[c - NF, x, 8 * h : 8 * h + 8, :] = value

            tile(source, s, row, write)
        return carry

    lax.fori_loop(0, nx, last, 0)


VMEM = pl.BlockSpec(memory_space=pltpu.VMEM)
SMEM = pl.BlockSpec(memory_space=pltpu.SMEM)
ANY = pl.BlockSpec(memory_space=pl.ANY)


def call(kernel, ins, outs, name, cost, scratch=(), limit=VMEM_LIMIT):
    return pl.pallas_call(
        kernel,
        in_specs=ins,
        out_shape=outs,
        out_specs=[VMEM] * len(outs),
        scratch_shapes=list(scratch),
        name=name,
        cost_estimate=pl.CostEstimate(flops=cost, bytes_accessed=1 << 23, transcendentals=0),
        compiler_params=pltpu.CompilerParams(vmem_limit_bytes=limit),
    )


def per_device(flow_adjoint, solute_adjoint, flow_density, flow_velocity, solute_level, solid, owner):
    steps = flow_density.shape[0]
    nx, ny, depth = solid.shape
    plan = Plan(steps, nx, ny, depth)
    ring = lax.axis_size("gz")
    w = plan.halo
    fields = (flow_adjoint, solute_adjoint, flow_density, flow_velocity, solute_level, solid)

    def move(value, axis, by):
        size = lax.axis_size(axis)
        return lax.ppermute(value, axis, [(i, i + by) for i in range(size) if 0 <= i + by < size])

    parts = 1 if ring == 2 else 2
    packed_shape = jax.ShapeDtypeStruct((plan.sent, 8, depth), F32)
    held = [pltpu.VMEM(f.shape, f.dtype) for f in fields] + [pltpu.SemaphoreType.DMA((len(fields),))]
    packed = call(
        functools.partial(pack_kernel, plan, ring, parts),
        [SMEM] + [ANY] * 6,
        [packed_shape] * parts,
        "pack_column",
        1 << 22,
        held,
        60 << 20,
    )(owner, *fields)
    if ring == 2:
        received = [lax.ppermute(packed[0], "gz", [(0, 1), (1, 0)])]
    else:
        received = [move(packed[0], "gz", 1), move(packed[1], "gz", -1)]

    def slab(rows):
        return jax.ShapeDtypeStruct((plan.slab, rows, depth), F32)

    y_low, y_high, x_low, x_high = call(
        functools.partial(faces_kernel, plan, ring, parts),
        [SMEM] + [ANY] * 6 + [VMEM] * parts,
        [slab(nx), slab(nx), slab(ny), slab(ny)],
        "faces",
        1 << 22,
        [pltpu.VMEM((plan.sent, nx * ny, depth), F32)] + held,
    )(owner, *fields, *received)
    from_y_low = move(y_high, "gy", 1)
    from_y_high = move(y_low, "gy", -1)
    from_x_low = move(x_high, "gx", 1)
    from_x_high = move(x_low, "gx", -1)
    inner = call(
        functools.partial(inner_kernel, plan, ring, parts),
        [SMEM] + [ANY] * 6 + [VMEM] * parts,
        [jax.ShapeDtypeStruct((plan.chan, nx * plan.pitch, depth), F32)],
        "inner",
        1 << 24,
        held,
    )(owner, *fields, *received)[0]

    def rows(value):
        return value.reshape(-1, depth)

    corner = jax.ShapeDtypeStruct((plan.slab * 2 * w, depth), F32)
    c_low, c_high = call(
        functools.partial(corners_kernel, plan), [VMEM] * 2 + [ANY], [corner, corner], "corners", 1 << 20
    )(rows(from_y_low), rows(from_y_high), inner)
    shape = (plan.slab, 2 * w, depth)
    from_c_low = move(c_high, "gx", 1).reshape(shape)
    from_c_high = move(c_low, "gx", -1).reshape(shape)
    height = plan.wide * plan.pitch + 2 * PAD
    flow, solute = call(
        functools.partial(steps_kernel, plan),
        [SMEM, ANY] + [VMEM] * 6,
        [jax.ShapeDtypeStruct(flow_adjoint.shape, F32), jax.ShapeDtypeStruct(solute_adjoint.shape, F32)],
        "steps",
        1 << 28,
        [
            pltpu.VMEM((SOLID, height, depth), F32),
            pltpu.VMEM((SOLID, height, depth), F32),
            pltpu.VMEM((plan.chan - SOLID, height, depth), F32),
            pltpu.VMEM((3, height, depth), F32),
            pltpu.SemaphoreType.DMA((2,)),
        ],
    )(owner, inner, from_y_low, from_y_high, from_x_low, from_x_high, from_c_low, from_c_high)
    return (flow, solute)


def solution(mesh):
    in_specs = (
        P(None, "gx", "gy", "gz"),
        P(None, "gx", "gy", "gz"),
        P(None, "gx", "gy", "gz"),
        P(None, None, "gx", "gy", "gz"),
        P(None, "gx", "gy", "gz"),
        P("gx", "gy", "gz"),
        P(),
    )
    out_specs = (P(None, "gx", "gy", "gz"), P(None, "gx", "gy", "gz"))
    return jax.shard_map(
        per_device, mesh=mesh, in_specs=in_specs, out_specs=out_specs, check_vma=False
    )
```

```python
import functools

import jax
import jax.numpy as jnp
from jax import lax
from jax.experimental import pallas as pl
from jax.experimental.pallas import tpu as pltpu
from jax.sharding import PartitionSpec as P

BZC = 16

FLOW_DIRS = [
    (0, 0, 0),
    (1, 0, 0),
    (-1, 0, 0),
    (0, 1, 0),
    (0, -1, 0),
    (0, 0, 1),
    (0, 0, -1),
    (1, 1, 0),
    (-1, -1, 0),
    (1, -1, 0),
    (-1, 1, 0),
    (1, 0, 1),
    (-1, 0, -1),
    (1, 0, -1),
    (-1, 0, 1),
    (0, 1, 1),
    (0, -1, -1),
    (0, 1, -1),
    (0, -1, 1),
]
NF = 19
NS = 7
OPPOSITE = [FLOW_DIRS.index((-a, -b, -c)) for a, b, c in FLOW_DIRS]
SOLID = NF + NS
AUX = SOLID + 1
NA = 5
flow_omega = 1.25
solute_omega = 1.6
langmuir_rate = 0.05
VMEM_LIMIT = 50 * 1024 * 1024
F32 = jnp.float32


class Plan:
    def __init__(self, steps, nx, ny, depth):
        self.steps, self.nx, self.ny, self.depth = steps, nx, ny, depth
        self.halo = w = steps
        self.chan = AUX + NA * steps
        self.sent = AUX + NA * (steps - 1)
        self.pitch = -(-(ny + 2 * w) // 8) * 8
        self.wide = nx + 2 * w
        self.count = {k: AUX + NA * (steps - k) for k in range(1, w)}
        self.base, at = {}, 0
        for k in range(1, w):
            self.base[k] = at
            at += self.count[k]
        self.base[w] = at
        self.slab = at + 7

    def last(self, axis, sign):
        flow = [i for i, c in enumerate(FLOW_DIRS) if c[axis] == sign]
        solute = [NF + i for i, c in enumerate(FLOW_DIRS[:NS]) if c[axis] == sign]
        return flow + solute + [SOLID]


def lanes(depth):
    return lax.broadcasted_iota(jnp.int32, (8, depth), 1)


def occupied(owner_ref):
    me = lax.axis_index("gz")
    count = jnp.int32(0)
    for j in range(owner_ref.shape[0]):
        count = count + jnp.where(owner_ref[j] == me, 1, 0).astype(jnp.int32)
    return count * BZC


def z_places(plan, length, ring):
    w, depth = plan.halo, plan.depth
    if ring == 2:
        first = lax.axis_index("gz") == 0
        return [(jnp.where(first, length - w, 0), jnp.where(first, length, depth - w))]
    return [(length - w, jnp.int32(depth - w)), (jnp.int32(0), length)]


def each(number, body, unroll=4):
    def several(i, carry):
        for u in range(unroll):
            body(i * unroll + u)
        return carry

    turns = number // unroll
    if turns > 1:
        lax.fori_loop(0, turns, several, 0)
    else:
        turns = 0
    for i in range(turns * unroll, number):
        body(i)


def fetch(arrays, held, sems):
    copies = [pltpu.make_async_copy(a, b, sems.at[i]) for i, (a, b) in enumerate(zip(arrays, held))]
    for copy in copies:
        copy.start()
    return copies


def gather(plan, arrays, held, wide, sems, steps, body):
    copies = fetch(arrays, held, sems)
    flow, solute, density, velocity, level, solid = held
    ny = plan.ny
    copies[0].wait()
    body(0, NF, flow)
    for copy in copies[1:]:
        copy.wait()
    body(NF, NS, solute)
    sources = [(solid, 0)]
    for s in range(steps):
        t = plan.steps - 1 - s
        sources += [(density, t), (level, t), (velocity, 3 * t), (velocity, 3 * t + 1), (velocity, 3 * t + 2)]

    for c, (ref, i) in enumerate(sources):
        for x in range(plan.nx):
            wide[c, x * ny : (x + 1) * ny, :] = ref[i, x * ny : (x + 1) * ny, :].astype(F32)
    body(SOLID, len(sources), wide)


def tiles_of(plan):
    return [(y * (plan.nx // 8) + h, y, 8 * h) for y in range(plan.ny) for h in range(plan.nx // 8)]


def pack_kernel(plan, ring, parts, *refs):
    owner, arrays, outs, held, wide, sems = refs[0], refs[1:7], refs[7 : 7 + parts], refs[7 + parts : 13 + parts], refs[-2], refs[-1]
    w, depth, ny = plan.halo, plan.depth, plan.ny
    length = occupied(owner)
    group = lanes(depth) // w
    places = z_places(plan, length, ring)
    shifts = [{n: (w * n + depth - start) & (depth - 1) for n, _, _ in tiles_of(plan)} for start, _ in places]

    def body(at, number, ref):
        def one(i):
            packed = [None] * parts
            for n, y, x in tiles_of(plan):
                tile = ref[i, pl.ds(x * ny + y, 8, stride=ny), :]
                for p in range(parts):
                    moved = pltpu.roll(tile, shifts[p][n], 1)
                    packed[p] = moved if n == 0 else jnp.where(group == n, moved, packed[p])
            for p in range(parts):
                outs[p][at + i] = packed[p]

        each(number, one, 3)

    gather(plan, arrays, held, wide, sems, plan.steps - 1, body)


def faces_kernel(plan, *refs):
    arrays, (y_low, y_high), held, wide, sems = refs[:6], refs[7:9], refs[9:15], refs[15], refs[16]
    w, nx, ny = plan.halo, plan.nx, plan.ny

    def body(at, number, ref):
        def row(c, y):
            return ref[c, pl.ds(y, nx, stride=ny), :]

        for k in range(1, w):

            def one(c, k=k):
                y_low[plan.base[k] + at + c] = row(c, k - 1)
                y_high[plan.base[k] + at + c] = row(c, ny - k)

            each(min(number, plan.count[k] - at), one)
        for out, sign, y in ((y_low, 1, w - 1), (y_high, -1, ny - w)):
            for j, c in enumerate(plan.last(1, sign)):
                if at <= c < at + number:
                    out[plan.base[w] + j] = row(c - at, y)

    gather(plan, arrays, held, wide, sems, plan.steps - 1, body)


def column(plan, ring, owner, received):
    w, depth = plan.halo, plan.depth
    length = occupied(owner)
    lane = lanes(depth)
    live = lane < length
    places = [to for _, to in z_places(plan, length, ring)]
    halos = [((lane - to) & (depth - 1)) < w for to in places]
    shifts = [{n: (to + depth - w * n) & (depth - 1) for n, _, _ in tiles_of(plan)} for to in places]

    def put(tile, slabs, n):
        tile = jnp.where(live, tile, 0.0)
        for slab, halo, shift in zip(slabs, halos, shifts):
            tile = jnp.where(halo, pltpu.roll(slab, shift[n], 1), tile)
        return tile

    return put


def insert_kernel(plan, ring, parts, owner, low, high, *rest):
    received, (y_low, y_high) = rest[:parts], rest[parts:]
    put = column(plan, ring, owner, received)
    w, ny = plan.halo, plan.ny
    tall = plan.nx // 8

    def one(raw, out, j, c, y):
        slabs = [r[c] for r in received]
        for h in range(tall):
            out[j, 8 * h : 8 * h + 8, :] = put(raw[j, 8 * h : 8 * h + 8, :], slabs, y * tall + h)

    for k in range(1, w):

        def both(c, k=k):
            one(low, y_low, plan.base[k] + c, c, k - 1)
            one(high, y_high, plan.base[k] + c, c, ny - k)

        each(plan.count[k], both)
    for raw, out, sign, y in ((low, y_low, 1, w - 1), (high, y_high, -1, ny - w)):
        for j, c in enumerate(plan.last(1, sign)):
            one(raw, out, plan.base[w] + j, c, y)


def inner_kernel(plan, ring, parts, *refs):
    owner, arrays, received, rest = refs[0], refs[1:7], refs[7 : 7 + parts], refs[7 + parts :]
    (out, x_low, x_high), held, wide, sems = rest[:3], rest[3:9], rest[9], rest[10]
    w, nx, ny, pitch = plan.halo, plan.nx, plan.ny, plan.pitch
    put = column(plan, ring, owner, received)

    def body(at, number, ref):
        def one(i, sent=True):
            slabs = [r[at + i] for r in received] if sent else []
            for n, y, x in tiles_of(plan):
                tile = ref[i, pl.ds(x * ny + y, 8, stride=ny), :]
                out[at + i, pl.ds(x * pitch + w + y, 8, stride=pitch), :] = put(tile, slabs, n)

        within = min(number, plan.sent - at)
        each(within, one, 3)
        each(number - within, lambda i: one(within + i, False), 1)

    gather(plan, arrays, held, wide, sems, plan.steps, body)

    def row(c, x):
        return out[c, x * pitch + w : x * pitch + w + ny, :]

    for k in range(1, w):

        def both(c, k=k):
            x_low[plan.base[k] + c] = row(c, k - 1)
            x_high[plan.base[k] + c] = row(c, nx - k)

        each(plan.count[k], both)
    for slab, sign, x in ((x_low, 1, w - 1), (x_high, -1, nx - w)):
        for j, c in enumerate(plan.last(0, sign)):
            slab[plan.base[w] + j] = row(c, x)


def corners_kernel(plan, from_low, from_high, inner, low, high):
    w, nx, ny = plan.halo, plan.nx, plan.ny
    low[...] = jnp.zeros(low.shape, F32)
    high[...] = jnp.zeros(high.shape, F32)
    tall = 2 * w
    for out, sign in ((low, 1), (high, -1)):
        x_last = plan.last(0, sign)
        for k in range(1, w + 1):
            x = k - 1 if sign == 1 else nx - k
            for m in range(1, w + 1):
                for source, row, y_sign in ((from_low, w - m, -1), (from_high, w - 1 + m, 1)):
                    y_last = plan.last(1, y_sign)
                    if k < w and m < w:
                        number = min(plan.count[k], plan.count[m])
                        out[pl.ds(plan.base[k] * tall + row, number, stride=tall), :] = source[
                            pl.ds(plan.base[m] * nx + x, number, stride=nx), :
                        ]
                        continue
                    for c in range(AUX):
                        if (k == w and c not in x_last) or (m == w and c not in y_last):
                            continue
                        to = plan.base[k] + (x_last.index(c) if k == w else c)
                        at = plan.base[m] + (y_last.index(c) if m == w else c)
                        out[to * tall + row : to * tall + row + 1, :] = source[at * nx + x : at * nx + x + 1, :]


PAD = 8


def steps_kernel(plan, owner, inner, y_low, y_high, x_low, x_high, c_low, c_high, flow_out, solute_out, cells, other, fields, masks, sems):
    w, nx, ny, depth, pitch = plan.halo, plan.nx, plan.ny, plan.depth, plan.pitch
    middle = pl.ds(PAD + w * pitch, nx * pitch)
    copies = [
        pltpu.make_async_copy(inner.at[pl.ds(0, SOLID)], cells.at[:, middle, :], sems.at[0]),
        pltpu.make_async_copy(inner.at[pl.ds(SOLID, plan.chan - SOLID)], fields.at[:, middle, :], sems.at[1]),
    ]
    for copy in copies:
        copy.start()

    def channels(number, body):
        each(SOLID, lambda c: body(cells, c, c))
        each(number - SOLID, lambda c: body(fields, c, SOLID + c))

    def channel(c):
        return (cells, c) if c < SOLID else (fields, c - SOLID)

    for k in range(1, w + 1):
        for x_part, c_part, x, sign in ((x_low, c_low, w - k, -1), (x_high, c_high, w + nx - 1 + k, 1)):
            row = PAD + x * pitch

            def one(ref, c, j, row=row, x_part=x_part, c_part=c_part):
                ref[c, row : row + w, :] = c_part[j, 0:w, :]
                ref[c, row + w : row + w + ny, :] = x_part[j]
                ref[c, row + w + ny : row + w + ny + w, :] = c_part[j, w : 2 * w, :]

            if k < w:
                channels(plan.count[k], lambda ref, c, j, one=one, k=k: one(ref, c, plan.base[k] + j))
            else:
                for j, c in enumerate(plan.last(0, sign)):
                    one(*channel(c), plan.base[w] + j)
    for copy in copies:
        copy.wait()
    for m in range(1, w + 1):
        for part, y, sign in ((y_low, w - m, -1), (y_high, w + ny - 1 + m, 1)):
            row = PAD + w * pitch + y

            def one(ref, c, j, row=row, part=part):
                ref[c, pl.ds(row, nx, stride=pitch), :] = part[j]

            if m < w:
                channels(plan.count[m], lambda ref, c, j, one=one, m=m: one(ref, c, plan.base[m] + j))
            else:
                for j, c in enumerate(plan.last(1, sign)):
                    one(*channel(c), plan.base[w] + j)

    length = occupied(owner)
    lane = lanes(depth)
    gx, gy, gz = (lax.axis_index(a) for a in ("gx", "gy", "gz"))
    last_x, last_y, last_z = (lax.axis_size(a) - 1 for a in ("gx", "gy", "gz"))
    above = jnp.where(gz < last_z, w, 0)
    below = jnp.where(gz > 0, w, 0)
    in_z = (lane < length + above) | (lane >= depth - below)
    y_first = jnp.where(gy > 0, 0, w)
    y_end = jnp.where(gy < last_y, ny + 2 * w, w + ny)
    x_first = jnp.where(gx > 0, 0, w)
    x_end = jnp.where(gx < last_x, nx + 2 * w, w + nx)
    sub = lax.broadcasted_iota(jnp.int32, (8, depth), 0)

    def prepare(x, carry):
        in_x = ((x >= x_first) & (x < x_end)).astype(F32)
        for h in range(pitch // 8):
            row = pl.multiple_of(PAD + x * pitch + 8 * h, 8)
            flags = fields[0, pl.ds(row, 8), :]
            y = sub + 8 * h
            masks[0, pl.ds(row, 8), :] = pltpu.roll(flags, depth - 1, 1)
            masks[1, pl.ds(row, 8), :] = pltpu.roll(flags, 1, 1)
            inside = in_z & (y >= y_first) & (y < y_end) & (flags == 0.0)
            masks[2, pl.ds(row, 8), :] = jnp.where(inside, in_x, 0.0)
        return carry

    lax.fori_loop(0, plan.wide, prepare, 0)

    live = lane < length

    def tile(source, s, row, write):
        def field(ref, c, move=0):
            return ref[c, pl.ds(row + move, 8), :]

        blocked = {}

        def reads(first, number):
            result = []
            for i in range(number):
                sx, sy, sz = FLOW_DIRS[i]
                if i == 0:
                    result.append(field(source, first))
                    continue
                move = sx * pitch + sy
                near = field(source, first + i, move)
                if sz:
                    near = pltpu.roll(near, (depth - sz) % depth, 1)
                if i not in blocked:
                    flags = field(fields, 0, move) if sz == 0 else field(masks, 0 if sz == 1 else 1, move)
                    blocked[i] = flags != 0.0
                result.append(jnp.where(blocked[i], field(source, first + OPPOSITE[i]), near))
            return result

        valid = field(masks, 2)
        if s == plan.steps - 1:
            valid = jnp.where(live, valid, 0.0)
        aux = AUX - SOLID + NA * s
        density, level, ux, uy, uz = (field(fields, aux + n) for n in range(NA))

        h = reads(NF, NS)
        px, py, pz = h[1] - h[2], h[3] - h[4], h[5] - h[6]
        p0 = 0.25 * h[0] + 0.125 * ((h[1] + h[2]) + (h[3] + h[4]) + (h[5] + h[6]))
        grown = 1.0 + level
        uptake = langmuir_rate / (grown * grown)
        common = valid * (
            (solute_omega - uptake) * p0 + (solute_omega * 0.5) * (px * ux + py * uy + pz * uz)
        )
        keep = (1.0 - solute_omega) * valid
        for i in range(NS):
            write(NF + i, keep * h[i] + common)
        factor = (0.5 * solute_omega) * level / jnp.maximum(density, 0.5)
        fx, fy, fz = factor * px, factor * py, factor * pz

        g = reads(0, NF)
        a = {i: g[i] + g[i + 1] for i in range(1, NF, 2)}
        d = {i: g[i] - g[i + 1] for i in range(1, NF, 2)}
        m1x = (d[1] + d[1]) + (d[7] + d[9]) + (d[11] + d[13])
        m1y = (d[3] + d[3]) + (d[7] - d[9]) + (d[15] + d[17])
        m1z = (d[5] + d[5]) + (d[11] - d[13]) + (d[15] - d[17])
        exy, exz, eyz = a[7] + a[9], a[11] + a[13], a[15] + a[17]
        tx, ty, tz = a[1] + a[1], a[3] + a[3], a[5] + a[5]
        mxx, myy, mzz = tx + exy + exz, ty + exy + eyz, tz + exz + eyz
        mxy, mxz, myz = a[7] - a[9], a[11] - a[13], a[15] - a[17]
        m0 = 12.0 * g[0] + (tx + ty + tz) + (exy + exz + eyz)
        qx = mxx * ux + mxy * uy + mxz * uz
        qy = mxy * ux + myy * uy + myz * uz
        qz = mxz * ux + myz * uy + mzz * uz
        square = ux * ux + uy * uy + uz * uz
        scaled = flow_omega / 36.0
        zero = m0 * (scaled + (1.5 * scaled) * square) - (4.5 * scaled) * (qx * ux + qy * uy + qz * uz)
        zero = valid * (zero - (fx * ux + fy * uy + fz * uz))
        bx = valid * ((3.0 * scaled) * (m1x + 3.0 * qx - m0 * ux) + fx)
        by = valid * ((3.0 * scaled) * (m1y + 3.0 * qy - m0 * uy) + fy)
        bz = valid * ((3.0 * scaled) * (m1z + 3.0 * qz - m0 * uz) + fz)
        keep = (1.0 - flow_omega) * valid
        write(0, keep * g[0] + zero)
        moves = {1: bx, 3: by, 5: bz, 7: bx + by, 9: bx - by, 11: bx + bz, 13: bx - bz, 15: by + bz, 17: by - bz}
        for i, move in moves.items():
            write(i, keep * g[i] + (zero + move))
            write(i + 1, keep * g[i + 1] + (zero - move))

    buffers = [cells, other]
    for s in range(plan.steps - 1):
        source, target = buffers[s % 2], buffers[(s + 1) % 2]
        first = PAD + (1 + s) * pitch

        def body(n, carry, source=source, target=target, first=first, s=s):
            for h in range(pitch // 8):
                row = pl.multiple_of(first + pitch * n + 8 * h, 8)

                def write(c, value, row=row):
                    target[c, pl.ds(row, 8), :] = value

                tile(source, s, row, write)
            return carry

        lax.fori_loop(0, plan.wide - 2 - 2 * s, body, 0)

    s = plan.steps - 1
    source = buffers[s % 2]

    def last(x, carry):
        for h in range(ny // 8):
            row = PAD + (x + w) * pitch + w + 8 * h

            def write(c, value, h=h):
                if c < NF:
                    flow_out[c, x, 8 * h : 8 * h + 8, :] = value
                else:
                    solute_out[c - NF, x, 8 * h : 8 * h + 8, :] = value

            tile(source, s, row, write)
        return carry

    lax.fori_loop(0, nx, last, 0)


VMEM = pl.BlockSpec(memory_space=pltpu.VMEM)
SMEM = pl.BlockSpec(memory_space=pltpu.SMEM)
ANY = pl.BlockSpec(memory_space=pl.ANY)


def call(kernel, ins, outs, name, cost, scratch=(), limit=VMEM_LIMIT):
    return pl.pallas_call(
        kernel,
        in_specs=ins,
        out_shape=outs,
        out_specs=[VMEM] * len(outs),
        scratch_shapes=list(scratch),
        name=name,
        cost_estimate=pl.CostEstimate(flops=cost, bytes_accessed=1 << 23, transcendentals=0),
        compiler_params=pltpu.CompilerParams(vmem_limit_bytes=limit),
    )


def per_device(flow_adjoint, solute_adjoint, flow_density, flow_velocity, solute_level, solid, owner):
    steps = flow_density.shape[0]
    nx, ny, depth = solid.shape
    plan = Plan(steps, nx, ny, depth)
    ring = lax.axis_size("gz")
    w = plan.halo
    arguments = (flow_adjoint, solute_adjoint, flow_density, flow_velocity, solute_level, solid)
    fields = [f.reshape(-1, nx * ny, depth) for f in arguments]

    def move(value, axis, by):
        size = lax.axis_size(axis)
        return lax.ppermute(value, axis, [(i, i + by) for i in range(size) if 0 <= i + by < size])

    def scratch(steps):
        held = [pltpu.VMEM(f.shape, f.dtype) for f in fields]
        wide = pltpu.VMEM((AUX - SOLID + NA * steps, nx * ny, depth), F32)
        return held + [wide, pltpu.SemaphoreType.DMA((len(fields),))]

    parts = 1 if ring == 2 else 2
    packed = call(
        functools.partial(pack_kernel, plan, ring, parts),
        [SMEM] + [ANY] * 6,
        [jax.ShapeDtypeStruct((plan.sent, 8, depth), F32)] * parts,
        "pack_column",
        1 << 22,
        scratch(steps - 1),
        60 << 20,
    )(owner, *fields)
    if ring == 2:
        received = [lax.ppermute(packed[0], "gz", [(0, 1), (1, 0)])]
    else:
        received = [move(packed[0], "gz", 1), move(packed[1], "gz", -1)]

    slab = [jax.ShapeDtypeStruct((plan.slab, nx, depth), F32)] * 2
    raw = call(functools.partial(faces_kernel, plan), [ANY] * 7, slab, "faces", 1 << 24, scratch(steps - 1), 24 << 20)(
        *fields, packed[0]
    )
    y_low, y_high = call(
        functools.partial(insert_kernel, plan, ring, parts), [SMEM] + [VMEM] * (2 + parts), slab, "insert", 1 << 22, (), 24 << 20
    )(owner, *raw, *received)
    from_y_low = move(y_high, "gy", 1)
    from_y_high = move(y_low, "gy", -1)
    inner, x_low, x_high = call(
        functools.partial(inner_kernel, plan, ring, parts),
        [SMEM] + [ANY] * 6 + [VMEM] * parts,
        [jax.ShapeDtypeStruct((plan.chan, nx * plan.pitch, depth), F32)] + [jax.ShapeDtypeStruct((plan.slab, ny, depth), F32)] * 2,
        "inner",
        1 << 24,
        scratch(steps),
    )(owner, *fields, *received)
    from_x_low = move(x_high, "gx", 1)
    from_x_high = move(x_low, "gx", -1)

    def rows(value):
        return value.reshape(-1, depth)

    corner = jax.ShapeDtypeStruct((plan.slab * 2 * w, depth), F32)
    c_low, c_high = call(
        functools.partial(corners_kernel, plan), [VMEM] * 2 + [ANY], [corner, corner], "corners", 1 << 20
    )(rows(from_y_low), rows(from_y_high), inner)
    shape = (plan.slab, 2 * w, depth)
    from_c_low = move(c_high, "gx", 1).reshape(shape)
    from_c_high = move(c_low, "gx", -1).reshape(shape)
    height = plan.wide * plan.pitch + 2 * PAD
    flow, solute = call(
        functools.partial(steps_kernel, plan),
        [SMEM, ANY] + [VMEM] * 6,
        [jax.ShapeDtypeStruct(flow_adjoint.shape, F32), jax.ShapeDtypeStruct(solute_adjoint.shape, F32)],
        "steps",
        1 << 28,
        [
            pltpu.VMEM((SOLID, height, depth), F32),
            pltpu.VMEM((SOLID, height, depth), F32),
            pltpu.VMEM((plan.chan - SOLID, height, depth), F32),
            pltpu.VMEM((3, height, depth), F32),
            pltpu.SemaphoreType.DMA((2,)),
        ],
    )(owner, inner, from_y_low, from_y_high, from_x_low, from_x_high, from_c_low, from_c_high)
    return (flow, solute)


def solution(mesh):
    in_specs = (
        P(None, "gx", "gy", "gz"),
        P(None, "gx", "gy", "gz"),
        P(None, "gx", "gy", "gz"),
        P(None, None, "gx", "gy", "gz"),
        P(None, "gx", "gy", "gz"),
        P("gx", "gy", "gz"),
        P(),
    )
    out_specs = (P(None, "gx", "gy", "gz"), P(None, "gx", "gy", "gz"))
    return jax.shard_map(
        per_device, mesh=mesh, in_specs=in_specs, out_specs=out_specs, check_vma=False
    )
```

```python
import functools

import jax
import jax.numpy as jnp
from jax import lax
from jax.experimental import pallas as pl
from jax.experimental.pallas import tpu as pltpu
from jax.sharding import PartitionSpec as P

BZC = 16

FLOW_DIRS = [
    (0, 0, 0),
    (1, 0, 0),
    (-1, 0, 0),
    (0, 1, 0),
    (0, -1, 0),
    (0, 0, 1),
    (0, 0, -1),
    (1, 1, 0),
    (-1, -1, 0),
    (1, -1, 0),
    (-1, 1, 0),
    (1, 0, 1),
    (-1, 0, -1),
    (1, 0, -1),
    (-1, 0, 1),
    (0, 1, 1),
    (0, -1, -1),
    (0, 1, -1),
    (0, -1, 1),
]
NF = 19
NS = 7
OPPOSITE = [FLOW_DIRS.index((-a, -b, -c)) for a, b, c in FLOW_DIRS]
SOLID = NF + NS
AUX = SOLID + 1
NA = 5
flow_omega = 1.25
solute_omega = 1.6
langmuir_rate = 0.05
VMEM_LIMIT = 24 << 20
F32 = jnp.float32


class Plan:
    def __init__(self, steps, nx, ny, depth):
        self.steps, self.nx, self.ny, self.depth = steps, nx, ny, depth
        self.halo = w = steps
        self.chan = AUX + NA * steps
        self.sent = AUX + NA * (steps - 1)
        self.pitch = -(-(ny + 2 * w) // 8) * 8
        self.wide = nx + 2 * w
        self.count = {k: AUX + NA * (steps - k) for k in range(1, w)}
        self.base, at = {}, 0
        for k in range(1, w):
            self.base[k] = at
            at += self.count[k]
        self.base[w] = at
        self.slab = at + 7

    def last(self, axis, sign):
        flow = [i for i, c in enumerate(FLOW_DIRS) if c[axis] == sign]
        solute = [NF + i for i, c in enumerate(FLOW_DIRS[:NS]) if c[axis] == sign]
        return flow + solute + [SOLID]


def lanes(depth):
    return lax.broadcasted_iota(jnp.int32, (8, depth), 1)


def occupied(owner_ref):
    me = lax.axis_index("gz")
    count = jnp.int32(0)
    for j in range(owner_ref.shape[0]):
        count = count + jnp.where(owner_ref[j] == me, 1, 0).astype(jnp.int32)
    return count * BZC


def z_places(plan, length, ring):
    w, depth = plan.halo, plan.depth
    if ring == 2:
        first = lax.axis_index("gz") == 0
        return [(jnp.where(first, length - w, 0), jnp.where(first, length, depth - w))]
    return [(length - w, jnp.int32(depth - w)), (jnp.int32(0), length)]


def each(number, body, unroll=4):
    def several(i, carry):
        for u in range(unroll):
            body(i * unroll + u)
        return carry

    turns = number // unroll
    if turns > 1:
        lax.fori_loop(0, turns, several, 0)
    else:
        turns = 0
    for i in range(turns * unroll, number):
        body(i)


def fetch(arrays, held, sems):
    copies = [pltpu.make_async_copy(a, b, sems.at[i]) for i, (a, b) in enumerate(zip(arrays, held))]
    for copy in copies:
        copy.start()
    return copies


def gather(plan, arrays, held, wide, sems, steps, body):
    copies = fetch(arrays, held, sems)
    flow, solute, density, velocity, level, solid = held
    ny = plan.ny
    copies[0].wait()
    body(0, NF, flow)
    for copy in copies[1:]:
        copy.wait()
    body(NF, NS, solute)
    sources = [(solid, 0)]
    for s in range(steps):
        t = plan.steps - 1 - s
        sources += [(density, t), (level, t), (velocity, 3 * t), (velocity, 3 * t + 1), (velocity, 3 * t + 2)]

    for c, (ref, i) in enumerate(sources):
        for x in range(plan.nx):
            wide[c, x * ny : (x + 1) * ny, :] = ref[i, x * ny : (x + 1) * ny, :].astype(F32)
    body(SOLID, len(sources), wide)


def tiles_of(plan):
    return [(y * (plan.nx // 8) + h, y, 8 * h) for y in range(plan.ny) for h in range(plan.nx // 8)]


def pack_kernel(plan, ring, parts, *refs):
    owner, arrays, outs, held, wide, sems = refs[0], refs[1:7], refs[7 : 7 + parts], refs[7 + parts : 13 + parts], refs[-2], refs[-1]
    w, depth, ny = plan.halo, plan.depth, plan.ny
    length = occupied(owner)
    group = lanes(depth) // w
    places = z_places(plan, length, ring)
    shifts = [{n: (w * n + depth - start) & (depth - 1) for n, _, _ in tiles_of(plan)} for start, _ in places]

    def body(at, number, ref):
        def one(i):
            packed = [None] * parts
            for n, y, x in tiles_of(plan):
                tile = ref[i, pl.ds(x * ny + y, 8, stride=ny), :]
                for p in range(parts):
                    moved = pltpu.roll(tile, shifts[p][n], 1)
                    packed[p] = moved if n == 0 else jnp.where(group == n, moved, packed[p])
            for p in range(parts):
                outs[p][at + i] = packed[p]

        each(number, one, 3)

    gather(plan, arrays, held, wide, sems, plan.steps - 1, body)


def faces_kernel(plan, *refs):
    arrays, (y_low, y_high), held, wide, sems = refs[:6], refs[7:9], refs[9:15], refs[15], refs[16]
    w, nx, ny = plan.halo, plan.nx, plan.ny

    def body(at, number, ref):
        def row(c, y):
            return ref[c, pl.ds(y, nx, stride=ny), :]

        for k in range(1, w):

            def one(c, k=k):
                y_low[plan.base[k] + at + c] = row(c, k - 1)
                y_high[plan.base[k] + at + c] = row(c, ny - k)

            each(min(number, plan.count[k] - at), one)
        for out, sign, y in ((y_low, 1, w - 1), (y_high, -1, ny - w)):
            for j, c in enumerate(plan.last(1, sign)):
                if at <= c < at + number:
                    out[plan.base[w] + j] = row(c - at, y)

    gather(plan, arrays, held, wide, sems, plan.steps - 1, body)


def column(plan, ring, owner, received):
    w, depth = plan.halo, plan.depth
    length = occupied(owner)
    lane = lanes(depth)
    live = lane < length
    places = [to for _, to in z_places(plan, length, ring)]
    halos = [((lane - to) & (depth - 1)) < w for to in places]
    shifts = [{n: (to + depth - w * n) & (depth - 1) for n, _, _ in tiles_of(plan)} for to in places]

    def put(tile, slabs, n):
        tile = jnp.where(live, tile, 0.0)
        for slab, halo, shift in zip(slabs, halos, shifts):
            tile = jnp.where(halo, pltpu.roll(slab, shift[n], 1), tile)
        return tile

    return put


def insert_kernel(plan, ring, parts, owner, low, high, *rest):
    received, (y_low, y_high) = rest[:parts], rest[parts:]
    put = column(plan, ring, owner, received)
    w, ny = plan.halo, plan.ny
    tall = plan.nx // 8

    def one(raw, out, j, c, y):
        slabs = [r[c] for r in received]
        for h in range(tall):
            out[j, 8 * h : 8 * h + 8, :] = put(raw[j, 8 * h : 8 * h + 8, :], slabs, y * tall + h)

    for k in range(1, w):

        def both(c, k=k):
            one(low, y_low, plan.base[k] + c, c, k - 1)
            one(high, y_high, plan.base[k] + c, c, ny - k)

        each(plan.count[k], both, 10)
    for raw, out, sign, y in ((low, y_low, 1, w - 1), (high, y_high, -1, ny - w)):
        for j, c in enumerate(plan.last(1, sign)):
            one(raw, out, plan.base[w] + j, c, y)


def inner_kernel(plan, ring, parts, *refs):
    owner, arrays, received, rest = refs[0], refs[1:7], refs[7 : 7 + parts], refs[7 + parts :]
    (out, x_low, x_high), held, wide, sems = rest[:3], rest[3:9], rest[9], rest[10]
    w, nx, ny, pitch = plan.halo, plan.nx, plan.ny, plan.pitch
    put = column(plan, ring, owner, received)

    def body(at, number, ref):
        def one(i, sent=True):
            slabs = [r[at + i] for r in received] if sent else []
            for n, y, x in tiles_of(plan):
                tile = ref[i, pl.ds(x * ny + y, 8, stride=ny), :]
                out[at + i, pl.ds(x * pitch + w + y, 8, stride=pitch), :] = put(tile, slabs, n)

        within = min(number, plan.sent - at)
        each(within, one, 3)
        each(number - within, lambda i: one(within + i, False), 1)

    gather(plan, arrays, held, wide, sems, plan.steps, body)

    def row(c, x):
        return out[c, x * pitch + w : x * pitch + w + ny, :]

    for k in range(1, w):

        def both(c, k=k):
            x_low[plan.base[k] + c] = row(c, k - 1)
            x_high[plan.base[k] + c] = row(c, nx - k)

        each(plan.count[k], both)
    for slab, sign, x in ((x_low, 1, w - 1), (x_high, -1, nx - w)):
        for j, c in enumerate(plan.last(0, sign)):
            slab[plan.base[w] + j] = row(c, x)


def corners_kernel(plan, from_low, from_high, inner, low, high):
    w, nx, ny = plan.halo, plan.nx, plan.ny
    low[...] = jnp.zeros(low.shape, F32)
    high[...] = jnp.zeros(high.shape, F32)
    tall = 2 * w
    for out, sign in ((low, 1), (high, -1)):
        x_last = plan.last(0, sign)
        for k in range(1, w + 1):
            x = k - 1 if sign == 1 else nx - k
            for m in range(1, w + 1):
                for source, row, y_sign in ((from_low, w - m, -1), (from_high, w - 1 + m, 1)):
                    y_last = plan.last(1, y_sign)
                    if k < w and m < w:
                        number = min(plan.count[k], plan.count[m])
                        out[pl.ds(plan.base[k] * tall + row, number, stride=tall), :] = source[
                            pl.ds(plan.base[m] * nx + x, number, stride=nx), :
                        ]
                        continue
                    for c in range(AUX):
                        if (k == w and c not in x_last) or (m == w and c not in y_last):
                            continue
                        to = plan.base[k] + (x_last.index(c) if k == w else c)
                        at = plan.base[m] + (y_last.index(c) if m == w else c)
                        out[to * tall + row : to * tall + row + 1, :] = source[at * nx + x : at * nx + x + 1, :]


PAD = 8


def channels(cells, fields, number, body):
    each(SOLID, lambda c: body(cells, c, c))
    each(number - SOLID, lambda c: body(fields, c, SOLID + c))


def insert_layers(plan, cells, fields, axis, parts, put):
    w = plan.halo
    for k in range(1, w + 1):
        for part, sign in zip(parts, (-1, 1)):
            if k < w:
                channels(
                    cells,
                    fields,
                    plan.count[k],
                    lambda ref, c, j, k=k, part=part, sign=sign: put(ref, c, part, plan.base[k] + j, k, sign),
                )
                continue
            for j, c in enumerate(plan.last(axis, sign)):
                ref, at = (cells, c) if c < SOLID else (fields, c - SOLID)
                put(ref, at, part, plan.base[w] + j, k, sign)


def first_kernel(plan, owner, inner, y_low, y_high, x_low, x_high, cells, fields, other, masks, sems):
    w, nx, ny, pitch = plan.halo, plan.nx, plan.ny, plan.pitch
    middle = pl.ds(PAD + w * pitch, nx * pitch)
    copies = [
        pltpu.make_async_copy(inner.at[pl.ds(0, SOLID)], cells.at[:, middle, :], sems.at[0]),
        pltpu.make_async_copy(inner.at[pl.ds(SOLID, plan.chan - SOLID)], fields.at[:, middle, :], sems.at[1]),
    ]
    for copy in copies:
        copy.start()

    def put_x(ref, c, part, j, k, sign):
        row = PAD + (w - k if sign < 0 else w + nx - 1 + k) * pitch + w
        ref[c, row : row + ny, :] = part[j]

    insert_layers(plan, cells, fields, 0, (x_low, x_high), put_x)
    for copy in copies:
        copy.wait()

    def put_y(ref, c, part, j, m, sign):
        row = PAD + w * pitch + (w - m if sign < 0 else w + ny - 1 + m)
        ref[c, pl.ds(row, nx, stride=pitch), :] = part[j]

    insert_layers(plan, cells, fields, 1, (y_low, y_high), put_y)
    prepare(plan, owner, fields, masks, w, w + nx)
    sweep(plan, owner, cells, other, fields, masks, 0, w + 1, w + nx - 1)


def steps_kernel(plan, owner, cells, fields, other, masks, c_low, c_high, flow_out, solute_out):
    w, nx, ny, pitch = plan.halo, plan.nx, plan.ny, plan.pitch

    def put(ref, c, part, j, k, sign):
        row = PAD + (w - k if sign < 0 else w + nx - 1 + k) * pitch
        ref[c, row : row + w, :] = part[j, 0:w, :]
        ref[c, row + w + ny : row + w + ny + w, :] = part[j, w : 2 * w, :]

    insert_layers(plan, cells, fields, 0, (c_low, c_high), put)
    prepare(plan, owner, fields, masks, 0, w)
    prepare(plan, owner, fields, masks, w + nx, plan.wide)
    sweep(plan, owner, cells, other, fields, masks, 0, 1, w + 1)
    sweep(plan, owner, cells, other, fields, masks, 0, w + nx - 1, plan.wide - 1)
    buffers = [cells, other]
    for s in range(1, plan.steps - 1):
        sweep(plan, owner, buffers[s % 2], buffers[(s + 1) % 2], fields, masks, s, 1 + s, plan.wide - 1 - s)
    s = plan.steps - 1
    source = buffers[s % 2]

    def last(x, carry):
        for h in range(ny // 8):
            row = PAD + (x + w) * pitch + w + 8 * h

            def write(c, value, h=h):
                if c < NF:
                    flow_out[c, x, 8 * h : 8 * h + 8, :] = value
                else:
                    solute_out[c - NF, x, 8 * h : 8 * h + 8, :] = value

            advance(plan, owner, source, fields, masks, s, row, write)
        return carry

    lax.fori_loop(0, nx, last, 0)


def prepare(plan, owner, fields, masks, from_x, to_x):
    w, nx, ny, depth, pitch = plan.halo, plan.nx, plan.ny, plan.depth, plan.pitch
    length = occupied(owner)
    lane = lanes(depth)
    gx, gy, gz = (lax.axis_index(a) for a in ("gx", "gy", "gz"))
    last_x, last_y, last_z = (lax.axis_size(a) - 1 for a in ("gx", "gy", "gz"))
    above = jnp.where(gz < last_z, w, 0)
    below = jnp.where(gz > 0, w, 0)
    in_z = (lane < length + above) | (lane >= depth - below)
    y_first = jnp.where(gy > 0, 0, w)
    y_end = jnp.where(gy < last_y, ny + 2 * w, w + ny)
    x_first = jnp.where(gx > 0, 0, w)
    x_end = jnp.where(gx < last_x, nx + 2 * w, w + nx)
    sub = lax.broadcasted_iota(jnp.int32, (8, depth), 0)

    def one(x, carry):
        in_x = ((x >= x_first) & (x < x_end)).astype(F32)
        for h in range(pitch // 8):
            row = pl.multiple_of(PAD + x * pitch + 8 * h, 8)
            flags = fields[0, pl.ds(row, 8), :]
            y = sub + 8 * h
            masks[0, pl.ds(row, 8), :] = pltpu.roll(flags, depth - 1, 1)
            masks[1, pl.ds(row, 8), :] = pltpu.roll(flags, 1, 1)
            inside = in_z & (y >= y_first) & (y < y_end) & (flags == 0.0)
            masks[2, pl.ds(row, 8), :] = jnp.where(inside, in_x, 0.0)
        return carry

    lax.fori_loop(from_x, to_x, one, 0)


def sweep(plan, owner, source, target, fields, masks, s, from_x, to_x):
    pitch = plan.pitch

    def body(x, carry):
        for h in range(pitch // 8):
            row = pl.multiple_of(PAD + pitch * x + 8 * h, 8)

            def write(c, value, row=row):
                target[c, pl.ds(row, 8), :] = value

            advance(plan, owner, source, fields, masks, s, row, write)
        return carry

    lax.fori_loop(from_x, to_x, body, 0)


def advance(plan, owner, source, fields, masks, s, row, write):
    depth, pitch = plan.depth, plan.pitch
    def field(ref, c, move=0):
        return ref[c, pl.ds(row + move, 8), :]

    blocked = {}

    def reads(first, number):
        result = []
        for i in range(number):
            sx, sy, sz = FLOW_DIRS[i]
            if i == 0:
                result.append(field(source, first))
                continue
            move = sx * pitch + sy
            near = field(source, first + i, move)
            if sz:
                near = pltpu.roll(near, (depth - sz) % depth, 1)
            if i not in blocked:
                flags = field(fields, 0, move) if sz == 0 else field(masks, 0 if sz == 1 else 1, move)
                blocked[i] = flags != 0.0
            result.append(jnp.where(blocked[i], field(source, first + OPPOSITE[i]), near))
        return result

    valid = field(masks, 2)
    if s == plan.steps - 1:
        valid = jnp.where(lanes(depth) < occupied(owner), valid, 0.0)
    aux = AUX - SOLID + NA * s
    density, level, ux, uy, uz = (field(fields, aux + n) for n in range(NA))

    h = reads(NF, NS)
    px, py, pz = h[1] - h[2], h[3] - h[4], h[5] - h[6]
    p0 = 0.25 * h[0] + 0.125 * ((h[1] + h[2]) + (h[3] + h[4]) + (h[5] + h[6]))
    grown = 1.0 + level
    uptake = langmuir_rate / (grown * grown)
    common = valid * (
        (solute_omega - uptake) * p0 + (solute_omega * 0.5) * (px * ux + py * uy + pz * uz)
    )
    keep = (1.0 - solute_omega) * valid
    for i in range(NS):
        write(NF + i, keep * h[i] + common)
    factor = (0.5 * solute_omega) * level / jnp.maximum(density, 0.5)
    fx, fy, fz = factor * px, factor * py, factor * pz

    g = reads(0, NF)
    a = {i: g[i] + g[i + 1] for i in range(1, NF, 2)}
    d = {i: g[i] - g[i + 1] for i in range(1, NF, 2)}
    m1x = (d[1] + d[1]) + (d[7] + d[9]) + (d[11] + d[13])
    m1y = (d[3] + d[3]) + (d[7] - d[9]) + (d[15] + d[17])
    m1z = (d[5] + d[5]) + (d[11] - d[13]) + (d[15] - d[17])
    exy, exz, eyz = a[7] + a[9], a[11] + a[13], a[15] + a[17]
    tx, ty, tz = a[1] + a[1], a[3] + a[3], a[5] + a[5]
    mxx, myy, mzz = tx + exy + exz, ty + exy + eyz, tz + exz + eyz
    mxy, mxz, myz = a[7] - a[9], a[11] - a[13], a[15] - a[17]
    m0 = 12.0 * g[0] + (tx + ty + tz) + (exy + exz + eyz)
    qx = mxx * ux + mxy * uy + mxz * uz
    qy = mxy * ux + myy * uy + myz * uz
    qz = mxz * ux + myz * uy + mzz * uz
    square = ux * ux + uy * uy + uz * uz
    scaled = flow_omega / 36.0
    zero = m0 * (scaled + (1.5 * scaled) * square) - (4.5 * scaled) * (qx * ux + qy * uy + qz * uz)
    zero = valid * (zero - (fx * ux + fy * uy + fz * uz))
    bx = valid * ((3.0 * scaled) * (m1x + 3.0 * qx - m0 * ux) + fx)
    by = valid * ((3.0 * scaled) * (m1y + 3.0 * qy - m0 * uy) + fy)
    bz = valid * ((3.0 * scaled) * (m1z + 3.0 * qz - m0 * uz) + fz)
    keep = (1.0 - flow_omega) * valid
    write(0, keep * g[0] + zero)
    moves = {1: bx, 3: by, 5: bz, 7: bx + by, 9: bx - by, 11: bx + bz, 13: bx - bz, 15: by + bz, 17: by - bz}
    for i, move in moves.items():
        write(i, keep * g[i] + (zero + move))
        write(i + 1, keep * g[i + 1] + (zero - move))


VMEM = pl.BlockSpec(memory_space=pltpu.VMEM)
SMEM = pl.BlockSpec(memory_space=pltpu.SMEM)
ANY = pl.BlockSpec(memory_space=pl.ANY)


def call(kernel, ins, outs, name, cost, scratch=(), limit=VMEM_LIMIT):
    return pl.pallas_call(
        kernel,
        in_specs=ins,
        out_shape=outs,
        out_specs=[VMEM] * len(outs),
        scratch_shapes=list(scratch),
        name=name,
        cost_estimate=pl.CostEstimate(flops=cost, bytes_accessed=1 << 23, transcendentals=0),
        compiler_params=pltpu.CompilerParams(vmem_limit_bytes=limit),
    )


def per_device(flow_adjoint, solute_adjoint, flow_density, flow_velocity, solute_level, solid, owner):
    steps = flow_density.shape[0]
    nx, ny, depth = solid.shape
    plan = Plan(steps, nx, ny, depth)
    ring = lax.axis_size("gz")
    w = plan.halo
    arguments = (flow_adjoint, solute_adjoint, flow_density, flow_velocity, solute_level, solid)
    fields = [f.reshape(-1, nx * ny, depth) for f in arguments]

    def move(value, axis, by):
        size = lax.axis_size(axis)
        return lax.ppermute(value, axis, [(i, i + by) for i in range(size) if 0 <= i + by < size])

    def scratch(steps):
        held = [pltpu.VMEM(f.shape, f.dtype) for f in fields]
        wide = pltpu.VMEM((AUX - SOLID + NA * steps, nx * ny, depth), F32)
        return held + [wide, pltpu.SemaphoreType.DMA((len(fields),))]

    parts = 1 if ring == 2 else 2
    packed = call(
        functools.partial(pack_kernel, plan, ring, parts),
        [SMEM] + [ANY] * 6,
        [jax.ShapeDtypeStruct((plan.sent, 8, depth), F32)] * parts,
        "pack_column",
        1 << 22,
        scratch(steps - 1),
        60 << 20,
    )(owner, *fields)
    if ring == 2:
        received = [lax.ppermute(packed[0], "gz", [(0, 1), (1, 0)])]
    else:
        received = [move(packed[0], "gz", 1), move(packed[1], "gz", -1)]

    slab = [jax.ShapeDtypeStruct((plan.slab, nx, depth), F32)] * 2
    raw = call(functools.partial(faces_kernel, plan), [ANY] * 7, slab, "faces", 1 << 24, scratch(steps - 1), 24 << 20)(
        *fields, packed[0]
    )
    y_low, y_high = call(
        functools.partial(insert_kernel, plan, ring, parts), [SMEM] + [VMEM] * (2 + parts), slab, "insert", 1 << 22, (), 24 << 20
    )(owner, *raw, *received)
    from_y_low = move(y_high, "gy", 1)
    from_y_high = move(y_low, "gy", -1)
    inner, x_low, x_high = call(
        functools.partial(inner_kernel, plan, ring, parts),
        [SMEM] + [ANY] * 6 + [VMEM] * parts,
        [jax.ShapeDtypeStruct((plan.chan, nx * plan.pitch, depth), F32)] + [jax.ShapeDtypeStruct((plan.slab, ny, depth), F32)] * 2,
        "inner",
        1 << 24,
        scratch(steps),
    )(owner, *fields, *received)
    from_x_low = move(x_high, "gx", 1)
    from_x_high = move(x_low, "gx", -1)

    def rows(value):
        return value.reshape(-1, depth)

    corner = jax.ShapeDtypeStruct((plan.slab * 2 * w, depth), F32)
    c_low, c_high = call(
        functools.partial(corners_kernel, plan), [VMEM] * 2 + [ANY], [corner, corner], "corners", 1 << 20
    )(rows(from_y_low), rows(from_y_high), inner)
    shape = (plan.slab, 2 * w, depth)
    from_c_low = move(c_high, "gx", 1).reshape(shape)
    from_c_high = move(c_low, "gx", -1).reshape(shape)
    height = plan.wide * plan.pitch + 2 * PAD
    state = jax.ShapeDtypeStruct((SOLID, height, depth), F32)
    wide = call(
        functools.partial(first_kernel, plan),
        [SMEM, ANY] + [VMEM] * 4,
        [
            state,
            jax.ShapeDtypeStruct((plan.chan - SOLID, height, depth), F32),
            state,
            jax.ShapeDtypeStruct((3, height, depth), F32),
        ],
        "first",
        1 << 26,
        [pltpu.SemaphoreType.DMA((2,))],
        8 << 20,
    )(owner, inner, from_y_low, from_y_high, from_x_low, from_x_high)
    flow, solute = call(
        functools.partial(steps_kernel, plan),
        [SMEM] + [VMEM] * 6,
        [jax.ShapeDtypeStruct(flow_adjoint.shape, F32), jax.ShapeDtypeStruct(solute_adjoint.shape, F32)],
        "steps",
        1 << 28,
        (),
        10 << 20,
    )(owner, *wide, from_c_low, from_c_high)
    return (flow, solute)


def solution(mesh):
    in_specs = (
        P(None, "gx", "gy", "gz"),
        P(None, "gx", "gy", "gz"),
        P(None, "gx", "gy", "gz"),
        P(None, None, "gx", "gy", "gz"),
        P(None, "gx", "gy", "gz"),
        P("gx", "gy", "gz"),
        P(),
    )
    out_specs = (P(None, "gx", "gy", "gz"), P(None, "gx", "gy", "gz"))
    return jax.shard_map(
        per_device, mesh=mesh, in_specs=in_specs, out_specs=out_specs, check_vma=False
    )
```

```python
import functools

import jax
import jax.numpy as jnp
from jax import lax
from jax.experimental import pallas as pl
from jax.experimental.pallas import tpu as pltpu
from jax.sharding import PartitionSpec as P

BZC = 16

FLOW_DIRS = [
    (0, 0, 0),
    (1, 0, 0),
    (-1, 0, 0),
    (0, 1, 0),
    (0, -1, 0),
    (0, 0, 1),
    (0, 0, -1),
    (1, 1, 0),
    (-1, -1, 0),
    (1, -1, 0),
    (-1, 1, 0),
    (1, 0, 1),
    (-1, 0, -1),
    (1, 0, -1),
    (-1, 0, 1),
    (0, 1, 1),
    (0, -1, -1),
    (0, 1, -1),
    (0, -1, 1),
]
NF = 19
NS = 7
OPPOSITE = [FLOW_DIRS.index((-a, -b, -c)) for a, b, c in FLOW_DIRS]
SOLID = NF + NS
AUX = SOLID + 1
NA = 5
flow_omega = 1.25
solute_omega = 1.6
langmuir_rate = 0.05
VMEM_LIMIT = 24 << 20
F32 = jnp.float32


class Plan:
    def __init__(self, steps, nx, ny, depth):
        self.steps, self.nx, self.ny, self.depth = steps, nx, ny, depth
        self.halo = w = steps
        self.chan = AUX + NA * steps
        self.sent = AUX + NA * (steps - 1)
        self.pitch = -(-(ny + 2 * w) // 8) * 8
        self.wide = nx + 2 * w
        self.count = {k: AUX + NA * (steps - k) for k in range(1, w)}
        self.base, at = {}, 0
        for k in range(1, w):
            self.base[k] = at
            at += self.count[k]
        self.base[w] = at
        self.slab = at + 7

    def last(self, axis, sign):
        flow = [i for i, c in enumerate(FLOW_DIRS) if c[axis] == sign]
        solute = [NF + i for i, c in enumerate(FLOW_DIRS[:NS]) if c[axis] == sign]
        return flow + solute + [SOLID]


def lanes(depth):
    return lax.broadcasted_iota(jnp.int32, (8, depth), 1)


def occupied(owner_ref):
    me = lax.axis_index("gz")
    count = jnp.int32(0)
    for j in range(owner_ref.shape[0]):
        count = count + jnp.where(owner_ref[j] == me, 1, 0).astype(jnp.int32)
    return count * BZC


def z_places(plan, length, ring):
    w, depth = plan.halo, plan.depth
    if ring == 2:
        first = lax.axis_index("gz") == 0
        return [(jnp.where(first, length - w, 0), jnp.where(first, length, depth - w))]
    return [(length - w, jnp.int32(depth - w)), (jnp.int32(0), length)]


def each(number, body, unroll=4):
    def several(i, carry):
        for u in range(unroll):
            body(i * unroll + u)
        return carry

    turns = number // unroll
    if turns > 1:
        lax.fori_loop(0, turns, several, 0)
    else:
        turns = 0
    for i in range(turns * unroll, number):
        body(i)


def tiles_of(plan):
    return [(y * (plan.nx // 8) + h, y, 8 * h) for y in range(plan.ny) for h in range(plan.nx // 8)]


def pack_kernel(plan, ring, parts, owner, flow, solute, density, velocity, level, solid, *refs):
    outs, (flow_out, solute_out, wide), (density_in, velocity_in, level_in, solid_in, sems) = (
        refs[:parts],
        refs[parts : parts + 3],
        refs[parts + 3 :],
    )
    w, depth, nx, ny = plan.halo, plan.depth, plan.nx, plan.ny
    cuts = [0, 7, 13, NF]
    flows = [pl.ds(a, b - a) for a, b in zip(cuts, cuts[1:])]
    pairs = [(flow.at[cut], flow_out.at[cut]) for cut in flows] + [
        (solute, solute_out),
        (solid, solid_in),
        (density, density_in),
        (level, level_in),
        (velocity, velocity_in),
    ]
    copies = [pltpu.make_async_copy(a, b, sems.at[i]) for i, (a, b) in enumerate(pairs)]
    for copy in copies:
        copy.start()

    length = occupied(owner)
    group = lanes(depth) // w
    places = z_places(plan, length, ring)
    shifts = [{n: (w * n + depth - start) & (depth - 1) for n, _, _ in tiles_of(plan)} for start, _ in places]

    def pack(at, first, number, ref):
        def one(i):
            packed = [None] * parts
            for n, y, x in tiles_of(plan):
                tile = ref[first + i, pl.ds(x * ny + y, 8, stride=ny), :]
                for p in range(parts):
                    moved = pltpu.roll(tile, shifts[p][n], 1)
                    packed[p] = moved if n == 0 else jnp.where(group == n, moved, packed[p])
            for p in range(parts):
                outs[p][at + first + i] = packed[p]

        each(number, one, 6)

    for copy, a, b in zip(copies, cuts, cuts[1:]):
        copy.wait()
        pack(0, a, b - a, flow_out)
    for copy in copies[3:]:
        copy.wait()
    pack(NF, 0, NS, solute_out)
    sources = [(solid_in, 0)]
    for s in range(plan.steps):
        t = plan.steps - 1 - s
        sources += [(density_in, t), (level_in, t)] + [(velocity_in, 3 * t + i) for i in range(3)]
    for c, (ref, i) in enumerate(sources):
        for x in range(nx):
            wide[c, x * ny : (x + 1) * ny, :] = ref[i, x * ny : (x + 1) * ny, :].astype(F32)
    pack(SOLID, 0, plan.sent - SOLID, wide)


def faces_kernel(plan, flow, solute, wide, packed, y_low, y_high):
    w, nx, ny = plan.halo, plan.nx, plan.ny
    for at, number, ref in ((0, NF, flow), (NF, NS, solute), (SOLID, plan.sent - SOLID, wide)):

        def row(c, y, ref=ref):
            return ref[c, pl.ds(y, nx, stride=ny), :]

        for k in range(1, w):

            def one(c, k=k, at=at, row=row):
                y_low[plan.base[k] + at + c] = row(c, k - 1)
                y_high[plan.base[k] + at + c] = row(c, ny - k)

            each(min(number, plan.count[k] - at), one)
        for out, sign, y in ((y_low, 1, w - 1), (y_high, -1, ny - w)):
            for j, c in enumerate(plan.last(1, sign)):
                if at <= c < at + number:
                    out[plan.base[w] + j] = row(c - at, y)


def column(plan, ring, owner, received):
    w, depth = plan.halo, plan.depth
    length = occupied(owner)
    lane = lanes(depth)
    live = lane < length
    places = [to for _, to in z_places(plan, length, ring)]
    halos = [((lane - to) & (depth - 1)) < w for to in places]
    shifts = [{n: (to + depth - w * n) & (depth - 1) for n, _, _ in tiles_of(plan)} for to in places]

    def put(tile, slabs, n):
        tile = jnp.where(live, tile, 0.0)
        for slab, halo, shift in zip(slabs, halos, shifts):
            tile = jnp.where(halo, pltpu.roll(slab, shift[n], 1), tile)
        return tile

    return put


def insert_kernel(plan, ring, parts, owner, low, high, *rest):
    received, (y_low, y_high) = rest[:parts], rest[parts:]
    put = column(plan, ring, owner, received)
    w, ny = plan.halo, plan.ny
    tall = plan.nx // 8

    def one(raw, out, j, c, y):
        slabs = [r[c] for r in received]
        for h in range(tall):
            out[j, 8 * h : 8 * h + 8, :] = put(raw[j, 8 * h : 8 * h + 8, :], slabs, y * tall + h)

    for k in range(1, w):

        def both(c, k=k):
            one(low, y_low, plan.base[k] + c, c, k - 1)
            one(high, y_high, plan.base[k] + c, c, ny - k)

        each(plan.count[k], both, 10)
    for raw, out, sign, y in ((low, y_low, 1, w - 1), (high, y_high, -1, ny - w)):
        for j, c in enumerate(plan.last(1, sign)):
            one(raw, out, plan.base[w] + j, c, y)


def inner_kernel(plan, ring, parts, owner, flow, solute, wide, *rest):
    received, (out, x_low, x_high) = rest[:parts], rest[parts:]
    w, nx, ny, pitch = plan.halo, plan.nx, plan.ny, plan.pitch
    put = column(plan, ring, owner, received)
    for at, number, ref in ((0, NF, flow), (NF, NS, solute), (SOLID, plan.chan - SOLID, wide)):

        def one(i, sent=True, at=at, ref=ref):
            slabs = [r[at + i] for r in received] if sent else []
            for n, y, x in tiles_of(plan):
                tile = ref[i, pl.ds(x * ny + y, 8, stride=ny), :]
                out[at + i, pl.ds(x * pitch + w + y, 8, stride=pitch), :] = put(tile, slabs, n)

        within = min(number, plan.sent - at)
        each(within, one, 3)
        each(number - within, lambda i, one=one, within=within: one(within + i, False), 1)

    def row(c, x):
        return out[c, x * pitch + w : x * pitch + w + ny, :]

    for k in range(1, w):

        def both(c, k=k):
            x_low[plan.base[k] + c] = row(c, k - 1)
            x_high[plan.base[k] + c] = row(c, nx - k)

        each(plan.count[k], both)
    for slab, sign, x in ((x_low, 1, w - 1), (x_high, -1, nx - w)):
        for j, c in enumerate(plan.last(0, sign)):
            slab[plan.base[w] + j] = row(c, x)


def corners_kernel(plan, from_low, from_high, inner, low, high):
    w, nx, ny = plan.halo, plan.nx, plan.ny
    low[...] = jnp.zeros(low.shape, F32)
    high[...] = jnp.zeros(high.shape, F32)
    tall = 2 * w
    for out, sign in ((low, 1), (high, -1)):
        x_last = plan.last(0, sign)
        for k in range(1, w + 1):
            x = k - 1 if sign == 1 else nx - k
            for m in range(1, w + 1):
                for source, row, y_sign in ((from_low, w - m, -1), (from_high, w - 1 + m, 1)):
                    y_last = plan.last(1, y_sign)
                    if k < w and m < w:
                        number = min(plan.count[k], plan.count[m])
                        out[pl.ds(plan.base[k] * tall + row, number, stride=tall), :] = source[
                            pl.ds(plan.base[m] * nx + x, number, stride=nx), :
                        ]
                        continue
                    for c in range(AUX):
                        if (k == w and c not in x_last) or (m == w and c not in y_last):
                            continue
                        to = plan.base[k] + (x_last.index(c) if k == w else c)
                        at = plan.base[m] + (y_last.index(c) if m == w else c)
                        out[to * tall + row : to * tall + row + 1, :] = source[at * nx + x : at * nx + x + 1, :]


PAD = 8


def channels(cells, fields, number, body):
    each(SOLID, lambda c: body(cells, c, c))
    each(number - SOLID, lambda c: body(fields, c, SOLID + c))


def insert_layers(plan, cells, fields, axis, parts, put):
    w = plan.halo
    for k in range(1, w + 1):
        for part, sign in zip(parts, (-1, 1)):
            if k < w:
                channels(
                    cells,
                    fields,
                    plan.count[k],
                    lambda ref, c, j, k=k, part=part, sign=sign: put(ref, c, part, plan.base[k] + j, k, sign),
                )
                continue
            for j, c in enumerate(plan.last(axis, sign)):
                ref, at = (cells, c) if c < SOLID else (fields, c - SOLID)
                put(ref, at, part, plan.base[w] + j, k, sign)


def first_kernel(plan, owner, inner, y_low, y_high, x_low, x_high, cells, fields, other, masks, sems):
    w, nx, ny, pitch = plan.halo, plan.nx, plan.ny, plan.pitch
    middle = pl.ds(PAD + w * pitch, nx * pitch)
    copies = [
        pltpu.make_async_copy(inner.at[pl.ds(0, SOLID)], cells.at[:, middle, :], sems.at[0]),
        pltpu.make_async_copy(inner.at[pl.ds(SOLID, plan.chan - SOLID)], fields.at[:, middle, :], sems.at[1]),
    ]
    for copy in copies:
        copy.start()

    def put_x(ref, c, part, j, k, sign):
        row = PAD + (w - k if sign < 0 else w + nx - 1 + k) * pitch + w
        ref[c, row : row + ny, :] = part[j]

    insert_layers(plan, cells, fields, 0, (x_low, x_high), put_x)
    for copy in copies:
        copy.wait()

    def put_y(ref, c, part, j, m, sign):
        row = PAD + w * pitch + (w - m if sign < 0 else w + ny - 1 + m)
        ref[c, pl.ds(row, nx, stride=pitch), :] = part[j]

    insert_layers(plan, cells, fields, 1, (y_low, y_high), put_y)
    prepare(plan, owner, fields, masks, w, w + nx)
    sweep(plan, owner, cells, other, fields, masks, 0, w + 1, w + nx - 1)


def steps_kernel(plan, owner, cells, fields, other, masks, c_low, c_high, flow_out, solute_out):
    w, nx, ny, pitch = plan.halo, plan.nx, plan.ny, plan.pitch

    def put(ref, c, part, j, k, sign):
        row = PAD + (w - k if sign < 0 else w + nx - 1 + k) * pitch
        ref[c, row : row + w, :] = part[j, 0:w, :]
        ref[c, row + w + ny : row + w + ny + w, :] = part[j, w : 2 * w, :]

    insert_layers(plan, cells, fields, 0, (c_low, c_high), put)
    prepare(plan, owner, fields, masks, 0, w)
    prepare(plan, owner, fields, masks, w + nx, plan.wide)
    sweep(plan, owner, cells, other, fields, masks, 0, 1, w + 1)
    sweep(plan, owner, cells, other, fields, masks, 0, w + nx - 1, plan.wide - 1)
    buffers = [cells, other]
    for s in range(1, plan.steps - 1):
        sweep(plan, owner, buffers[s % 2], buffers[(s + 1) % 2], fields, masks, s, 1 + s, plan.wide - 1 - s)
    s = plan.steps - 1
    source = buffers[s % 2]

    def last(x, carry):
        for h in range(ny // 8):
            row = PAD + (x + w) * pitch + w + 8 * h

            def write(c, value, h=h):
                if c < NF:
                    flow_out[c, x, 8 * h : 8 * h + 8, :] = value
                else:
                    solute_out[c - NF, x, 8 * h : 8 * h + 8, :] = value

            advance(plan, owner, source, fields, masks, s, row, write)
        return carry

    lax.fori_loop(0, nx, last, 0)


def prepare(plan, owner, fields, masks, from_x, to_x):
    w, nx, ny, depth, pitch = plan.halo, plan.nx, plan.ny, plan.depth, plan.pitch
    length = occupied(owner)
    lane = lanes(depth)
    gx, gy, gz = (lax.axis_index(a) for a in ("gx", "gy", "gz"))
    last_x, last_y, last_z = (lax.axis_size(a) - 1 for a in ("gx", "gy", "gz"))
    above = jnp.where(gz < last_z, w, 0)
    below = jnp.where(gz > 0, w, 0)
    in_z = (lane < length + above) | (lane >= depth - below)
    y_first = jnp.where(gy > 0, 0, w)
    y_end = jnp.where(gy < last_y, ny + 2 * w, w + ny)
    x_first = jnp.where(gx > 0, 0, w)
    x_end = jnp.where(gx < last_x, nx + 2 * w, w + nx)
    sub = lax.broadcasted_iota(jnp.int32, (8, depth), 0)

    def one(x, carry):
        in_x = ((x >= x_first) & (x < x_end)).astype(F32)
        for h in range(pitch // 8):
            row = pl.multiple_of(PAD + x * pitch + 8 * h, 8)
            flags = fields[0, pl.ds(row, 8), :]
            y = sub + 8 * h
            masks[0, pl.ds(row, 8), :] = pltpu.roll(flags, depth - 1, 1)
            masks[1, pl.ds(row, 8), :] = pltpu.roll(flags, 1, 1)
            inside = in_z & (y >= y_first) & (y < y_end) & (flags == 0.0)
            masks[2, pl.ds(row, 8), :] = jnp.where(inside, in_x, 0.0)
        return carry

    lax.fori_loop(from_x, to_x, one, 0)


def sweep(plan, owner, source, target, fields, masks, s, from_x, to_x):
    pitch = plan.pitch

    def body(x, carry):
        for h in range(pitch // 8):
            row = pl.multiple_of(PAD + pitch * x + 8 * h, 8)

            def write(c, value, row=row):
                target[c, pl.ds(row, 8), :] = value

            advance(plan, owner, source, fields, masks, s, row, write)
        return carry

    lax.fori_loop(from_x, to_x, body, 0)


def advance(plan, owner, source, fields, masks, s, row, write):
    depth, pitch = plan.depth, plan.pitch
    def field(ref, c, move=0):
        return ref[c, pl.ds(row + move, 8), :]

    blocked = {}

    def reads(first, number):
        result = []
        for i in range(number):
            sx, sy, sz = FLOW_DIRS[i]
            if i == 0:
                result.append(field(source, first))
                continue
            move = sx * pitch + sy
            near = field(source, first + i, move)
            if sz:
                near = pltpu.roll(near, (depth - sz) % depth, 1)
            if i not in blocked:
                flags = field(fields, 0, move) if sz == 0 else field(masks, 0 if sz == 1 else 1, move)
                blocked[i] = flags != 0.0
            result.append(jnp.where(blocked[i], field(source, first + OPPOSITE[i]), near))
        return result

    valid = field(masks, 2)
    if s == plan.steps - 1:
        valid = jnp.where(lanes(depth) < occupied(owner), valid, 0.0)
    aux = AUX - SOLID + NA * s
    density, level, ux, uy, uz = (field(fields, aux + n) for n in range(NA))

    h = reads(NF, NS)
    px, py, pz = h[1] - h[2], h[3] - h[4], h[5] - h[6]
    p0 = 0.25 * h[0] + 0.125 * ((h[1] + h[2]) + (h[3] + h[4]) + (h[5] + h[6]))
    grown = 1.0 + level
    uptake = langmuir_rate / (grown * grown)
    common = valid * (
        (solute_omega - uptake) * p0 + (solute_omega * 0.5) * (px * ux + py * uy + pz * uz)
    )
    keep = (1.0 - solute_omega) * valid
    for i in range(NS):
        write(NF + i, keep * h[i] + common)
    factor = (0.5 * solute_omega) * level / jnp.maximum(density, 0.5)
    fx, fy, fz = factor * px, factor * py, factor * pz

    g = reads(0, NF)
    a = {i: g[i] + g[i + 1] for i in range(1, NF, 2)}
    d = {i: g[i] - g[i + 1] for i in range(1, NF, 2)}
    m1x = (d[1] + d[1]) + (d[7] + d[9]) + (d[11] + d[13])
    m1y = (d[3] + d[3]) + (d[7] - d[9]) + (d[15] + d[17])
    m1z = (d[5] + d[5]) + (d[11] - d[13]) + (d[15] - d[17])
    exy, exz, eyz = a[7] + a[9], a[11] + a[13], a[15] + a[17]
    tx, ty, tz = a[1] + a[1], a[3] + a[3], a[5] + a[5]
    mxx, myy, mzz = tx + exy + exz, ty + exy + eyz, tz + exz + eyz
    mxy, mxz, myz = a[7] - a[9], a[11] - a[13], a[15] - a[17]
    m0 = 12.0 * g[0] + (tx + ty + tz) + (exy + exz + eyz)
    qx = mxx * ux + mxy * uy + mxz * uz
    qy = mxy * ux + myy * uy + myz * uz
    qz = mxz * ux + myz * uy + mzz * uz
    square = ux * ux + uy * uy + uz * uz
    scaled = flow_omega / 36.0
    zero = m0 * (scaled + (1.5 * scaled) * square) - (4.5 * scaled) * (qx * ux + qy * uy + qz * uz)
    zero = valid * (zero - (fx * ux + fy * uy + fz * uz))
    bx = valid * ((3.0 * scaled) * (m1x + 3.0 * qx - m0 * ux) + fx)
    by = valid * ((3.0 * scaled) * (m1y + 3.0 * qy - m0 * uy) + fy)
    bz = valid * ((3.0 * scaled) * (m1z + 3.0 * qz - m0 * uz) + fz)
    keep = (1.0 - flow_omega) * valid
    write(0, keep * g[0] + zero)
    moves = {1: bx, 3: by, 5: bz, 7: bx + by, 9: bx - by, 11: bx + bz, 13: bx - bz, 15: by + bz, 17: by - bz}
    for i, move in moves.items():
        write(i, keep * g[i] + (zero + move))
        write(i + 1, keep * g[i + 1] + (zero - move))


VMEM = pl.BlockSpec(memory_space=pltpu.VMEM)
SMEM = pl.BlockSpec(memory_space=pltpu.SMEM)
ANY = pl.BlockSpec(memory_space=pl.ANY)
HBM = pl.BlockSpec(memory_space=pltpu.HBM)


def call(kernel, ins, outs, name, cost, scratch=(), limit=VMEM_LIMIT):
    return pl.pallas_call(
        kernel,
        in_specs=ins,
        out_shape=outs,
        out_specs=[VMEM] * len(outs),
        scratch_shapes=list(scratch),
        name=name,
        cost_estimate=pl.CostEstimate(flops=cost, bytes_accessed=1 << 23, transcendentals=0),
        compiler_params=pltpu.CompilerParams(vmem_limit_bytes=limit),
    )


def per_device(flow_adjoint, solute_adjoint, flow_density, flow_velocity, solute_level, solid, owner):
    steps = flow_density.shape[0]
    nx, ny, depth = solid.shape
    plan = Plan(steps, nx, ny, depth)
    ring = lax.axis_size("gz")
    w = plan.halo
    arguments = (flow_adjoint, solute_adjoint, flow_density, flow_velocity, solute_level, solid)
    fields = [f.reshape(-1, nx * ny, depth) for f in arguments]
    owner, *fields = (pltpu.with_memory_space_constraint(f, pltpu.HBM) for f in (owner, *fields))

    def move(value, axis, by):
        size = lax.axis_size(axis)
        return lax.ppermute(value, axis, [(i, i + by) for i in range(size) if 0 <= i + by < size])

    parts = 1 if ring == 2 else 2

    def like(channels):
        return jax.ShapeDtypeStruct((channels, nx * ny, depth), F32)

    *packed, flow, solute, wide = call(
        functools.partial(pack_kernel, plan, ring, parts),
        [SMEM] + [HBM] * 6,
        [jax.ShapeDtypeStruct((plan.sent, 8, depth), F32)] * parts + [like(NF), like(NS), like(plan.chan - SOLID)],
        "pack_column",
        1 << 22,
        [pltpu.VMEM(f.shape, f.dtype) for f in fields[2:]] + [pltpu.SemaphoreType.DMA((8,))],
    )(owner, *fields)
    loaded = (flow, solute, wide)
    if ring == 2:
        received = [lax.ppermute(packed[0], "gz", [(0, 1), (1, 0)])]
    else:
        received = [move(packed[0], "gz", 1), move(packed[1], "gz", -1)]

    slab = [jax.ShapeDtypeStruct((plan.slab, nx, depth), F32)] * 2
    raw = call(functools.partial(faces_kernel, plan), [VMEM] * 3 + [ANY], slab, "faces", 1 << 24)(
        *loaded, packed[0]
    )
    y_low, y_high = call(
        functools.partial(insert_kernel, plan, ring, parts), [SMEM] + [VMEM] * (2 + parts), slab, "insert", 1 << 22, (), 24 << 20
    )(owner, *raw, *received)
    from_y_low = move(y_high, "gy", 1)
    from_y_high = move(y_low, "gy", -1)
    inner, x_low, x_high = call(
        functools.partial(inner_kernel, plan, ring, parts),
        [SMEM] + [VMEM] * (3 + parts),
        [jax.ShapeDtypeStruct((plan.chan, nx * plan.pitch, depth), F32)] + [jax.ShapeDtypeStruct((plan.slab, ny, depth), F32)] * 2,
        "inner",
        1 << 24,
    )(owner, *loaded, *received)
    from_x_low = move(x_high, "gx", 1)
    from_x_high = move(x_low, "gx", -1)

    def rows(value):
        return value.reshape(-1, depth)

    corner = jax.ShapeDtypeStruct((plan.slab * 2 * w, depth), F32)
    c_low, c_high = call(
        functools.partial(corners_kernel, plan), [VMEM] * 2 + [ANY], [corner, corner], "corners", 1 << 20
    )(rows(from_y_low), rows(from_y_high), inner)
    shape = (plan.slab, 2 * w, depth)
    from_c_low = move(c_high, "gx", 1).reshape(shape)
    from_c_high = move(c_low, "gx", -1).reshape(shape)
    height = plan.wide * plan.pitch + 2 * PAD
    state = jax.ShapeDtypeStruct((SOLID, height, depth), F32)
    wide = call(
        functools.partial(first_kernel, plan),
        [SMEM, ANY] + [VMEM] * 4,
        [
            state,
            jax.ShapeDtypeStruct((plan.chan - SOLID, height, depth), F32),
            state,
            jax.ShapeDtypeStruct((3, height, depth), F32),
        ],
        "first",
        1 << 26,
        [pltpu.SemaphoreType.DMA((2,))],
        8 << 20,
    )(owner, inner, from_y_low, from_y_high, from_x_low, from_x_high)
    flow, solute = call(
        functools.partial(steps_kernel, plan),
        [SMEM] + [VMEM] * 6,
        [jax.ShapeDtypeStruct(flow_adjoint.shape, F32), jax.ShapeDtypeStruct(solute_adjoint.shape, F32)],
        "steps",
        1 << 28,
        (),
        10 << 20,
    )(owner, *wide, from_c_low, from_c_high)
    return (flow, solute)


def solution(mesh):
    in_specs = (
        P(None, "gx", "gy", "gz"),
        P(None, "gx", "gy", "gz"),
        P(None, "gx", "gy", "gz"),
        P(None, None, "gx", "gy", "gz"),
        P(None, "gx", "gy", "gz"),
        P("gx", "gy", "gz"),
        P(),
    )
    out_specs = (P(None, "gx", "gy", "gz"), P(None, "gx", "gy", "gz"))
    return jax.shard_map(
        per_device, mesh=mesh, in_specs=in_specs, out_specs=out_specs, check_vma=False
    )
```

```python
import functools

import jax
import jax.numpy as jnp
from jax import lax
from jax.experimental import pallas as pl
from jax.experimental.pallas import tpu as pltpu
from jax.sharding import PartitionSpec as P

BZC = 16

FLOW_DIRS = [
    (0, 0, 0),
    (1, 0, 0),
    (-1, 0, 0),
    (0, 1, 0),
    (0, -1, 0),
    (0, 0, 1),
    (0, 0, -1),
    (1, 1, 0),
    (-1, -1, 0),
    (1, -1, 0),
    (-1, 1, 0),
    (1, 0, 1),
    (-1, 0, -1),
    (1, 0, -1),
    (-1, 0, 1),
    (0, 1, 1),
    (0, -1, -1),
    (0, 1, -1),
    (0, -1, 1),
]
NF = 19
NS = 7
OPPOSITE = [FLOW_DIRS.index((-a, -b, -c)) for a, b, c in FLOW_DIRS]
SOLID = NF + NS
AUX = SOLID + 1
NA = 5
flow_omega = 1.25
solute_omega = 1.6
langmuir_rate = 0.05
VMEM_LIMIT = 24 << 20
F32 = jnp.float32
PAD = 8


class Plan:
    def __init__(self, steps, nx, ny, depth):
        self.steps, self.nx, self.ny, self.depth = steps, nx, ny, depth
        self.halo = w = steps
        self.chan = AUX + NA * steps
        self.sent = AUX + NA * (steps - 1)
        self.pitch = -(-(ny + 2 * w) // 8) * 8
        self.wide = nx + 2 * w
        self.height = self.wide * self.pitch + 2 * PAD
        self.tiles = list(range(self.pitch // 8))
        self.inside = [h for h in self.tiles if 8 * h > w and 8 * h + 8 < w + ny]
        self.outside = [h for h in self.tiles if h not in self.inside]
        self.count = {k: AUX + NA * (steps - k) for k in range(1, w)}
        self.base, at = {}, 0
        for k in range(1, w):
            self.base[k] = at
            at += self.count[k]
        self.base[w] = at
        self.slab = at + 7

    def last(self, axis, sign):
        flow = [i for i, c in enumerate(FLOW_DIRS) if c[axis] == sign]
        solute = [NF + i for i, c in enumerate(FLOW_DIRS[:NS]) if c[axis] == sign]
        return flow + solute + [SOLID]


def lanes(depth):
    return lax.broadcasted_iota(jnp.int32, (8, depth), 1)


def occupied(owner_ref):
    me = lax.axis_index("gz")
    count = jnp.int32(0)
    for j in range(owner_ref.shape[0]):
        count = count + jnp.where(owner_ref[j] == me, 1, 0).astype(jnp.int32)
    return count * BZC


def z_places(plan, length, ring):
    w, depth = plan.halo, plan.depth
    if ring == 2:
        first = lax.axis_index("gz") == 0
        return [(jnp.where(first, length - w, 0), jnp.where(first, length, depth - w))]
    return [(length - w, jnp.int32(depth - w)), (jnp.int32(0), length)]


def each(number, body, unroll=4):
    def several(i, carry):
        for u in range(unroll):
            body(i * unroll + u)
        return carry

    turns = number // unroll
    if turns > 1:
        lax.fori_loop(0, turns, several, 0)
    else:
        turns = 0
    for i in range(turns * unroll, number):
        body(i)


def tiles_of(plan):
    return [(y * (plan.nx // 8) + h, y, 8 * h) for y in range(plan.ny) for h in range(plan.nx // 8)]


def pack_kernel(plan, ring, parts, owner, flow, solute, density, velocity, level, solid, *refs):
    outs, (flow_out, solute_out, wide), (density_in, velocity_in, level_in, solid_in, sems) = (
        refs[:parts],
        refs[parts : parts + 3],
        refs[parts + 3 :],
    )
    w, depth, nx, ny = plan.halo, plan.depth, plan.nx, plan.ny
    cuts = [0, 7, 13, NF]
    flows = [pl.ds(a, b - a) for a, b in zip(cuts, cuts[1:])]
    pairs = [(flow.at[cut], flow_out.at[cut]) for cut in flows] + [
        (solute, solute_out),
        (solid, solid_in),
        (density, density_in),
        (level, level_in),
        (velocity, velocity_in),
    ]
    copies = [pltpu.make_async_copy(a, b, sems.at[i]) for i, (a, b) in enumerate(pairs)]
    for copy in copies:
        copy.start()

    length = occupied(owner)
    group = lanes(depth) // w
    places = z_places(plan, length, ring)
    shifts = [{n: (w * n + depth - start) & (depth - 1) for n, _, _ in tiles_of(plan)} for start, _ in places]

    def pack(at, first, number, ref):
        def one(i):
            packed = [None] * parts
            for n, y, x in tiles_of(plan):
                tile = ref[first + i, pl.ds(x * ny + y, 8, stride=ny), :]
                for p in range(parts):
                    moved = pltpu.roll(tile, shifts[p][n], 1)
                    packed[p] = moved if n == 0 else jnp.where(group == n, moved, packed[p])
            for p in range(parts):
                outs[p][at + first + i] = packed[p]

        each(number, one, 6)

    for copy, a, b in zip(copies, cuts, cuts[1:]):
        copy.wait()
        pack(0, a, b - a, flow_out)
    for copy in copies[3:]:
        copy.wait()
    pack(NF, 0, NS, solute_out)
    sources = [(solid_in, 0)]
    for s in range(plan.steps):
        t = plan.steps - 1 - s
        sources += [(density_in, t), (level_in, t)] + [(velocity_in, 3 * t + i) for i in range(3)]
    for c, (ref, i) in enumerate(sources):
        for x in range(nx):
            wide[c, x * ny : (x + 1) * ny, :] = ref[i, x * ny : (x + 1) * ny, :].astype(F32)
    pack(SOLID, 0, plan.sent - SOLID, wide)


def faces_kernel(plan, flow, solute, wide, packed, y_low, y_high):
    w, nx, ny = plan.halo, plan.nx, plan.ny
    for at, number, ref in ((0, NF, flow), (NF, NS, solute), (SOLID, plan.sent - SOLID, wide)):

        def row(c, y, ref=ref):
            return ref[c, pl.ds(y, nx, stride=ny), :]

        for k in range(1, w):

            def one(c, k=k, at=at, row=row):
                y_low[plan.base[k] + at + c] = row(c, k - 1)
                y_high[plan.base[k] + at + c] = row(c, ny - k)

            each(min(number, plan.count[k] - at), one)
        for out, sign, y in ((y_low, 1, w - 1), (y_high, -1, ny - w)):
            for j, c in enumerate(plan.last(1, sign)):
                if at <= c < at + number:
                    out[plan.base[w] + j] = row(c - at, y)


def column(plan, ring, owner, received):
    w, depth = plan.halo, plan.depth
    length = occupied(owner)
    lane = lanes(depth)
    live = lane < length
    places = [to for _, to in z_places(plan, length, ring)]
    halos = [((lane - to) & (depth - 1)) < w for to in places]
    shifts = [{n: (to + depth - w * n) & (depth - 1) for n, _, _ in tiles_of(plan)} for to in places]

    def put(tile, slabs, n):
        tile = jnp.where(live, tile, 0.0)
        for slab, halo, shift in zip(slabs, halos, shifts):
            tile = jnp.where(halo, pltpu.roll(slab, shift[n], 1), tile)
        return tile

    return put


def insert_kernel(plan, ring, parts, owner, low, high, *rest):
    received, (y_low, y_high) = rest[:parts], rest[parts:]
    put = column(plan, ring, owner, received)
    w, ny = plan.halo, plan.ny
    tall = plan.nx // 8

    def one(raw, out, j, c, y):
        slabs = [r[c] for r in received]
        for h in range(tall):
            out[j, 8 * h : 8 * h + 8, :] = put(raw[j, 8 * h : 8 * h + 8, :], slabs, y * tall + h)

    for k in range(1, w):

        def both(c, k=k):
            one(low, y_low, plan.base[k] + c, c, k - 1)
            one(high, y_high, plan.base[k] + c, c, ny - k)

        each(plan.count[k], both, 10)
    for raw, out, sign, y in ((low, y_low, 1, w - 1), (high, y_high, -1, ny - w)):
        for j, c in enumerate(plan.last(1, sign)):
            one(raw, out, plan.base[w] + j, c, y)


def inner_kernel(plan, ring, parts, owner, flow, solute, wide, *rest):
    received, (cells, fields, x_low, x_high) = rest[:parts], rest[parts:]
    w, nx, ny, pitch = plan.halo, plan.nx, plan.ny, plan.pitch
    put = column(plan, ring, owner, received)
    for at, number, ref, out, to in (
        (0, NF, flow, cells, 0),
        (NF, NS, solute, cells, NF),
        (SOLID, plan.chan - SOLID, wide, fields, 0),
    ):

        def one(i, sent=True, at=at, ref=ref, out=out, to=to):
            slabs = [r[at + i] for r in received] if sent else []
            for n, y, x in tiles_of(plan):
                tile = ref[i, pl.ds(x * ny + y, 8, stride=ny), :]
                out[to + i, pl.ds(PAD + (w + x) * pitch + w + y, 8, stride=pitch), :] = put(tile, slabs, n)

        within = min(number, plan.sent - at)
        each(within, one, 3)
        each(number - within, lambda i, one=one, within=within: one(within + i, False), 1)

    def row(ref, c, x):
        at = PAD + (w + x) * pitch + w
        return ref[c, at : at + ny, :]

    for k in range(1, w):

        def both(ref, c, j, k=k):
            x_low[plan.base[k] + j] = row(ref, c, k - 1)
            x_high[plan.base[k] + j] = row(ref, c, nx - k)

        channels(cells, fields, plan.count[k], both)
    for slab, sign, x in ((x_low, 1, w - 1), (x_high, -1, nx - w)):
        for j, c in enumerate(plan.last(0, sign)):
            ref, at = (cells, c) if c < SOLID else (fields, c - SOLID)
            slab[plan.base[w] + j] = row(ref, at, x)


def middle_kernel(plan, owner, cells, fields, other, masks):
    w, nx = plan.halo, plan.nx
    prepare(plan, owner, fields, masks, w, w + nx)
    sweep(plan, owner, cells, other, fields, masks, 0, w + 1, w + nx - 1, plan.inside)


def corners_kernel(plan, from_low, from_high, masks, low, high):
    w, nx, ny = plan.halo, plan.nx, plan.ny
    low[...] = jnp.zeros(low.shape, F32)
    high[...] = jnp.zeros(high.shape, F32)
    tall = 2 * w
    for out, sign in ((low, 1), (high, -1)):
        x_last = plan.last(0, sign)
        for k in range(1, w + 1):
            x = k - 1 if sign == 1 else nx - k
            for m in range(1, w + 1):
                for source, row, y_sign in ((from_low, w - m, -1), (from_high, w - 1 + m, 1)):
                    y_last = plan.last(1, y_sign)
                    if k < w and m < w:
                        number = min(plan.count[k], plan.count[m])
                        out[pl.ds(plan.base[k] * tall + row, number, stride=tall), :] = source[
                            pl.ds(plan.base[m] * nx + x, number, stride=nx), :
                        ]
                        continue
                    for c in range(AUX):
                        if (k == w and c not in x_last) or (m == w and c not in y_last):
                            continue
                        to = plan.base[k] + (x_last.index(c) if k == w else c)
                        at = plan.base[m] + (y_last.index(c) if m == w else c)
                        out[to * tall + row : to * tall + row + 1, :] = source[at * nx + x : at * nx + x + 1, :]


def channels(cells, fields, number, body):
    each(SOLID, lambda c: body(cells, c, c))
    each(number - SOLID, lambda c: body(fields, c, SOLID + c))


def insert_layers(plan, cells, fields, axis, parts, put):
    w = plan.halo
    for k in range(1, w + 1):
        for part, sign in zip(parts, (-1, 1)):
            if k < w:
                channels(
                    cells,
                    fields,
                    plan.count[k],
                    lambda ref, c, j, k=k, part=part, sign=sign: put(ref, c, part, plan.base[k] + j, k, sign),
                )
                continue
            for j, c in enumerate(plan.last(axis, sign)):
                ref, at = (cells, c) if c < SOLID else (fields, c - SOLID)
                put(ref, at, part, plan.base[w] + j, k, sign)


def first_kernel(plan, owner, y_low, y_high, x_low, x_high, *refs):
    cells, fields, other, masks = refs[4:]
    w, nx, ny, pitch = plan.halo, plan.nx, plan.ny, plan.pitch

    def put_x(ref, c, part, j, k, sign):
        row = PAD + (w - k if sign < 0 else w + nx - 1 + k) * pitch + w
        ref[c, row : row + ny, :] = part[j]

    insert_layers(plan, cells, fields, 0, (x_low, x_high), put_x)

    def put_y(ref, c, part, j, m, sign):
        row = PAD + w * pitch + (w - m if sign < 0 else w + ny - 1 + m)
        ref[c, pl.ds(row, nx, stride=pitch), :] = part[j]

    insert_layers(plan, cells, fields, 1, (y_low, y_high), put_y)
    prepare(plan, owner, fields, masks, w, w + nx)
    sweep(plan, owner, cells, other, fields, masks, 0, w + 1, w + nx - 1, plan.outside)


def steps_kernel(plan, owner, cells, fields, other, masks, c_low, c_high, flow_hbm, solute_hbm, flow_out, solute_out, sems):
    w, nx, ny, pitch = plan.halo, plan.nx, plan.ny, plan.pitch

    def put(ref, c, part, j, k, sign):
        row = PAD + (w - k if sign < 0 else w + nx - 1 + k) * pitch
        ref[c, row : row + w, :] = part[j, 0:w, :]
        ref[c, row + w + ny : row + w + ny + w, :] = part[j, w : 2 * w, :]

    insert_layers(plan, cells, fields, 0, (c_low, c_high), put)
    prepare(plan, owner, fields, masks, 0, w)
    prepare(plan, owner, fields, masks, w + nx, plan.wide)
    sweep(plan, owner, cells, other, fields, masks, 0, 1, w + 1)
    sweep(plan, owner, cells, other, fields, masks, 0, w + nx - 1, plan.wide - 1)
    buffers = [cells, other]
    for s in range(1, plan.steps - 1):
        sweep(plan, owner, buffers[s % 2], buffers[(s + 1) % 2], fields, masks, s, 1 + s, plan.wide - 1 - s)
    s = plan.steps - 1
    source = buffers[s % 2]

    def leave(x):
        return [
            pltpu.make_async_copy(ref.at[:, x], to.at[:, x], sems.at[n, x])
            for n, (ref, to) in enumerate(((flow_out, flow_hbm), (solute_out, solute_hbm)))
        ]

    def last(x, carry):
        for h in range(ny // 8):
            row = PAD + (x + w) * pitch + w + 8 * h

            def write(c, value, h=h):
                if c < NF:
                    flow_out[c, x, 8 * h : 8 * h + 8, :] = value
                else:
                    solute_out[c - NF, x, 8 * h : 8 * h + 8, :] = value

            advance(plan, owner, source, fields, masks, s, row, write)
        for copy in leave(x):
            copy.start()
        return carry

    lax.fori_loop(0, nx, last, 0)
    for x in range(nx):
        for copy in leave(x):
            copy.wait()


def prepare(plan, owner, fields, masks, from_x, to_x):
    w, nx, ny, depth, pitch = plan.halo, plan.nx, plan.ny, plan.depth, plan.pitch
    length = occupied(owner)
    lane = lanes(depth)
    gx, gy, gz = (lax.axis_index(a) for a in ("gx", "gy", "gz"))
    last_x, last_y, last_z = (lax.axis_size(a) - 1 for a in ("gx", "gy", "gz"))
    above = jnp.where(gz < last_z, w, 0)
    below = jnp.where(gz > 0, w, 0)
    in_z = (lane < length + above) | (lane >= depth - below)
    y_first = jnp.where(gy > 0, 0, w)
    y_end = jnp.where(gy < last_y, ny + 2 * w, w + ny)
    x_first = jnp.where(gx > 0, 0, w)
    x_end = jnp.where(gx < last_x, nx + 2 * w, w + nx)
    sub = lax.broadcasted_iota(jnp.int32, (8, depth), 0)

    def one(x, carry):
        in_x = ((x >= x_first) & (x < x_end)).astype(F32)
        for h in range(pitch // 8):
            row = pl.multiple_of(PAD + x * pitch + 8 * h, 8)
            flags = fields[0, pl.ds(row, 8), :]
            y = sub + 8 * h
            masks[0, pl.ds(row, 8), :] = pltpu.roll(flags, depth - 1, 1)
            masks[1, pl.ds(row, 8), :] = pltpu.roll(flags, 1, 1)
            inside = in_z & (y >= y_first) & (y < y_end) & (flags == 0.0)
            masks[2, pl.ds(row, 8), :] = jnp.where(inside, in_x, 0.0)
        return carry

    lax.fori_loop(from_x, to_x, one, 0)


def sweep(plan, owner, source, target, fields, masks, s, from_x, to_x, tiles=None):
    pitch = plan.pitch

    def body(x, carry):
        for h in tiles or plan.tiles:
            row = pl.multiple_of(PAD + pitch * x + 8 * h, 8)

            def write(c, value, row=row):
                target[c, pl.ds(row, 8), :] = value

            advance(plan, owner, source, fields, masks, s, row, write)
        return carry

    lax.fori_loop(from_x, to_x, body, 0)


def advance(plan, owner, source, fields, masks, s, row, write):
    depth, pitch = plan.depth, plan.pitch
    def field(ref, c, move=0):
        return ref[c, pl.ds(row + move, 8), :]

    blocked = {}

    def reads(first, number):
        result = []
        for i in range(number):
            sx, sy, sz = FLOW_DIRS[i]
            if i == 0:
                result.append(field(source, first))
                continue
            move = sx * pitch + sy
            near = field(source, first + i, move)
            if sz:
                near = pltpu.roll(near, (depth - sz) % depth, 1)
            if i not in blocked:
                flags = field(fields, 0, move) if sz == 0 else field(masks, 0 if sz == 1 else 1, move)
                blocked[i] = flags != 0.0
            result.append(jnp.where(blocked[i], field(source, first + OPPOSITE[i]), near))
        return result

    valid = field(masks, 2)
    if s == plan.steps - 1:
        valid = jnp.where(lanes(depth) < occupied(owner), valid, 0.0)
    aux = AUX - SOLID + NA * s
    density, level, ux, uy, uz = (field(fields, aux + n) for n in range(NA))

    h = reads(NF, NS)
    px, py, pz = h[1] - h[2], h[3] - h[4], h[5] - h[6]
    p0 = 0.25 * h[0] + 0.125 * ((h[1] + h[2]) + (h[3] + h[4]) + (h[5] + h[6]))
    grown = 1.0 + level
    uptake = langmuir_rate / (grown * grown)
    common = valid * (
        (solute_omega - uptake) * p0 + (solute_omega * 0.5) * (px * ux + py * uy + pz * uz)
    )
    keep = (1.0 - solute_omega) * valid
    for i in range(NS):
        write(NF + i, keep * h[i] + common)
    factor = (0.5 * solute_omega) * level / jnp.maximum(density, 0.5)
    fx, fy, fz = factor * px, factor * py, factor * pz

    g = reads(0, NF)
    a = {i: g[i] + g[i + 1] for i in range(1, NF, 2)}
    d = {i: g[i] - g[i + 1] for i in range(1, NF, 2)}
    m1x = (d[1] + d[1]) + (d[7] + d[9]) + (d[11] + d[13])
    m1y = (d[3] + d[3]) + (d[7] - d[9]) + (d[15] + d[17])
    m1z = (d[5] + d[5]) + (d[11] - d[13]) + (d[15] - d[17])
    exy, exz, eyz = a[7] + a[9], a[11] + a[13], a[15] + a[17]
    tx, ty, tz = a[1] + a[1], a[3] + a[3], a[5] + a[5]
    mxx, myy, mzz = tx + exy + exz, ty + exy + eyz, tz + exz + eyz
    mxy, mxz, myz = a[7] - a[9], a[11] - a[13], a[15] - a[17]
    m0 = 12.0 * g[0] + (tx + ty + tz) + (exy + exz + eyz)
    qx = mxx * ux + mxy * uy + mxz * uz
    qy = mxy * ux + myy * uy + myz * uz
    qz = mxz * ux + myz * uy + mzz * uz
    square = ux * ux + uy * uy + uz * uz
    scaled = flow_omega / 36.0
    zero = m0 * (scaled + (1.5 * scaled) * square) - (4.5 * scaled) * (qx * ux + qy * uy + qz * uz)
    zero = valid * (zero - (fx * ux + fy * uy + fz * uz))
    bx = valid * ((3.0 * scaled) * (m1x + 3.0 * qx - m0 * ux) + fx)
    by = valid * ((3.0 * scaled) * (m1y + 3.0 * qy - m0 * uy) + fy)
    bz = valid * ((3.0 * scaled) * (m1z + 3.0 * qz - m0 * uz) + fz)
    keep = (1.0 - flow_omega) * valid
    write(0, keep * g[0] + zero)
    moves = {1: bx, 3: by, 5: bz, 7: bx + by, 9: bx - by, 11: bx + bz, 13: bx - bz, 15: by + bz, 17: by - bz}
    for i, move in moves.items():
        write(i, keep * g[i] + (zero + move))
        write(i + 1, keep * g[i + 1] + (zero - move))


VMEM = pl.BlockSpec(memory_space=pltpu.VMEM)
SMEM = pl.BlockSpec(memory_space=pltpu.SMEM)
ANY = pl.BlockSpec(memory_space=pl.ANY)
HBM = pl.BlockSpec(memory_space=pltpu.HBM)


def call(kernel, ins, outs, name, cost, scratch=(), limit=VMEM_LIMIT, place=VMEM, aliases={}):
    return pl.pallas_call(
        kernel,
        in_specs=ins,
        out_shape=outs,
        out_specs=[place] * len(outs),
        input_output_aliases=aliases,
        scratch_shapes=list(scratch),
        name=name,
        cost_estimate=pl.CostEstimate(flops=cost, bytes_accessed=1 << 23, transcendentals=0),
        compiler_params=pltpu.CompilerParams(vmem_limit_bytes=limit),
    )


def per_device(flow_adjoint, solute_adjoint, flow_density, flow_velocity, solute_level, solid, owner):
    steps = flow_density.shape[0]
    nx, ny, depth = solid.shape
    plan = Plan(steps, nx, ny, depth)
    ring = lax.axis_size("gz")
    w = plan.halo
    arguments = (flow_adjoint, solute_adjoint, flow_density, flow_velocity, solute_level, solid)
    fields = [f.reshape(-1, nx * ny, depth) for f in arguments]
    owner, *fields = (pltpu.with_memory_space_constraint(f, pltpu.HBM) for f in (owner, *fields))

    def move(value, axis, by):
        size = lax.axis_size(axis)
        return lax.ppermute(value, axis, [(i, i + by) for i in range(size) if 0 <= i + by < size])

    parts = 1 if ring == 2 else 2

    def like(channels):
        return jax.ShapeDtypeStruct((channels, nx * ny, depth), F32)

    *packed, flow, solute, wide = call(
        functools.partial(pack_kernel, plan, ring, parts),
        [SMEM] + [HBM] * 6,
        [jax.ShapeDtypeStruct((plan.sent, 8, depth), F32)] * parts + [like(NF), like(NS), like(plan.chan - SOLID)],
        "pack_column",
        1 << 22,
        [pltpu.VMEM(f.shape, f.dtype) for f in fields[2:]] + [pltpu.SemaphoreType.DMA((8,))],
    )(owner, *fields)
    loaded = (flow, solute, wide)
    if ring == 2:
        received = [lax.ppermute(packed[0], "gz", [(0, 1), (1, 0)])]
    else:
        received = [move(packed[0], "gz", 1), move(packed[1], "gz", -1)]

    slab = [jax.ShapeDtypeStruct((plan.slab, nx, depth), F32)] * 2
    raw = call(functools.partial(faces_kernel, plan), [VMEM] * 3 + [ANY], slab, "faces", 1 << 24)(
        *loaded, packed[0]
    )
    y_low, y_high = call(
        functools.partial(insert_kernel, plan, ring, parts), [SMEM] + [VMEM] * (2 + parts), slab, "insert", 1 << 22, (), 24 << 20
    )(owner, *raw, *received)
    from_y_low = move(y_high, "gy", 1)
    from_y_high = move(y_low, "gy", -1)
    state = jax.ShapeDtypeStruct((SOLID, plan.height, depth), F32)
    saved = jax.ShapeDtypeStruct((plan.chan - SOLID, plan.height, depth), F32)
    flags = jax.ShapeDtypeStruct((3, plan.height, depth), F32)
    cells, kept, x_low, x_high = call(
        functools.partial(inner_kernel, plan, ring, parts),
        [SMEM] + [VMEM] * (3 + parts),
        [state, saved] + [jax.ShapeDtypeStruct((plan.slab, ny, depth), F32)] * 2,
        "inner",
        1 << 24,
    )(owner, *loaded, *received)
    from_x_low = move(x_high, "gx", 1)
    from_x_high = move(x_low, "gx", -1)
    other, masks = call(
        functools.partial(middle_kernel, plan), [SMEM] + [VMEM] * 2, [state, flags], "middle", 1 << 24, (), 8 << 20
    )(owner, cells, kept)

    def rows(value):
        return value.reshape(-1, depth)

    corner = jax.ShapeDtypeStruct((plan.slab * 2 * w, depth), F32)
    c_low, c_high = call(
        functools.partial(corners_kernel, plan), [VMEM] * 2 + [ANY], [corner, corner], "corners", 1 << 20
    )(rows(from_y_low), rows(from_y_high), masks)
    shape = (plan.slab, 2 * w, depth)
    from_c_low = move(c_high, "gx", 1).reshape(shape)
    from_c_high = move(c_low, "gx", -1).reshape(shape)
    assembled = [pltpu.with_memory_space_constraint(a, pltpu.VMEM) for a in (cells, kept, other, masks)]
    assembled = call(
        functools.partial(first_kernel, plan),
        [SMEM] + [VMEM] * 8,
        [state, saved, state, flags],
        "first",
        1 << 26,
        (),
        8 << 20,
        aliases={5: 0, 6: 1, 7: 2, 8: 3},
    )(owner, from_y_low, from_y_high, from_x_low, from_x_high, *assembled)
    flow, solute = call(
        functools.partial(steps_kernel, plan),
        [SMEM] + [VMEM] * 6,
        [jax.ShapeDtypeStruct(flow_adjoint.shape, F32), jax.ShapeDtypeStruct(solute_adjoint.shape, F32)],
        "steps",
        1 << 28,
        [
            pltpu.VMEM((NF, nx, ny, depth), F32),
            pltpu.VMEM((NS, nx, ny, depth), F32),
            pltpu.SemaphoreType.DMA((2, nx)),
        ],
        10 << 20,
        ANY,
    )(owner, *assembled, from_c_low, from_c_high)
    return (flow, solute)


def solution(mesh):
    in_specs = (
        P(None, "gx", "gy", "gz"),
        P(None, "gx", "gy", "gz"),
        P(None, "gx", "gy", "gz"),
        P(None, None, "gx", "gy", "gz"),
        P(None, "gx", "gy", "gz"),
        P("gx", "gy", "gz"),
        P(),
    )
    out_specs = (P(None, "gx", "gy", "gz"), P(None, "gx", "gy", "gz"))
    return jax.shard_map(
        per_device, mesh=mesh, in_specs=in_specs, out_specs=out_specs, check_vma=False
    )
```

```python
import functools

import jax
import jax.numpy as jnp
from jax import lax
from jax.experimental import pallas as pl
from jax.experimental.pallas import tpu as pltpu
from jax.sharding import PartitionSpec as P

BZC = 16

FLOW_DIRS = [
    (0, 0, 0),
    (1, 0, 0),
    (-1, 0, 0),
    (0, 1, 0),
    (0, -1, 0),
    (0, 0, 1),
    (0, 0, -1),
    (1, 1, 0),
    (-1, -1, 0),
    (1, -1, 0),
    (-1, 1, 0),
    (1, 0, 1),
    (-1, 0, -1),
    (1, 0, -1),
    (-1, 0, 1),
    (0, 1, 1),
    (0, -1, -1),
    (0, 1, -1),
    (0, -1, 1),
]
NF = 19
NS = 7
OPPOSITE = [FLOW_DIRS.index((-a, -b, -c)) for a, b, c in FLOW_DIRS]
SOLID = NF + NS
AUX = SOLID + 1
NA = 5
flow_omega = 1.25
solute_omega = 1.6
langmuir_rate = 0.05
VMEM_LIMIT = 24 << 20
F32 = jnp.float32
PAD = 8


class Plan:
    def __init__(self, steps, nx, ny, depth):
        self.steps, self.nx, self.ny, self.depth = steps, nx, ny, depth
        self.halo = w = steps
        self.chan = AUX + NA * steps
        self.sent = AUX + NA * (steps - 1)
        self.pitch = -(-(ny + 2 * w) // 8) * 8
        self.wide = nx + 2 * w
        self.height = self.wide * self.pitch + 2 * PAD
        self.tiles = list(range(self.pitch // 8))
        self.inside = [h for h in self.tiles if 8 * h > w and 8 * h + 8 < w + ny]
        self.outside = [h for h in self.tiles if h not in self.inside]
        self.count = {k: AUX + NA * (steps - k) for k in range(1, w)}
        self.base, at = {}, 0
        for k in range(1, w):
            self.base[k] = at
            at += self.count[k]
        self.base[w] = at
        self.slab = at + 7

    def last(self, axis, sign):
        flow = [i for i, c in enumerate(FLOW_DIRS) if c[axis] == sign]
        solute = [NF + i for i, c in enumerate(FLOW_DIRS[:NS]) if c[axis] == sign]
        return flow + solute + [SOLID]


def lanes(depth):
    return lax.broadcasted_iota(jnp.int32, (8, depth), 1)


def occupied(owner_ref):
    me = lax.axis_index("gz")
    count = jnp.int32(0)
    for j in range(owner_ref.shape[0]):
        count = count + jnp.where(owner_ref[j] == me, 1, 0).astype(jnp.int32)
    return count * BZC


def z_places(plan, length, ring):
    w, depth = plan.halo, plan.depth
    if ring == 2:
        first = lax.axis_index("gz") == 0
        return [(jnp.where(first, length - w, 0), jnp.where(first, length, depth - w))]
    return [(length - w, jnp.int32(depth - w)), (jnp.int32(0), length)]


def each(number, body, unroll=4):
    def several(i, carry):
        for u in range(unroll):
            body(i * unroll + u)
        return carry

    turns = number // unroll
    if turns > 1:
        lax.fori_loop(0, turns, several, 0)
    else:
        turns = 0
    for i in range(turns * unroll, number):
        body(i)


def tiles_of(plan):
    return [(y * (plan.nx // 8) + h, y, 8 * h) for y in range(plan.ny) for h in range(plan.nx // 8)]


def pack_kernel(plan, ring, parts, owner, flow, solute, density, velocity, level, solid, *refs):
    outs, (flow_out, solute_out, wide), (density_in, velocity_in, level_in, solid_in, sems) = (
        refs[:parts],
        refs[parts : parts + 3],
        refs[parts + 3 :],
    )
    w, depth, nx, ny = plan.halo, plan.depth, plan.nx, plan.ny
    cuts = [0, 7, 13, NF]
    flows = [pl.ds(a, b - a) for a, b in zip(cuts, cuts[1:])]
    pairs = [(flow.at[cut], flow_out.at[cut]) for cut in flows] + [
        (solute, solute_out),
        (solid, solid_in),
        (density, density_in),
        (level, level_in),
        (velocity, velocity_in),
    ]
    copies = [pltpu.make_async_copy(a, b, sems.at[i]) for i, (a, b) in enumerate(pairs)]
    for copy in copies:
        copy.start()

    length = occupied(owner)
    group = lanes(depth) // w
    places = z_places(plan, length, ring)
    shifts = [{n: (w * n + depth - start) & (depth - 1) for n, _, _ in tiles_of(plan)} for start, _ in places]

    def pack(at, first, number, ref):
        def one(i):
            packed = [None] * parts
            for n, y, x in tiles_of(plan):
                tile = ref[first + i, pl.ds(x * ny + y, 8, stride=ny), :]
                for p in range(parts):
                    moved = pltpu.roll(tile, shifts[p][n], 1)
                    packed[p] = moved if n == 0 else jnp.where(group == n, moved, packed[p])
            for p in range(parts):
                outs[p][at + first + i] = packed[p]

        each(number, one, 6)

    for copy, a, b in zip(copies, cuts, cuts[1:]):
        copy.wait()
        pack(0, a, b - a, flow_out)
    for copy in copies[3:]:
        copy.wait()
    pack(NF, 0, NS, solute_out)
    sources = [(solid_in, 0)]
    for s in range(plan.steps):
        t = plan.steps - 1 - s
        sources += [(density_in, t), (level_in, t)] + [(velocity_in, 3 * t + i) for i in range(3)]
    for c, (ref, i) in enumerate(sources):
        for x in range(nx):
            wide[c, x * ny : (x + 1) * ny, :] = ref[i, x * ny : (x + 1) * ny, :].astype(F32)
    pack(SOLID, 0, plan.sent - SOLID, wide)


def faces_kernel(plan, flow, solute, wide, packed, y_low, y_high):
    w, nx, ny = plan.halo, plan.nx, plan.ny
    for at, number, ref in ((0, NF, flow), (NF, NS, solute), (SOLID, plan.sent - SOLID, wide)):

        def row(c, y, ref=ref):
            return ref[c, pl.ds(y, nx, stride=ny), :]

        for k in range(1, w):

            def one(c, k=k, at=at, row=row):
                y_low[plan.base[k] + at + c] = row(c, k - 1)
                y_high[plan.base[k] + at + c] = row(c, ny - k)

            each(min(number, plan.count[k] - at), one)
        for out, sign, y in ((y_low, 1, w - 1), (y_high, -1, ny - w)):
            for j, c in enumerate(plan.last(1, sign)):
                if at <= c < at + number:
                    out[plan.base[w] + j] = row(c - at, y)


def column(plan, ring, owner, received):
    w, depth = plan.halo, plan.depth
    length = occupied(owner)
    lane = lanes(depth)
    live = lane < length
    places = [to for _, to in z_places(plan, length, ring)]
    halos = [((lane - to) & (depth - 1)) < w for to in places]
    shifts = [{n: (to + depth - w * n) & (depth - 1) for n, _, _ in tiles_of(plan)} for to in places]

    def put(tile, slabs, n):
        tile = jnp.where(live, tile, 0.0)
        for slab, halo, shift in zip(slabs, halos, shifts):
            tile = jnp.where(halo, pltpu.roll(slab, shift[n], 1), tile)
        return tile

    return put


def insert_kernel(plan, ring, parts, owner, low, high, *rest):
    received, (y_low, y_high) = rest[:parts], rest[parts:]
    put = column(plan, ring, owner, received)
    w, ny = plan.halo, plan.ny
    tall = plan.nx // 8

    def one(raw, out, j, c, y):
        slabs = [r[c] for r in received]
        for h in range(tall):
            out[j, 8 * h : 8 * h + 8, :] = put(raw[j, 8 * h : 8 * h + 8, :], slabs, y * tall + h)

    for k in range(1, w):

        def both(c, k=k):
            one(low, y_low, plan.base[k] + c, c, k - 1)
            one(high, y_high, plan.base[k] + c, c, ny - k)

        each(plan.count[k], both, 10)
    for raw, out, sign, y in ((low, y_low, 1, w - 1), (high, y_high, -1, ny - w)):
        for j, c in enumerate(plan.last(1, sign)):
            one(raw, out, plan.base[w] + j, c, y)


def inner_kernel(plan, ring, parts, owner, flow, solute, wide, *rest):
    received, (cells, fields, x_low, x_high) = rest[:parts], rest[parts:]
    w, nx, ny, pitch = plan.halo, plan.nx, plan.ny, plan.pitch
    put = column(plan, ring, owner, received)
    for at, number, ref, out, to in (
        (0, NF, flow, cells, 0),
        (NF, NS, solute, cells, NF),
        (SOLID, plan.chan - SOLID, wide, fields, 0),
    ):

        def one(i, sent=True, at=at, ref=ref, out=out, to=to):
            slabs = [r[at + i] for r in received] if sent else []
            for n, y, x in tiles_of(plan):
                tile = ref[i, pl.ds(x * ny + y, 8, stride=ny), :]
                out[to + i, pl.ds(PAD + (w + x) * pitch + w + y, 8, stride=pitch), :] = put(tile, slabs, n)

        within = min(number, plan.sent - at)
        each(within, one, 3)
        each(number - within, lambda i, one=one, within=within: one(within + i, False), 1)

    def row(ref, c, x):
        at = PAD + (w + x) * pitch + w
        return ref[c, at : at + ny, :]

    for k in range(1, w):

        def both(ref, c, j, k=k):
            x_low[plan.base[k] + j] = row(ref, c, k - 1)
            x_high[plan.base[k] + j] = row(ref, c, nx - k)

        channels(cells, fields, plan.count[k], both)
    for slab, sign, x in ((x_low, 1, w - 1), (x_high, -1, nx - w)):
        for j, c in enumerate(plan.last(0, sign)):
            ref, at = (cells, c) if c < SOLID else (fields, c - SOLID)
            slab[plan.base[w] + j] = row(ref, at, x)


def middle_kernel(plan, owner, cells, fields, other, masks):
    w, nx = plan.halo, plan.nx
    prepare(plan, owner, fields, masks, w, w + nx)
    sweep(plan, owner, cells, other, fields, masks, 0, w + 1, w + nx - 1, plan.inside)


def corners_kernel(plan, from_low, from_high, masks, low, high):
    w, nx, ny = plan.halo, plan.nx, plan.ny
    low[...] = jnp.zeros(low.shape, F32)
    high[...] = jnp.zeros(high.shape, F32)
    tall = 2 * w
    for out, sign in ((low, 1), (high, -1)):
        x_last = plan.last(0, sign)
        for k in range(1, w + 1):
            x = k - 1 if sign == 1 else nx - k
            for m in range(1, w + 1):
                for source, row, y_sign in ((from_low, w - m, -1), (from_high, w - 1 + m, 1)):
                    y_last = plan.last(1, y_sign)
                    if k < w and m < w:
                        number = min(plan.count[k], plan.count[m])
                        out[pl.ds(plan.base[k] * tall + row, number, stride=tall), :] = source[
                            pl.ds(plan.base[m] * nx + x, number, stride=nx), :
                        ]
                        continue
                    for c in range(AUX):
                        if (k == w and c not in x_last) or (m == w and c not in y_last):
                            continue
                        to = plan.base[k] + (x_last.index(c) if k == w else c)
                        at = plan.base[m] + (y_last.index(c) if m == w else c)
                        out[to * tall + row : to * tall + row + 1, :] = source[at * nx + x : at * nx + x + 1, :]


def channels(cells, fields, number, body):
    each(SOLID, lambda c: body(cells, c, c))
    each(number - SOLID, lambda c: body(fields, c, SOLID + c))


def insert_layers(plan, cells, fields, axis, parts, put):
    w = plan.halo
    for k in range(1, w + 1):
        for part, sign in zip(parts, (-1, 1)):
            if k < w:
                channels(
                    cells,
                    fields,
                    plan.count[k],
                    lambda ref, c, j, k=k, part=part, sign=sign: put(ref, c, part, plan.base[k] + j, k, sign),
                )
                continue
            for j, c in enumerate(plan.last(axis, sign)):
                ref, at = (cells, c) if c < SOLID else (fields, c - SOLID)
                put(ref, at, part, plan.base[w] + j, k, sign)


def first_kernel(plan, owner, y_low, y_high, x_low, x_high, *refs):
    cells, fields, other, masks = refs[4:]
    w, nx, ny, pitch = plan.halo, plan.nx, plan.ny, plan.pitch

    def put_x(ref, c, part, j, k, sign):
        row = PAD + (w - k if sign < 0 else w + nx - 1 + k) * pitch + w
        ref[c, row : row + ny, :] = part[j]

    insert_layers(plan, cells, fields, 0, (x_low, x_high), put_x)

    def put_y(ref, c, part, j, m, sign):
        row = PAD + w * pitch + (w - m if sign < 0 else w + ny - 1 + m)
        ref[c, pl.ds(row, nx, stride=pitch), :] = part[j]

    insert_layers(plan, cells, fields, 1, (y_low, y_high), put_y)
    prepare(plan, owner, fields, masks, w, w + nx, plan.outside)
    sweep(plan, owner, cells, other, fields, masks, 0, w + 1, w + nx - 1, plan.outside)
    buffers = [cells, other]
    for s in range(1, plan.steps - 1):
        sweep(plan, owner, buffers[s % 2], buffers[(s + 1) % 2], fields, masks, s, w + 1 + s, w + nx - 1 - s)


def steps_kernel(plan, owner, cells, fields, other, masks, c_low, c_high, flow_hbm, solute_hbm, flow_out, solute_out, sems):
    w, nx, ny, pitch = plan.halo, plan.nx, plan.ny, plan.pitch

    def put(ref, c, part, j, k, sign):
        row = PAD + (w - k if sign < 0 else w + nx - 1 + k) * pitch
        ref[c, row : row + w, :] = part[j, 0:w, :]
        ref[c, row + w + ny : row + w + ny + w, :] = part[j, w : 2 * w, :]

    insert_layers(plan, cells, fields, 0, (c_low, c_high), put)
    prepare(plan, owner, fields, masks, 0, w)
    prepare(plan, owner, fields, masks, w + nx, plan.wide)
    buffers = [cells, other]
    for s in range(plan.steps - 1):
        source, target = buffers[s % 2], buffers[(s + 1) % 2]
        sweep(plan, owner, source, target, fields, masks, s, 1 + s, w + 1 + s)
        sweep(plan, owner, source, target, fields, masks, s, w + nx - 1 - s, plan.wide - 1 - s)
    s = plan.steps - 1
    source = buffers[s % 2]

    def leave(x):
        return [
            pltpu.make_async_copy(ref.at[:, x], to.at[:, x], sems.at[n, x])
            for n, (ref, to) in enumerate(((flow_out, flow_hbm), (solute_out, solute_hbm)))
        ]

    def last(x, carry):
        for h in range(ny // 8):
            row = PAD + (x + w) * pitch + w + 8 * h

            def write(c, value, h=h):
                if c < NF:
                    flow_out[c, x, 8 * h : 8 * h + 8, :] = value
                else:
                    solute_out[c - NF, x, 8 * h : 8 * h + 8, :] = value

            advance(plan, owner, source, fields, masks, s, row, write)
        for copy in leave(x):
            copy.start()
        return carry

    lax.fori_loop(0, nx, last, 0)
    for x in range(nx):
        for copy in leave(x):
            copy.wait()


def prepare(plan, owner, fields, masks, from_x, to_x, tiles=None):
    w, nx, ny, depth, pitch = plan.halo, plan.nx, plan.ny, plan.depth, plan.pitch
    length = occupied(owner)
    lane = lanes(depth)
    gx, gy, gz = (lax.axis_index(a) for a in ("gx", "gy", "gz"))
    last_x, last_y, last_z = (lax.axis_size(a) - 1 for a in ("gx", "gy", "gz"))
    above = jnp.where(gz < last_z, w, 0)
    below = jnp.where(gz > 0, w, 0)
    in_z = (lane < length + above) | (lane >= depth - below)
    y_first = jnp.where(gy > 0, 0, w)
    y_end = jnp.where(gy < last_y, ny + 2 * w, w + ny)
    x_first = jnp.where(gx > 0, 0, w)
    x_end = jnp.where(gx < last_x, nx + 2 * w, w + nx)
    sub = lax.broadcasted_iota(jnp.int32, (8, depth), 0)

    def one(i):
        x = from_x + i
        in_x = ((x >= x_first) & (x < x_end)).astype(F32)
        for h in tiles or plan.tiles:
            row = pl.multiple_of(PAD + x * pitch + 8 * h, 8)
            flags = fields[0, pl.ds(row, 8), :]
            y = sub + 8 * h
            masks[0, pl.ds(row, 8), :] = pltpu.roll(flags, depth - 1, 1)
            masks[1, pl.ds(row, 8), :] = pltpu.roll(flags, 1, 1)
            inside = in_z & (y >= y_first) & (y < y_end) & (flags == 0.0)
            masks[2, pl.ds(row, 8), :] = jnp.where(inside, in_x, 0.0)

    each(to_x - from_x, one)


def sweep(plan, owner, source, target, fields, masks, s, from_x, to_x, tiles=None):
    pitch = plan.pitch

    def body(x, carry):
        for h in tiles or plan.tiles:
            row = pl.multiple_of(PAD + pitch * x + 8 * h, 8)

            def write(c, value, row=row):
                target[c, pl.ds(row, 8), :] = value

            advance(plan, owner, source, fields, masks, s, row, write)
        return carry

    lax.fori_loop(from_x, to_x, body, 0)


def advance(plan, owner, source, fields, masks, s, row, write):
    depth, pitch = plan.depth, plan.pitch
    def field(ref, c, move=0):
        return ref[c, pl.ds(row + move, 8), :]

    blocked = {}

    def reads(first, number):
        result = []
        for i in range(number):
            sx, sy, sz = FLOW_DIRS[i]
            if i == 0:
                result.append(field(source, first))
                continue
            move = sx * pitch + sy
            near = field(source, first + i, move)
            if sz:
                near = pltpu.roll(near, (depth - sz) % depth, 1)
            if i not in blocked:
                flags = field(fields, 0, move) if sz == 0 else field(masks, 0 if sz == 1 else 1, move)
                blocked[i] = flags != 0.0
            result.append(jnp.where(blocked[i], field(source, first + OPPOSITE[i]), near))
        return result

    valid = field(masks, 2)
    if s == plan.steps - 1:
        valid = jnp.where(lanes(depth) < occupied(owner), valid, 0.0)
    aux = AUX - SOLID + NA * s
    density, level, ux, uy, uz = (field(fields, aux + n) for n in range(NA))

    h = reads(NF, NS)
    px, py, pz = h[1] - h[2], h[3] - h[4], h[5] - h[6]
    p0 = 0.25 * h[0] + 0.125 * ((h[1] + h[2]) + (h[3] + h[4]) + (h[5] + h[6]))
    grown = 1.0 + level
    uptake = langmuir_rate / (grown * grown)
    common = valid * (
        (solute_omega - uptake) * p0 + (solute_omega * 0.5) * (px * ux + py * uy + pz * uz)
    )
    keep = (1.0 - solute_omega) * valid
    for i in range(NS):
        write(NF + i, keep * h[i] + common)
    factor = (0.5 * solute_omega) * level / jnp.maximum(density, 0.5)
    fx, fy, fz = factor * px, factor * py, factor * pz

    g = reads(0, NF)
    a = {i: g[i] + g[i + 1] for i in range(1, NF, 2)}
    d = {i: g[i] - g[i + 1] for i in range(1, NF, 2)}
    m1x = (d[1] + d[1]) + (d[7] + d[9]) + (d[11] + d[13])
    m1y = (d[3] + d[3]) + (d[7] - d[9]) + (d[15] + d[17])
    m1z = (d[5] + d[5]) + (d[11] - d[13]) + (d[15] - d[17])
    exy, exz, eyz = a[7] + a[9], a[11] + a[13], a[15] + a[17]
    tx, ty, tz = a[1] + a[1], a[3] + a[3], a[5] + a[5]
    mxx, myy, mzz = tx + exy + exz, ty + exy + eyz, tz + exz + eyz
    mxy, mxz, myz = a[7] - a[9], a[11] - a[13], a[15] - a[17]
    m0 = 12.0 * g[0] + (tx + ty + tz) + (exy + exz + eyz)
    qx = mxx * ux + mxy * uy + mxz * uz
    qy = mxy * ux + myy * uy + myz * uz
    qz = mxz * ux + myz * uy + mzz * uz
    square = ux * ux + uy * uy + uz * uz
    scaled = flow_omega / 36.0
    zero = m0 * (scaled + (1.5 * scaled) * square) - (4.5 * scaled) * (qx * ux + qy * uy + qz * uz)
    zero = valid * (zero - (fx * ux + fy * uy + fz * uz))
    bx = valid * ((3.0 * scaled) * (m1x + 3.0 * qx - m0 * ux) + fx)
    by = valid * ((3.0 * scaled) * (m1y + 3.0 * qy - m0 * uy) + fy)
    bz = valid * ((3.0 * scaled) * (m1z + 3.0 * qz - m0 * uz) + fz)
    keep = (1.0 - flow_omega) * valid
    write(0, keep * g[0] + zero)
    moves = {1: bx, 3: by, 5: bz, 7: bx + by, 9: bx - by, 11: bx + bz, 13: bx - bz, 15: by + bz, 17: by - bz}
    for i, move in moves.items():
        write(i, keep * g[i] + (zero + move))
        write(i + 1, keep * g[i + 1] + (zero - move))


VMEM = pl.BlockSpec(memory_space=pltpu.VMEM)
SMEM = pl.BlockSpec(memory_space=pltpu.SMEM)
ANY = pl.BlockSpec(memory_space=pl.ANY)
HBM = pl.BlockSpec(memory_space=pltpu.HBM)


def call(kernel, ins, outs, name, cost, scratch=(), limit=VMEM_LIMIT, place=VMEM, aliases={}):
    return pl.pallas_call(
        kernel,
        in_specs=ins,
        out_shape=outs,
        out_specs=[place] * len(outs),
        input_output_aliases=aliases,
        scratch_shapes=list(scratch),
        name=name,
        cost_estimate=pl.CostEstimate(flops=cost, bytes_accessed=1 << 23, transcendentals=0),
        compiler_params=pltpu.CompilerParams(vmem_limit_bytes=limit),
    )


def per_device(flow_adjoint, solute_adjoint, flow_density, flow_velocity, solute_level, solid, owner):
    steps = flow_density.shape[0]
    nx, ny, depth = solid.shape
    plan = Plan(steps, nx, ny, depth)
    ring = lax.axis_size("gz")
    w = plan.halo
    arguments = (flow_adjoint, solute_adjoint, flow_density, flow_velocity, solute_level, solid)
    fields = [f.reshape(-1, nx * ny, depth) for f in arguments]
    owner, *fields = (pltpu.with_memory_space_constraint(f, pltpu.HBM) for f in (owner, *fields))

    def move(value, axis, by):
        size = lax.axis_size(axis)
        return lax.ppermute(value, axis, [(i, i + by) for i in range(size) if 0 <= i + by < size])

    parts = 1 if ring == 2 else 2

    def like(channels):
        return jax.ShapeDtypeStruct((channels, nx * ny, depth), F32)

    *packed, flow, solute, wide = call(
        functools.partial(pack_kernel, plan, ring, parts),
        [SMEM] + [HBM] * 6,
        [jax.ShapeDtypeStruct((plan.sent, 8, depth), F32)] * parts + [like(NF), like(NS), like(plan.chan - SOLID)],
        "pack_column",
        1 << 22,
        [pltpu.VMEM(f.shape, f.dtype) for f in fields[2:]] + [pltpu.SemaphoreType.DMA((8,))],
    )(owner, *fields)
    loaded = (flow, solute, wide)
    if ring == 2:
        received = [lax.ppermute(packed[0], "gz", [(0, 1), (1, 0)])]
    else:
        received = [move(packed[0], "gz", 1), move(packed[1], "gz", -1)]

    slab = [jax.ShapeDtypeStruct((plan.slab, nx, depth), F32)] * 2
    raw = call(functools.partial(faces_kernel, plan), [VMEM] * 3 + [ANY], slab, "faces", 1 << 24)(
        *loaded, packed[0]
    )
    y_low, y_high = call(
        functools.partial(insert_kernel, plan, ring, parts), [SMEM] + [VMEM] * (2 + parts), slab, "insert", 1 << 22, (), 24 << 20
    )(owner, *raw, *received)
    from_y_low = move(y_high, "gy", 1)
    from_y_high = move(y_low, "gy", -1)
    state = jax.ShapeDtypeStruct((SOLID, plan.height, depth), F32)
    saved = jax.ShapeDtypeStruct((plan.chan - SOLID, plan.height, depth), F32)
    flags = jax.ShapeDtypeStruct((3, plan.height, depth), F32)
    cells, kept, x_low, x_high = call(
        functools.partial(inner_kernel, plan, ring, parts),
        [SMEM] + [VMEM] * (3 + parts),
        [state, saved] + [jax.ShapeDtypeStruct((plan.slab, ny, depth), F32)] * 2,
        "inner",
        1 << 24,
    )(owner, *loaded, *received)
    from_x_low = move(x_high, "gx", 1)
    from_x_high = move(x_low, "gx", -1)
    other, masks = call(
        functools.partial(middle_kernel, plan), [SMEM] + [VMEM] * 2, [state, flags], "middle", 1 << 24, (), 8 << 20
    )(owner, cells, kept)

    def rows(value):
        return value.reshape(-1, depth)

    corner = jax.ShapeDtypeStruct((plan.slab * 2 * w, depth), F32)
    c_low, c_high = call(
        functools.partial(corners_kernel, plan), [VMEM] * 2 + [ANY], [corner, corner], "corners", 1 << 20
    )(rows(from_y_low), rows(from_y_high), masks)
    shape = (plan.slab, 2 * w, depth)
    from_c_low = move(c_high, "gx", 1).reshape(shape)
    from_c_high = move(c_low, "gx", -1).reshape(shape)
    assembled = [pltpu.with_memory_space_constraint(a, pltpu.VMEM) for a in (cells, kept, other, masks)]
    assembled = call(
        functools.partial(first_kernel, plan),
        [SMEM] + [VMEM] * 8,
        [state, saved, state, flags],
        "first",
        1 << 26,
        (),
        8 << 20,
        aliases={5: 0, 6: 1, 7: 2, 8: 3},
    )(owner, from_y_low, from_y_high, from_x_low, from_x_high, *assembled)
    flow, solute = call(
        functools.partial(steps_kernel, plan),
        [SMEM] + [VMEM] * 6,
        [jax.ShapeDtypeStruct(flow_adjoint.shape, F32), jax.ShapeDtypeStruct(solute_adjoint.shape, F32)],
        "steps",
        1 << 28,
        [
            pltpu.VMEM((NF, nx, ny, depth), F32),
            pltpu.VMEM((NS, nx, ny, depth), F32),
            pltpu.SemaphoreType.DMA((2, nx)),
        ],
        10 << 20,
        ANY,
    )(owner, *assembled, from_c_low, from_c_high)
    return (flow, solute)


def solution(mesh):
    in_specs = (
        P(None, "gx", "gy", "gz"),
        P(None, "gx", "gy", "gz"),
        P(None, "gx", "gy", "gz"),
        P(None, None, "gx", "gy", "gz"),
        P(None, "gx", "gy", "gz"),
        P("gx", "gy", "gz"),
        P(),
    )
    out_specs = (P(None, "gx", "gy", "gz"), P(None, "gx", "gy", "gz"))
    return jax.shard_map(
        per_device, mesh=mesh, in_specs=in_specs, out_specs=out_specs, check_vma=False
    )
```

```python
import functools

import jax
import jax.numpy as jnp
from jax import lax
from jax.experimental import pallas as pl
from jax.experimental.pallas import tpu as pltpu
from jax.sharding import PartitionSpec as P

BZC = 16

FLOW_DIRS = [
    (0, 0, 0),
    (1, 0, 0),
    (-1, 0, 0),
    (0, 1, 0),
    (0, -1, 0),
    (0, 0, 1),
    (0, 0, -1),
    (1, 1, 0),
    (-1, -1, 0),
    (1, -1, 0),
    (-1, 1, 0),
    (1, 0, 1),
    (-1, 0, -1),
    (1, 0, -1),
    (-1, 0, 1),
    (0, 1, 1),
    (0, -1, -1),
    (0, 1, -1),
    (0, -1, 1),
]
NF = 19
NS = 7
OPPOSITE = [FLOW_DIRS.index((-a, -b, -c)) for a, b, c in FLOW_DIRS]
SOLID = NF + NS
AUX = SOLID + 1
NA = 5
flow_omega = 1.25
solute_omega = 1.6
langmuir_rate = 0.05
VMEM_LIMIT = 24 << 20
F32 = jnp.float32
PAD = 8


class Plan:
    def __init__(self, steps, nx, ny, depth):
        self.steps, self.nx, self.ny, self.depth = steps, nx, ny, depth
        self.halo = w = steps
        self.chan = AUX + NA * steps
        self.sent = AUX + NA * (steps - 1)
        self.pitch = -(-(ny + 2 * w) // 8) * 8
        self.wide = nx + 2 * w
        self.height = self.wide * self.pitch + 2 * PAD
        self.tiles = list(range(self.pitch // 8))
        self.inside = [h for h in self.tiles if 8 * h > w and 8 * h + 8 < w + ny]
        self.outside = [h for h in self.tiles if h not in self.inside]
        self.count = {k: AUX + NA * (steps - k) for k in range(1, w)}
        self.base, at = {}, 0
        for k in range(1, w):
            self.base[k] = at
            at += self.count[k]
        self.base[w] = at
        self.slab = at + 7

    def last(self, axis, sign):
        flow = [i for i, c in enumerate(FLOW_DIRS) if c[axis] == sign]
        solute = [NF + i for i, c in enumerate(FLOW_DIRS[:NS]) if c[axis] == sign]
        return flow + solute + [SOLID]


def lanes(depth):
    return lax.broadcasted_iota(jnp.int32, (8, depth), 1)


def occupied(owner_ref):
    me = lax.axis_index("gz")
    count = jnp.int32(0)
    for j in range(owner_ref.shape[0]):
        count = count + jnp.where(owner_ref[j] == me, 1, 0).astype(jnp.int32)
    return count * BZC


def z_places(plan, length, ring):
    w, depth = plan.halo, plan.depth
    if ring == 2:
        first = lax.axis_index("gz") == 0
        return [(jnp.where(first, length - w, 0), jnp.where(first, length, depth - w))]
    return [(length - w, jnp.int32(depth - w)), (jnp.int32(0), length)]


def each(number, body, unroll=4):
    def several(i, carry):
        for u in range(unroll):
            body(i * unroll + u)
        return carry

    turns = number // unroll
    if turns > 1:
        lax.fori_loop(0, turns, several, 0)
    else:
        turns = 0
    for i in range(turns * unroll, number):
        body(i)


def tiles_of(plan):
    return [(y * (plan.nx // 8) + h, y, 8 * h) for y in range(plan.ny) for h in range(plan.nx // 8)]


def pack_kernel(plan, ring, parts, owner, flow, solute, density, velocity, level, solid, *refs):
    outs, (flow_out, solute_out, wide), (density_in, velocity_in, level_in, solid_in, sems) = (
        refs[:parts],
        refs[parts : parts + 3],
        refs[parts + 3 :],
    )
    w, depth, nx, ny = plan.halo, plan.depth, plan.nx, plan.ny
    cuts = [0, 7, 13, NF]
    flows = [pl.ds(a, b - a) for a, b in zip(cuts, cuts[1:])]
    pairs = [(flow.at[cut], flow_out.at[cut]) for cut in flows] + [
        (solute, solute_out),
        (solid, solid_in),
        (density, density_in),
        (level, level_in),
        (velocity, velocity_in),
    ]
    copies = [pltpu.make_async_copy(a, b, sems.at[i]) for i, (a, b) in enumerate(pairs)]
    for copy in copies:
        copy.start()

    length = occupied(owner)
    group = lanes(depth) // w
    places = z_places(plan, length, ring)
    shifts = [{n: (w * n + depth - start) & (depth - 1) for n, _, _ in tiles_of(plan)} for start, _ in places]

    def pack(at, first, number, ref):
        def one(i):
            packed = [None] * parts
            for n, y, x in tiles_of(plan):
                tile = ref[first + i, pl.ds(x * ny + y, 8, stride=ny), :]
                for p in range(parts):
                    moved = pltpu.roll(tile, shifts[p][n], 1)
                    packed[p] = moved if n == 0 else jnp.where(group == n, moved, packed[p])
            for p in range(parts):
                outs[p][at + first + i] = packed[p]

        each(number, one, 6)

    for copy, a, b in zip(copies, cuts, cuts[1:]):
        copy.wait()
        pack(0, a, b - a, flow_out)
    for copy in copies[3:]:
        copy.wait()
    pack(NF, 0, NS, solute_out)
    sources = [(solid_in, 0)]
    for s in range(plan.steps):
        t = plan.steps - 1 - s
        sources += [(density_in, t), (level_in, t)] + [(velocity_in, 3 * t + i) for i in range(3)]
    for c, (ref, i) in enumerate(sources):
        for x in range(nx):
            wide[c, x * ny : (x + 1) * ny, :] = ref[i, x * ny : (x + 1) * ny, :].astype(F32)
    pack(SOLID, 0, plan.sent - SOLID, wide)


def faces_kernel(plan, flow, solute, wide, packed, y_low, y_high):
    w, nx, ny = plan.halo, plan.nx, plan.ny
    for at, number, ref in ((0, NF, flow), (NF, NS, solute), (SOLID, plan.sent - SOLID, wide)):

        def row(c, y, ref=ref):
            return ref[c, pl.ds(y, nx, stride=ny), :]

        for k in range(1, w):

            def one(c, k=k, at=at, row=row):
                y_low[plan.base[k] + at + c] = row(c, k - 1)
                y_high[plan.base[k] + at + c] = row(c, ny - k)

            each(min(number, plan.count[k] - at), one)
        for out, sign, y in ((y_low, 1, w - 1), (y_high, -1, ny - w)):
            for j, c in enumerate(plan.last(1, sign)):
                if at <= c < at + number:
                    out[plan.base[w] + j] = row(c - at, y)


def column(plan, ring, owner, received):
    w, depth = plan.halo, plan.depth
    length = occupied(owner)
    lane = lanes(depth)
    live = lane < length
    places = [to for _, to in z_places(plan, length, ring)]
    halos = [((lane - to) & (depth - 1)) < w for to in places]
    shifts = [{n: (to + depth - w * n) & (depth - 1) for n, _, _ in tiles_of(plan)} for to in places]

    def put(tile, slabs, n):
        tile = jnp.where(live, tile, 0.0)
        for slab, halo, shift in zip(slabs, halos, shifts):
            tile = jnp.where(halo, pltpu.roll(slab, shift[n], 1), tile)
        return tile

    return put


def insert_kernel(plan, ring, parts, owner, low, high, *rest):
    received, (y_low, y_high) = rest[:parts], rest[parts:]
    put = column(plan, ring, owner, received)
    w, ny = plan.halo, plan.ny
    tall = plan.nx // 8

    def one(raw, out, j, c, y):
        slabs = [r[c] for r in received]
        for h in range(tall):
            out[j, 8 * h : 8 * h + 8, :] = put(raw[j, 8 * h : 8 * h + 8, :], slabs, y * tall + h)

    for k in range(1, w):

        def both(c, k=k):
            one(low, y_low, plan.base[k] + c, c, k - 1)
            one(high, y_high, plan.base[k] + c, c, ny - k)

        each(plan.count[k], both, 10)
    for raw, out, sign, y in ((low, y_low, 1, w - 1), (high, y_high, -1, ny - w)):
        for j, c in enumerate(plan.last(1, sign)):
            one(raw, out, plan.base[w] + j, c, y)


def inner_kernel(plan, ring, parts, owner, flow, solute, wide, *rest):
    received, (cells, fields, x_low, x_high) = rest[:parts], rest[parts:]
    w, nx, ny, pitch = plan.halo, plan.nx, plan.ny, plan.pitch
    put = column(plan, ring, owner, received)
    for at, number, ref, out, to in (
        (0, NF, flow, cells, 0),
        (NF, NS, solute, cells, NF),
        (SOLID, plan.chan - SOLID, wide, fields, 0),
    ):

        def one(i, sent=True, at=at, ref=ref, out=out, to=to):
            slabs = [r[at + i] for r in received] if sent else []
            for n, y, x in tiles_of(plan):
                tile = ref[i, pl.ds(x * ny + y, 8, stride=ny), :]
                out[to + i, pl.ds(PAD + (w + x) * pitch + w + y, 8, stride=pitch), :] = put(tile, slabs, n)

        within = min(number, plan.sent - at)
        each(within, one, 3)
        each(number - within, lambda i, one=one, within=within: one(within + i, False), 1)

    def row(ref, c, x):
        at = PAD + (w + x) * pitch + w
        return ref[c, at : at + ny, :]

    for k in range(1, w):

        def both(ref, c, j, k=k):
            x_low[plan.base[k] + j] = row(ref, c, k - 1)
            x_high[plan.base[k] + j] = row(ref, c, nx - k)

        channels(cells, fields, plan.count[k], both)
    for slab, sign, x in ((x_low, 1, w - 1), (x_high, -1, nx - w)):
        for j, c in enumerate(plan.last(0, sign)):
            ref, at = (cells, c) if c < SOLID else (fields, c - SOLID)
            slab[plan.base[w] + j] = row(ref, at, x)


def middle_kernel(plan, owner, cells, fields, other, masks):
    w, nx = plan.halo, plan.nx
    prepare(plan, owner, fields, masks, w, w + nx)
    sweep(plan, owner, cells, other, fields, masks, 0, w + 1, w + nx - 1, plan.inside)


def corners_kernel(plan, from_low, from_high, masks, low, high):
    w, nx, ny = plan.halo, plan.nx, plan.ny
    low[...] = jnp.zeros(low.shape, F32)
    high[...] = jnp.zeros(high.shape, F32)
    tall = 2 * w
    for out, sign in ((low, 1), (high, -1)):
        x_last = plan.last(0, sign)
        for k in range(1, w + 1):
            x = k - 1 if sign == 1 else nx - k
            for m in range(1, w + 1):
                for source, row, y_sign in ((from_low, w - m, -1), (from_high, w - 1 + m, 1)):
                    y_last = plan.last(1, y_sign)
                    if k < w and m < w:
                        number = min(plan.count[k], plan.count[m])
                        out[pl.ds(plan.base[k] * tall + row, number, stride=tall), :] = source[
                            pl.ds(plan.base[m] * nx + x, number, stride=nx), :
                        ]
                        continue
                    for c in range(AUX):
                        if (k == w and c not in x_last) or (m == w and c not in y_last):
                            continue
                        to = plan.base[k] + (x_last.index(c) if k == w else c)
                        at = plan.base[m] + (y_last.index(c) if m == w else c)
                        out[to * tall + row : to * tall + row + 1, :] = source[at * nx + x : at * nx + x + 1, :]


def channels(cells, fields, number, body):
    each(SOLID, lambda c: body(cells, c, c))
    each(number - SOLID, lambda c: body(fields, c, SOLID + c))


def insert_layers(plan, cells, fields, axis, parts, put):
    w = plan.halo
    for k in range(1, w + 1):
        for part, sign in zip(parts, (-1, 1)):
            if k < w:
                channels(
                    cells,
                    fields,
                    plan.count[k],
                    lambda ref, c, j, k=k, part=part, sign=sign: put(ref, c, part, plan.base[k] + j, k, sign),
                )
                continue
            for j, c in enumerate(plan.last(axis, sign)):
                ref, at = (cells, c) if c < SOLID else (fields, c - SOLID)
                put(ref, at, part, plan.base[w] + j, k, sign)


def first_kernel(plan, owner, y_low, y_high, x_low, x_high, *refs):
    cells, fields, other, masks = refs[4:]
    w, nx, ny, pitch = plan.halo, plan.nx, plan.ny, plan.pitch

    def put_x(ref, c, part, j, k, sign):
        row = PAD + (w - k if sign < 0 else w + nx - 1 + k) * pitch + w
        ref[c, row : row + ny, :] = part[j]

    insert_layers(plan, cells, fields, 0, (x_low, x_high), put_x)

    def put_y(ref, c, part, j, m, sign):
        row = PAD + w * pitch + (w - m if sign < 0 else w + ny - 1 + m)
        ref[c, pl.ds(row, nx, stride=pitch), :] = part[j]

    insert_layers(plan, cells, fields, 1, (y_low, y_high), put_y)
    prepare(plan, owner, fields, masks, w, w + nx, plan.outside)
    sweep(plan, owner, cells, other, fields, masks, 0, w + 1, w + nx - 1, plan.outside)
    buffers = [cells, other]
    for s in range(1, plan.steps - 1):
        sweep(plan, owner, buffers[s % 2], buffers[(s + 1) % 2], fields, masks, s, w + 1 + s, w + nx - 1 - s)


def steps_kernel(plan, owner, cells, fields, other, masks, c_low, c_high, flow_hbm, solute_hbm, flow_out, solute_out, sems):
    w, nx, ny, pitch = plan.halo, plan.nx, plan.ny, plan.pitch

    def put(ref, c, part, j, k, sign):
        row = PAD + (w - k if sign < 0 else w + nx - 1 + k) * pitch
        ref[c, row : row + w, :] = part[j, 0:w, :]
        ref[c, row + w + ny : row + w + ny + w, :] = part[j, w : 2 * w, :]

    insert_layers(plan, cells, fields, 0, (c_low, c_high), put)
    prepare(plan, owner, fields, masks, 0, w)
    prepare(plan, owner, fields, masks, w + nx, plan.wide)
    buffers = [cells, other]
    for s in range(plan.steps - 1):
        source, target = buffers[s % 2], buffers[(s + 1) % 2]
        sweep(plan, owner, source, target, fields, masks, s, 1 + s, w + 1 + s)
        sweep(plan, owner, source, target, fields, masks, s, w + nx - 1 - s, plan.wide - 1 - s)
    s = plan.steps - 1
    source = buffers[s % 2]

    def leave(x):
        return [
            pltpu.make_async_copy(ref.at[:, x], to.at[:, x], sems.at[n, x])
            for n, (ref, to) in enumerate(((flow_out, flow_hbm), (solute_out, solute_hbm)))
        ]

    def last(x):
        for h in range(ny // 8):
            row = PAD + (x + w) * pitch + w + 8 * h

            def write(c, value, h=h):
                if c < NF:
                    flow_out[c, x, 8 * h : 8 * h + 8, :] = value
                else:
                    solute_out[c - NF, x, 8 * h : 8 * h + 8, :] = value

            advance(plan, owner, source, fields, masks, s, row, write)
        for copy in leave(x):
            copy.start()

    each(nx, last, 2)
    for x in range(nx):
        for copy in leave(x):
            copy.wait()


def prepare(plan, owner, fields, masks, from_x, to_x, tiles=None):
    w, nx, ny, depth, pitch = plan.halo, plan.nx, plan.ny, plan.depth, plan.pitch
    length = occupied(owner)
    lane = lanes(depth)
    gx, gy, gz = (lax.axis_index(a) for a in ("gx", "gy", "gz"))
    last_x, last_y, last_z = (lax.axis_size(a) - 1 for a in ("gx", "gy", "gz"))
    above = jnp.where(gz < last_z, w, 0)
    below = jnp.where(gz > 0, w, 0)
    in_z = (lane < length + above) | (lane >= depth - below)
    y_first = jnp.where(gy > 0, 0, w)
    y_end = jnp.where(gy < last_y, ny + 2 * w, w + ny)
    x_first = jnp.where(gx > 0, 0, w)
    x_end = jnp.where(gx < last_x, nx + 2 * w, w + nx)
    sub = lax.broadcasted_iota(jnp.int32, (8, depth), 0)

    def one(i):
        x = from_x + i
        in_x = ((x >= x_first) & (x < x_end)).astype(F32)
        for h in tiles or plan.tiles:
            row = pl.multiple_of(PAD + x * pitch + 8 * h, 8)
            flags = fields[0, pl.ds(row, 8), :]
            y = sub + 8 * h
            masks[0, pl.ds(row, 8), :] = pltpu.roll(flags, depth - 1, 1)
            masks[1, pl.ds(row, 8), :] = pltpu.roll(flags, 1, 1)
            inside = in_z & (y >= y_first) & (y < y_end) & (flags == 0.0)
            masks[2, pl.ds(row, 8), :] = jnp.where(inside, in_x, 0.0)

    each(to_x - from_x, one)


def sweep(plan, owner, source, target, fields, masks, s, from_x, to_x, tiles=None):
    pitch = plan.pitch

    def body(i):
        x = from_x + i
        for h in tiles or plan.tiles:
            row = pl.multiple_of(PAD + pitch * x + 8 * h, 8)

            def write(c, value, row=row):
                target[c, pl.ds(row, 8), :] = value

            advance(plan, owner, source, fields, masks, s, row, write)

    each(to_x - from_x, body, 2)


def advance(plan, owner, source, fields, masks, s, row, write):
    depth, pitch = plan.depth, plan.pitch
    def field(ref, c, move=0):
        return ref[c, pl.ds(row + move, 8), :]

    blocked = {}

    def reads(first, number):
        result = []
        for i in range(number):
            sx, sy, sz = FLOW_DIRS[i]
            if i == 0:
                result.append(field(source, first))
                continue
            move = sx * pitch + sy
            near = field(source, first + i, move)
            if sz:
                near = pltpu.roll(near, (depth - sz) % depth, 1)
            if i not in blocked:
                flags = field(fields, 0, move) if sz == 0 else field(masks, 0 if sz == 1 else 1, move)
                blocked[i] = flags != 0.0
            result.append(jnp.where(blocked[i], field(source, first + OPPOSITE[i]), near))
        return result

    valid = field(masks, 2)
    if s == plan.steps - 1:
        valid = jnp.where(lanes(depth) < occupied(owner), valid, 0.0)
    aux = AUX - SOLID + NA * s
    density, level, ux, uy, uz = (field(fields, aux + n) for n in range(NA))

    h = reads(NF, NS)
    px, py, pz = h[1] - h[2], h[3] - h[4], h[5] - h[6]
    p0 = 0.25 * h[0] + 0.125 * ((h[1] + h[2]) + (h[3] + h[4]) + (h[5] + h[6]))
    grown = 1.0 + level
    uptake = langmuir_rate / (grown * grown)
    common = valid * (
        (solute_omega - uptake) * p0 + (solute_omega * 0.5) * (px * ux + py * uy + pz * uz)
    )
    keep = (1.0 - solute_omega) * valid
    for i in range(NS):
        write(NF + i, keep * h[i] + common)
    factor = (0.5 * solute_omega) * level / jnp.maximum(density, 0.5)
    fx, fy, fz = factor * px, factor * py, factor * pz

    g = reads(0, NF)
    a = {i: g[i] + g[i + 1] for i in range(1, NF, 2)}
    d = {i: g[i] - g[i + 1] for i in range(1, NF, 2)}
    m1x = (d[1] + d[1]) + (d[7] + d[9]) + (d[11] + d[13])
    m1y = (d[3] + d[3]) + (d[7] - d[9]) + (d[15] + d[17])
    m1z = (d[5] + d[5]) + (d[11] - d[13]) + (d[15] - d[17])
    exy, exz, eyz = a[7] + a[9], a[11] + a[13], a[15] + a[17]
    tx, ty, tz = a[1] + a[1], a[3] + a[3], a[5] + a[5]
    mxx, myy, mzz = tx + exy + exz, ty + exy + eyz, tz + exz + eyz
    mxy, mxz, myz = a[7] - a[9], a[11] - a[13], a[15] - a[17]
    m0 = 12.0 * g[0] + (tx + ty + tz) + (exy + exz + eyz)
    qx = mxx * ux + mxy * uy + mxz * uz
    qy = mxy * ux + myy * uy + myz * uz
    qz = mxz * ux + myz * uy + mzz * uz
    square = ux * ux + uy * uy + uz * uz
    scaled = flow_omega / 36.0
    zero = m0 * (scaled + (1.5 * scaled) * square) - (4.5 * scaled) * (qx * ux + qy * uy + qz * uz)
    zero = valid * (zero - (fx * ux + fy * uy + fz * uz))
    bx = valid * ((3.0 * scaled) * (m1x + 3.0 * qx - m0 * ux) + fx)
    by = valid * ((3.0 * scaled) * (m1y + 3.0 * qy - m0 * uy) + fy)
    bz = valid * ((3.0 * scaled) * (m1z + 3.0 * qz - m0 * uz) + fz)
    keep = (1.0 - flow_omega) * valid
    write(0, keep * g[0] + zero)
    moves = {1: bx, 3: by, 5: bz, 7: bx + by, 9: bx - by, 11: bx + bz, 13: bx - bz, 15: by + bz, 17: by - bz}
    for i, move in moves.items():
        write(i, keep * g[i] + (zero + move))
        write(i + 1, keep * g[i + 1] + (zero - move))


VMEM = pl.BlockSpec(memory_space=pltpu.VMEM)
SMEM = pl.BlockSpec(memory_space=pltpu.SMEM)
ANY = pl.BlockSpec(memory_space=pl.ANY)
HBM = pl.BlockSpec(memory_space=pltpu.HBM)


def call(kernel, ins, outs, name, cost, scratch=(), limit=VMEM_LIMIT, place=VMEM, aliases={}):
    return pl.pallas_call(
        kernel,
        in_specs=ins,
        out_shape=outs,
        out_specs=[place] * len(outs),
        input_output_aliases=aliases,
        scratch_shapes=list(scratch),
        name=name,
        cost_estimate=pl.CostEstimate(flops=cost, bytes_accessed=1 << 23, transcendentals=0),
        compiler_params=pltpu.CompilerParams(vmem_limit_bytes=limit),
    )


def per_device(flow_adjoint, solute_adjoint, flow_density, flow_velocity, solute_level, solid, owner):
    steps = flow_density.shape[0]
    nx, ny, depth = solid.shape
    plan = Plan(steps, nx, ny, depth)
    ring = lax.axis_size("gz")
    w = plan.halo
    arguments = (flow_adjoint, solute_adjoint, flow_density, flow_velocity, solute_level, solid)
    fields = [f.reshape(-1, nx * ny, depth) for f in arguments]
    owner, *fields = (pltpu.with_memory_space_constraint(f, pltpu.HBM) for f in (owner, *fields))

    def move(value, axis, by):
        size = lax.axis_size(axis)
        return lax.ppermute(value, axis, [(i, i + by) for i in range(size) if 0 <= i + by < size])

    parts = 1 if ring == 2 else 2

    def like(channels):
        return jax.ShapeDtypeStruct((channels, nx * ny, depth), F32)

    *packed, flow, solute, wide = call(
        functools.partial(pack_kernel, plan, ring, parts),
        [SMEM] + [HBM] * 6,
        [jax.ShapeDtypeStruct((plan.sent, 8, depth), F32)] * parts + [like(NF), like(NS), like(plan.chan - SOLID)],
        "pack_column",
        1 << 22,
        [pltpu.VMEM(f.shape, f.dtype) for f in fields[2:]] + [pltpu.SemaphoreType.DMA((8,))],
    )(owner, *fields)
    loaded = (flow, solute, wide)
    if ring == 2:
        received = [lax.ppermute(packed[0], "gz", [(0, 1), (1, 0)])]
    else:
        received = [move(packed[0], "gz", 1), move(packed[1], "gz", -1)]

    slab = [jax.ShapeDtypeStruct((plan.slab, nx, depth), F32)] * 2
    raw = call(functools.partial(faces_kernel, plan), [VMEM] * 3 + [ANY], slab, "faces", 1 << 24)(
        *loaded, packed[0]
    )
    y_low, y_high = call(
        functools.partial(insert_kernel, plan, ring, parts), [SMEM] + [VMEM] * (2 + parts), slab, "insert", 1 << 22, (), 24 << 20
    )(owner, *raw, *received)
    from_y_low = move(y_high, "gy", 1)
    from_y_high = move(y_low, "gy", -1)
    state = jax.ShapeDtypeStruct((SOLID, plan.height, depth), F32)
    saved = jax.ShapeDtypeStruct((plan.chan - SOLID, plan.height, depth), F32)
    flags = jax.ShapeDtypeStruct((3, plan.height, depth), F32)
    cells, kept, x_low, x_high = call(
        functools.partial(inner_kernel, plan, ring, parts),
        [SMEM] + [VMEM] * (3 + parts),
        [state, saved] + [jax.ShapeDtypeStruct((plan.slab, ny, depth), F32)] * 2,
        "inner",
        1 << 24,
    )(owner, *loaded, *received)
    from_x_low = move(x_high, "gx", 1)
    from_x_high = move(x_low, "gx", -1)
    other, masks = call(
        functools.partial(middle_kernel, plan), [SMEM] + [VMEM] * 2, [state, flags], "middle", 1 << 24, (), 8 << 20
    )(owner, cells, kept)

    def rows(value):
        return value.reshape(-1, depth)

    corner = jax.ShapeDtypeStruct((plan.slab * 2 * w, depth), F32)
    c_low, c_high = call(
        functools.partial(corners_kernel, plan), [VMEM] * 2 + [ANY], [corner, corner], "corners", 1 << 20
    )(rows(from_y_low), rows(from_y_high), masks)
    shape = (plan.slab, 2 * w, depth)
    from_c_low = move(c_high, "gx", 1).reshape(shape)
    from_c_high = move(c_low, "gx", -1).reshape(shape)
    assembled = [pltpu.with_memory_space_constraint(a, pltpu.VMEM) for a in (cells, kept, other, masks)]
    assembled = call(
        functools.partial(first_kernel, plan),
        [SMEM] + [VMEM] * 8,
        [state, saved, state, flags],
        "first",
        1 << 26,
        (),
        8 << 20,
        aliases={5: 0, 6: 1, 7: 2, 8: 3},
    )(owner, from_y_low, from_y_high, from_x_low, from_x_high, *assembled)
    flow, solute = call(
        functools.partial(steps_kernel, plan),
        [SMEM] + [VMEM] * 6,
        [jax.ShapeDtypeStruct(flow_adjoint.shape, F32), jax.ShapeDtypeStruct(solute_adjoint.shape, F32)],
        "steps",
        1 << 28,
        [
            pltpu.VMEM((NF, nx, ny, depth), F32),
            pltpu.VMEM((NS, nx, ny, depth), F32),
            pltpu.SemaphoreType.DMA((2, nx)),
        ],
        10 << 20,
        ANY,
    )(owner, *assembled, from_c_low, from_c_high)
    return (flow, solute)


def solution(mesh):
    in_specs = (
        P(None, "gx", "gy", "gz"),
        P(None, "gx", "gy", "gz"),
        P(None, "gx", "gy", "gz"),
        P(None, None, "gx", "gy", "gz"),
        P(None, "gx", "gy", "gz"),
        P("gx", "gy", "gz"),
        P(),
    )
    out_specs = (P(None, "gx", "gy", "gz"), P(None, "gx", "gy", "gz"))
    return jax.shard_map(
        per_device, mesh=mesh, in_specs=in_specs, out_specs=out_specs, check_vma=False
    )
```

```python
import functools

import jax
import jax.numpy as jnp
from jax import lax
from jax.experimental import pallas as pl
from jax.experimental.pallas import tpu as pltpu
from jax.sharding import PartitionSpec as P

BZC = 16

FLOW_DIRS = [
    (0, 0, 0),
    (1, 0, 0),
    (-1, 0, 0),
    (0, 1, 0),
    (0, -1, 0),
    (0, 0, 1),
    (0, 0, -1),
    (1, 1, 0),
    (-1, -1, 0),
    (1, -1, 0),
    (-1, 1, 0),
    (1, 0, 1),
    (-1, 0, -1),
    (1, 0, -1),
    (-1, 0, 1),
    (0, 1, 1),
    (0, -1, -1),
    (0, 1, -1),
    (0, -1, 1),
]
NF = 19
NS = 7
OPPOSITE = [FLOW_DIRS.index((-a, -b, -c)) for a, b, c in FLOW_DIRS]
SOLID = NF + NS
AUX = SOLID + 1
NA = 5
flow_omega = 1.25
solute_omega = 1.6
langmuir_rate = 0.05
VMEM_LIMIT = 24 << 20
F32 = jnp.float32
PAD = 8


class Plan:
    def __init__(self, steps, nx, ny, depth):
        self.steps, self.nx, self.ny, self.depth = steps, nx, ny, depth
        self.halo = w = steps
        self.chan = AUX + NA * steps
        self.sent = AUX + NA * (steps - 1)
        self.pitch = -(-(ny + 2 * w) // 8) * 8
        self.wide = nx + 2 * w
        self.height = self.wide * self.pitch + 2 * PAD
        self.tiles = list(range(self.pitch // 8))
        self.inside = [h for h in self.tiles if 8 * h > w and 8 * h + 8 < w + ny]
        self.outside = [h for h in self.tiles if h not in self.inside]
        self.count = {k: AUX + NA * (steps - k) for k in range(1, w)}
        self.base, at = {}, 0
        for k in range(1, w):
            self.base[k] = at
            at += self.count[k]
        self.base[w] = at
        self.slab = at + 7

    def last(self, axis, sign):
        flow = [i for i, c in enumerate(FLOW_DIRS) if c[axis] == sign]
        solute = [NF + i for i, c in enumerate(FLOW_DIRS[:NS]) if c[axis] == sign]
        return flow + solute + [SOLID]


def lanes(depth):
    return lax.broadcasted_iota(jnp.int32, (8, depth), 1)


def occupied(owner_ref):
    me = lax.axis_index("gz")
    count = jnp.int32(0)
    for j in range(owner_ref.shape[0]):
        count = count + jnp.where(owner_ref[j] == me, 1, 0).astype(jnp.int32)
    return count * BZC


def z_places(plan, length, ring):
    w, depth = plan.halo, plan.depth
    if ring == 2:
        first = lax.axis_index("gz") == 0
        return [(jnp.where(first, length - w, 0), jnp.where(first, length, depth - w))]
    return [(length - w, jnp.int32(depth - w)), (jnp.int32(0), length)]


def each(number, body, unroll=4):
    def several(i, carry):
        for u in range(unroll):
            body(i * unroll + u)
        return carry

    turns = number // unroll
    if turns > 1:
        lax.fori_loop(0, turns, several, 0)
    else:
        turns = 0
    for i in range(turns * unroll, number):
        body(i)


def tiles_of(plan):
    return [(y * (plan.nx // 8) + h, y, 8 * h) for y in range(plan.ny) for h in range(plan.nx // 8)]


def pack_kernel(plan, ring, parts, owner, flow, solute, density, velocity, level, solid, *refs):
    outs, (flow_out, solute_out, wide), (density_in, velocity_in, level_in, solid_in, sems) = (
        refs[:parts],
        refs[parts : parts + 3],
        refs[parts + 3 :],
    )
    w, depth, nx, ny = plan.halo, plan.depth, plan.nx, plan.ny
    cuts = [0, 7, 13, NF]
    flows = [pl.ds(a, b - a) for a, b in zip(cuts, cuts[1:])]
    pairs = [(flow.at[cut], flow_out.at[cut]) for cut in flows] + [
        (solute, solute_out),
        (solid, solid_in),
        (density, density_in),
        (level, level_in),
        (velocity, velocity_in),
    ]
    copies = [pltpu.make_async_copy(a, b, sems.at[i]) for i, (a, b) in enumerate(pairs)]
    for copy in copies:
        copy.start()

    length = occupied(owner)
    group = lanes(depth) // w
    places = z_places(plan, length, ring)
    shifts = [{n: (w * n + depth - start) & (depth - 1) for n, _, _ in tiles_of(plan)} for start, _ in places]

    def pack(at, first, number, ref):
        def one(i):
            packed = [None] * parts
            for n, y, x in tiles_of(plan):
                tile = ref[first + i, pl.ds(x * ny + y, 8, stride=ny), :]
                for p in range(parts):
                    moved = pltpu.roll(tile, shifts[p][n], 1)
                    packed[p] = moved if n == 0 else jnp.where(group == n, moved, packed[p])
            for p in range(parts):
                outs[p][at + first + i] = packed[p]

        each(number, one, 6)

    for copy, a, b in zip(copies, cuts, cuts[1:]):
        copy.wait()
        pack(0, a, b - a, flow_out)
    for copy in copies[3:]:
        copy.wait()
    pack(NF, 0, NS, solute_out)
    sources = [(solid_in, 0)]
    for s in range(plan.steps):
        t = plan.steps - 1 - s
        sources += [(density_in, t), (level_in, t)] + [(velocity_in, 3 * t + i) for i in range(3)]
    for c, (ref, i) in enumerate(sources):
        for x in range(nx):
            wide[c, x * ny : (x + 1) * ny, :] = ref[i, x * ny : (x + 1) * ny, :].astype(F32)
    pack(SOLID, 0, plan.sent - SOLID, wide)


def faces_kernel(plan, flow, solute, wide, packed, y_low, y_high):
    w, nx, ny = plan.halo, plan.nx, plan.ny
    for at, number, ref in ((0, NF, flow), (NF, NS, solute), (SOLID, plan.sent - SOLID, wide)):

        def row(c, y, ref=ref):
            return ref[c, pl.ds(y, nx, stride=ny), :]

        for k in range(1, w):

            def one(c, k=k, at=at, row=row):
                y_low[plan.base[k] + at + c] = row(c, k - 1)
                y_high[plan.base[k] + at + c] = row(c, ny - k)

            each(min(number, plan.count[k] - at), one)
        for out, sign, y in ((y_low, 1, w - 1), (y_high, -1, ny - w)):
            for j, c in enumerate(plan.last(1, sign)):
                if at <= c < at + number:
                    out[plan.base[w] + j] = row(c - at, y)


def column(plan, ring, owner, received):
    w, depth = plan.halo, plan.depth
    length = occupied(owner)
    lane = lanes(depth)
    live = lane < length
    places = [to for _, to in z_places(plan, length, ring)]
    halos = [((lane - to) & (depth - 1)) < w for to in places]
    shifts = [{n: (to + depth - w * n) & (depth - 1) for n, _, _ in tiles_of(plan)} for to in places]

    def put(tile, slabs, n):
        tile = jnp.where(live, tile, 0.0)
        for slab, halo, shift in zip(slabs, halos, shifts):
            tile = jnp.where(halo, pltpu.roll(slab, shift[n], 1), tile)
        return tile

    return put


def insert_kernel(plan, ring, parts, owner, low, high, *rest):
    received, (y_low, y_high) = rest[:parts], rest[parts:]
    put = column(plan, ring, owner, received)
    w, ny = plan.halo, plan.ny
    tall = plan.nx // 8

    def one(raw, out, j, c, y):
        slabs = [r[c] for r in received]
        for h in range(tall):
            out[j, 8 * h : 8 * h + 8, :] = put(raw[j, 8 * h : 8 * h + 8, :], slabs, y * tall + h)

    for k in range(1, w):

        def both(c, k=k):
            one(low, y_low, plan.base[k] + c, c, k - 1)
            one(high, y_high, plan.base[k] + c, c, ny - k)

        each(plan.count[k], both, 10)
    for raw, out, sign, y in ((low, y_low, 1, w - 1), (high, y_high, -1, ny - w)):
        for j, c in enumerate(plan.last(1, sign)):
            one(raw, out, plan.base[w] + j, c, y)


def inner_kernel(plan, ring, parts, owner, flow, solute, wide, *rest):
    received, (cells, fields, x_low, x_high) = rest[:parts], rest[parts:]
    w, nx, ny, pitch = plan.halo, plan.nx, plan.ny, plan.pitch
    put = column(plan, ring, owner, received)
    for at, number, ref, out, to in (
        (0, NF, flow, cells, 0),
        (NF, NS, solute, cells, NF),
        (SOLID, plan.chan - SOLID, wide, fields, 0),
    ):

        def one(i, sent=True, at=at, ref=ref, out=out, to=to):
            slabs = [r[at + i] for r in received] if sent else []
            for n, y, x in tiles_of(plan):
                tile = ref[i, pl.ds(x * ny + y, 8, stride=ny), :]
                out[to + i, pl.ds(PAD + (w + x) * pitch + w + y, 8, stride=pitch), :] = put(tile, slabs, n)

        within = min(number, plan.sent - at)
        each(within, one, 3)
        each(number - within, lambda i, one=one, within=within: one(within + i, False), 1)

    def row(ref, c, x):
        at = PAD + (w + x) * pitch + w
        return ref[c, at : at + ny, :]

    for k in range(1, w):

        def both(ref, c, j, k=k):
            x_low[plan.base[k] + j] = row(ref, c, k - 1)
            x_high[plan.base[k] + j] = row(ref, c, nx - k)

        channels(cells, fields, plan.count[k], both)
    for slab, sign, x in ((x_low, 1, w - 1), (x_high, -1, nx - w)):
        for j, c in enumerate(plan.last(0, sign)):
            ref, at = (cells, c) if c < SOLID else (fields, c - SOLID)
            slab[plan.base[w] + j] = row(ref, at, x)


def middle_kernel(plan, owner, cells, fields, other, masks):
    w, nx = plan.halo, plan.nx
    prepare(plan, owner, fields, masks, w, w + nx)
    sweep(plan, owner, cells, other, fields, masks, 0, w + 1, w + nx - 1, plan.inside)


def corners_kernel(plan, from_low, from_high, masks, low, high):
    w, nx, ny = plan.halo, plan.nx, plan.ny
    low[...] = jnp.zeros(low.shape, F32)
    high[...] = jnp.zeros(high.shape, F32)
    tall = 2 * w
    for out, sign in ((low, 1), (high, -1)):
        x_last = plan.last(0, sign)
        for k in range(1, w + 1):
            x = k - 1 if sign == 1 else nx - k
            for m in range(1, w + 1):
                for source, row, y_sign in ((from_low, w - m, -1), (from_high, w - 1 + m, 1)):
                    y_last = plan.last(1, y_sign)
                    if k < w and m < w:
                        number = min(plan.count[k], plan.count[m])
                        out[pl.ds(plan.base[k] * tall + row, number, stride=tall), :] = source[
                            pl.ds(plan.base[m] * nx + x, number, stride=nx), :
                        ]
                        continue
                    for c in range(AUX):
                        if (k == w and c not in x_last) or (m == w and c not in y_last):
                            continue
                        to = plan.base[k] + (x_last.index(c) if k == w else c)
                        at = plan.base[m] + (y_last.index(c) if m == w else c)
                        out[to * tall + row : to * tall + row + 1, :] = source[at * nx + x : at * nx + x + 1, :]


def channels(cells, fields, number, body):
    each(SOLID, lambda c: body(cells, c, c))
    each(number - SOLID, lambda c: body(fields, c, SOLID + c))


def insert_layers(plan, cells, fields, axis, parts, put):
    w = plan.halo
    for k in range(1, w + 1):
        for part, sign in zip(parts, (-1, 1)):
            if k < w:
                channels(
                    cells,
                    fields,
                    plan.count[k],
                    lambda ref, c, j, k=k, part=part, sign=sign: put(ref, c, part, plan.base[k] + j, k, sign),
                )
                continue
            for j, c in enumerate(plan.last(axis, sign)):
                ref, at = (cells, c) if c < SOLID else (fields, c - SOLID)
                put(ref, at, part, plan.base[w] + j, k, sign)


def first_kernel(plan, owner, y_low, y_high, x_low, x_high, *refs):
    cells, fields, other, masks = refs[4:]
    w, nx, ny, pitch = plan.halo, plan.nx, plan.ny, plan.pitch

    def put_x(ref, c, part, j, k, sign):
        row = PAD + (w - k if sign < 0 else w + nx - 1 + k) * pitch + w
        ref[c, row : row + ny, :] = part[j]

    insert_layers(plan, cells, fields, 0, (x_low, x_high), put_x)

    def put_y(ref, c, part, j, m, sign):
        row = PAD + w * pitch + (w - m if sign < 0 else w + ny - 1 + m)
        ref[c, pl.ds(row, nx, stride=pitch), :] = part[j]

    insert_layers(plan, cells, fields, 1, (y_low, y_high), put_y)
    prepare(plan, owner, fields, masks, w, w + nx, plan.outside)
    prepare(plan, owner, fields, masks, 0, w)
    prepare(plan, owner, fields, masks, w + nx, plan.wide)
    edges(plan, owner, cells, other, fields, masks, 0, plan.inside)
    sweep(plan, owner, cells, other, fields, masks, 0, w + 1, w + nx - 1, plan.outside)
    buffers = [cells, other]
    for s in range(1, plan.steps - 1):
        sweep(plan, owner, buffers[s % 2], buffers[(s + 1) % 2], fields, masks, s, w + 1 + s, w + nx - 1 - s)


def steps_kernel(plan, owner, cells, fields, other, masks, c_low, c_high, flow_hbm, solute_hbm, flow_out, solute_out, sems):
    w, nx, ny, pitch = plan.halo, plan.nx, plan.ny, plan.pitch

    def put(ref, c, part, j, k, sign):
        row = PAD + (w - k if sign < 0 else w + nx - 1 + k) * pitch
        ref[c, row : row + w, :] = part[j, 0:w, :]
        ref[c, row + w + ny : row + w + ny + w, :] = part[j, w : 2 * w, :]

    insert_layers(plan, cells, fields, 0, (c_low, c_high), put)
    prepare(plan, owner, fields, masks, 0, w, plan.outside)
    prepare(plan, owner, fields, masks, w + nx, plan.wide, plan.outside)
    buffers = [cells, other]
    for s in range(plan.steps - 1):
        source, target = buffers[s % 2], buffers[(s + 1) % 2]
        edges(plan, owner, source, target, fields, masks, s, plan.outside if s == 0 else None)
    s = plan.steps - 1
    source = buffers[s % 2]

    def leave(x):
        return [
            pltpu.make_async_copy(ref.at[:, x], to.at[:, x], sems.at[n, x])
            for n, (ref, to) in enumerate(((flow_out, flow_hbm), (solute_out, solute_hbm)))
        ]

    def last(x):
        for h in range(ny // 8):
            row = PAD + (x + w) * pitch + w + 8 * h

            def write(c, value, h=h):
                if c < NF:
                    flow_out[c, x, 8 * h : 8 * h + 8, :] = value
                else:
                    solute_out[c - NF, x, 8 * h : 8 * h + 8, :] = value

            advance(plan, owner, source, fields, masks, s, row, write)
        for copy in leave(x):
            copy.start()

    each(nx, last, 2)
    for x in range(nx):
        for copy in leave(x):
            copy.wait()


def prepare(plan, owner, fields, masks, from_x, to_x, tiles=None):
    w, nx, ny, depth, pitch = plan.halo, plan.nx, plan.ny, plan.depth, plan.pitch
    length = occupied(owner)
    lane = lanes(depth)
    gx, gy, gz = (lax.axis_index(a) for a in ("gx", "gy", "gz"))
    last_x, last_y, last_z = (lax.axis_size(a) - 1 for a in ("gx", "gy", "gz"))
    above = jnp.where(gz < last_z, w, 0)
    below = jnp.where(gz > 0, w, 0)
    in_z = (lane < length + above) | (lane >= depth - below)
    y_first = jnp.where(gy > 0, 0, w)
    y_end = jnp.where(gy < last_y, ny + 2 * w, w + ny)
    x_first = jnp.where(gx > 0, 0, w)
    x_end = jnp.where(gx < last_x, nx + 2 * w, w + nx)
    sub = lax.broadcasted_iota(jnp.int32, (8, depth), 0)

    def one(i):
        x = from_x + i
        in_x = ((x >= x_first) & (x < x_end)).astype(F32)
        for h in tiles or plan.tiles:
            row = pl.multiple_of(PAD + x * pitch + 8 * h, 8)
            flags = fields[0, pl.ds(row, 8), :]
            y = sub + 8 * h
            masks[0, pl.ds(row, 8), :] = pltpu.roll(flags, depth - 1, 1)
            masks[1, pl.ds(row, 8), :] = pltpu.roll(flags, 1, 1)
            inside = in_z & (y >= y_first) & (y < y_end) & (flags == 0.0)
            masks[2, pl.ds(row, 8), :] = jnp.where(inside, in_x, 0.0)

    each(to_x - from_x, one)


def edges(plan, owner, source, target, fields, masks, s, tiles=None):
    sweep(plan, owner, source, target, fields, masks, s, 1 + s, plan.halo + 1 + s, tiles, plan.nx + plan.halo - 2 * s - 2)


def sweep(plan, owner, source, target, fields, masks, s, from_x, to_x, tiles=None, partner=None):
    pitch = plan.pitch

    def body(i):
        rows = [from_x + i] if partner is None else [from_x + i, from_x + i + partner]
        for x, h in [(x, h) for x in rows for h in tiles or plan.tiles]:
            row = pl.multiple_of(PAD + pitch * x + 8 * h, 8)

            def write(c, value, row=row):
                target[c, pl.ds(row, 8), :] = value

            advance(plan, owner, source, fields, masks, s, row, write)

    each(to_x - from_x, body, 2 if partner is None else 1)


def advance(plan, owner, source, fields, masks, s, row, write):
    depth, pitch = plan.depth, plan.pitch
    def field(ref, c, move=0):
        return ref[c, pl.ds(row + move, 8), :]

    blocked = {}

    def reads(first, number):
        result = []
        for i in range(number):
            sx, sy, sz = FLOW_DIRS[i]
            if i == 0:
                result.append(field(source, first))
                continue
            move = sx * pitch + sy
            near = field(source, first + i, move)
            if sz:
                near = pltpu.roll(near, (depth - sz) % depth, 1)
            if i not in blocked:
                flags = field(fields, 0, move) if sz == 0 else field(masks, 0 if sz == 1 else 1, move)
                blocked[i] = flags != 0.0
            result.append(jnp.where(blocked[i], field(source, first + OPPOSITE[i]), near))
        return result

    valid = field(masks, 2)
    if s == plan.steps - 1:
        valid = jnp.where(lanes(depth) < occupied(owner), valid, 0.0)
    aux = AUX - SOLID + NA * s
    density, level, ux, uy, uz = (field(fields, aux + n) for n in range(NA))

    h = reads(NF, NS)
    px, py, pz = h[1] - h[2], h[3] - h[4], h[5] - h[6]
    p0 = 0.25 * h[0] + 0.125 * ((h[1] + h[2]) + (h[3] + h[4]) + (h[5] + h[6]))
    grown = (1.0 + level) * (1.0 + level)
    density = jnp.maximum(density, 0.5)
    inverse = 1.0 / (grown * density)
    uptake = langmuir_rate * (density * inverse)
    common = valid * (
        (solute_omega - uptake) * p0 + (solute_omega * 0.5) * (px * ux + py * uy + pz * uz)
    )
    keep = (1.0 - solute_omega) * valid
    for i in range(NS):
        write(NF + i, keep * h[i] + common)
    factor = (0.5 * solute_omega) * level * (grown * inverse)
    fx, fy, fz = factor * px, factor * py, factor * pz

    g = reads(0, NF)
    a = {i: g[i] + g[i + 1] for i in range(1, NF, 2)}
    d = {i: g[i] - g[i + 1] for i in range(1, NF, 2)}
    m1x = (d[1] + d[1]) + (d[7] + d[9]) + (d[11] + d[13])
    m1y = (d[3] + d[3]) + (d[7] - d[9]) + (d[15] + d[17])
    m1z = (d[5] + d[5]) + (d[11] - d[13]) + (d[15] - d[17])
    exy, exz, eyz = a[7] + a[9], a[11] + a[13], a[15] + a[17]
    tx, ty, tz = a[1] + a[1], a[3] + a[3], a[5] + a[5]
    mxx, myy, mzz = tx + exy + exz, ty + exy + eyz, tz + exz + eyz
    mxy, mxz, myz = a[7] - a[9], a[11] - a[13], a[15] - a[17]
    m0 = 12.0 * g[0] + (tx + ty + tz) + (exy + exz + eyz)
    qx = mxx * ux + mxy * uy + mxz * uz
    qy = mxy * ux + myy * uy + myz * uz
    qz = mxz * ux + myz * uy + mzz * uz
    square = ux * ux + uy * uy + uz * uz
    scaled = flow_omega / 36.0
    zero = m0 * (scaled + (1.5 * scaled) * square) - (4.5 * scaled) * (qx * ux + qy * uy + qz * uz)
    zero = valid * (zero - (fx * ux + fy * uy + fz * uz))
    bx = valid * ((3.0 * scaled) * (m1x + 3.0 * qx - m0 * ux) + fx)
    by = valid * ((3.0 * scaled) * (m1y + 3.0 * qy - m0 * uy) + fy)
    bz = valid * ((3.0 * scaled) * (m1z + 3.0 * qz - m0 * uz) + fz)
    keep = (1.0 - flow_omega) * valid
    write(0, keep * g[0] + zero)
    moves = {1: bx, 3: by, 5: bz, 7: bx + by, 9: bx - by, 11: bx + bz, 13: bx - bz, 15: by + bz, 17: by - bz}
    for i, move in moves.items():
        write(i, keep * g[i] + (zero + move))
        write(i + 1, keep * g[i + 1] + (zero - move))


VMEM = pl.BlockSpec(memory_space=pltpu.VMEM)
SMEM = pl.BlockSpec(memory_space=pltpu.SMEM)
ANY = pl.BlockSpec(memory_space=pl.ANY)
HBM = pl.BlockSpec(memory_space=pltpu.HBM)


def call(kernel, ins, outs, name, cost, scratch=(), limit=VMEM_LIMIT, place=VMEM, aliases={}):
    return pl.pallas_call(
        kernel,
        in_specs=ins,
        out_shape=outs,
        out_specs=[place] * len(outs),
        input_output_aliases=aliases,
        scratch_shapes=list(scratch),
        name=name,
        cost_estimate=pl.CostEstimate(flops=cost, bytes_accessed=1 << 23, transcendentals=0),
        compiler_params=pltpu.CompilerParams(vmem_limit_bytes=limit),
    )


def per_device(flow_adjoint, solute_adjoint, flow_density, flow_velocity, solute_level, solid, owner):
    steps = flow_density.shape[0]
    nx, ny, depth = solid.shape
    plan = Plan(steps, nx, ny, depth)
    ring = lax.axis_size("gz")
    w = plan.halo
    arguments = (flow_adjoint, solute_adjoint, flow_density, flow_velocity, solute_level, solid)
    fields = [f.reshape(-1, nx * ny, depth) for f in arguments]
    owner, *fields = (pltpu.with_memory_space_constraint(f, pltpu.HBM) for f in (owner, *fields))

    def move(value, axis, by):
        size = lax.axis_size(axis)
        return lax.ppermute(value, axis, [(i, i + by) for i in range(size) if 0 <= i + by < size])

    parts = 1 if ring == 2 else 2

    def like(channels):
        return jax.ShapeDtypeStruct((channels, nx * ny, depth), F32)

    *packed, flow, solute, wide = call(
        functools.partial(pack_kernel, plan, ring, parts),
        [SMEM] + [HBM] * 6,
        [jax.ShapeDtypeStruct((plan.sent, 8, depth), F32)] * parts + [like(NF), like(NS), like(plan.chan - SOLID)],
        "pack_column",
        1 << 22,
        [pltpu.VMEM(f.shape, f.dtype) for f in fields[2:]] + [pltpu.SemaphoreType.DMA((8,))],
    )(owner, *fields)
    loaded = (flow, solute, wide)
    if ring == 2:
        received = [lax.ppermute(packed[0], "gz", [(0, 1), (1, 0)])]
    else:
        received = [move(packed[0], "gz", 1), move(packed[1], "gz", -1)]

    slab = [jax.ShapeDtypeStruct((plan.slab, nx, depth), F32)] * 2
    raw = call(functools.partial(faces_kernel, plan), [VMEM] * 3 + [ANY], slab, "faces", 1 << 24)(
        *loaded, packed[0]
    )
    y_low, y_high = call(
        functools.partial(insert_kernel, plan, ring, parts), [SMEM] + [VMEM] * (2 + parts), slab, "insert", 1 << 22, (), 24 << 20
    )(owner, *raw, *received)
    from_y_low = move(y_high, "gy", 1)
    from_y_high = move(y_low, "gy", -1)
    state = jax.ShapeDtypeStruct((SOLID, plan.height, depth), F32)
    saved = jax.ShapeDtypeStruct((plan.chan - SOLID, plan.height, depth), F32)
    flags = jax.ShapeDtypeStruct((3, plan.height, depth), F32)
    cells, kept, x_low, x_high = call(
        functools.partial(inner_kernel, plan, ring, parts),
        [SMEM] + [VMEM] * (3 + parts),
        [state, saved] + [jax.ShapeDtypeStruct((plan.slab, ny, depth), F32)] * 2,
        "inner",
        1 << 24,
    )(owner, *loaded, *received)
    from_x_low = move(x_high, "gx", 1)
    from_x_high = move(x_low, "gx", -1)
    other, masks = call(
        functools.partial(middle_kernel, plan), [SMEM] + [VMEM] * 2, [state, flags], "middle", 1 << 24, (), 8 << 20
    )(owner, cells, kept)

    def rows(value):
        return value.reshape(-1, depth)

    corner = jax.ShapeDtypeStruct((plan.slab * 2 * w, depth), F32)
    c_low, c_high = call(
        functools.partial(corners_kernel, plan), [VMEM] * 2 + [ANY], [corner, corner], "corners", 1 << 20
    )(rows(from_y_low), rows(from_y_high), masks)
    shape = (plan.slab, 2 * w, depth)
    from_c_low = move(c_high, "gx", 1).reshape(shape)
    from_c_high = move(c_low, "gx", -1).reshape(shape)
    assembled = [pltpu.with_memory_space_constraint(a, pltpu.VMEM) for a in (cells, kept, other, masks)]
    assembled = call(
        functools.partial(first_kernel, plan),
        [SMEM] + [VMEM] * 8,
        [state, saved, state, flags],
        "first",
        1 << 26,
        (),
        8 << 20,
        aliases={5: 0, 6: 1, 7: 2, 8: 3},
    )(owner, from_y_low, from_y_high, from_x_low, from_x_high, *assembled)
    flow, solute = call(
        functools.partial(steps_kernel, plan),
        [SMEM] + [VMEM] * 6,
        [jax.ShapeDtypeStruct(flow_adjoint.shape, F32), jax.ShapeDtypeStruct(solute_adjoint.shape, F32)],
        "steps",
        1 << 28,
        [
            pltpu.VMEM((NF, nx, ny, depth), F32),
            pltpu.VMEM((NS, nx, ny, depth), F32),
            pltpu.SemaphoreType.DMA((2, nx)),
        ],
        10 << 20,
        ANY,
    )(owner, *assembled, from_c_low, from_c_high)
    return (flow, solute)


def solution(mesh):
    in_specs = (
        P(None, "gx", "gy", "gz"),
        P(None, "gx", "gy", "gz"),
        P(None, "gx", "gy", "gz"),
        P(None, None, "gx", "gy", "gz"),
        P(None, "gx", "gy", "gz"),
        P("gx", "gy", "gz"),
        P(),
    )
    out_specs = (P(None, "gx", "gy", "gz"), P(None, "gx", "gy", "gz"))
    return jax.shard_map(
        per_device, mesh=mesh, in_specs=in_specs, out_specs=out_specs, check_vma=False
    )
```

```python
import functools

import jax
import jax.numpy as jnp
from jax import lax
from jax.experimental import pallas as pl
from jax.experimental.pallas import tpu as pltpu
from jax.sharding import PartitionSpec as P

BZC = 16

FLOW_DIRS = [
    (0, 0, 0),
    (1, 0, 0),
    (-1, 0, 0),
    (0, 1, 0),
    (0, -1, 0),
    (0, 0, 1),
    (0, 0, -1),
    (1, 1, 0),
    (-1, -1, 0),
    (1, -1, 0),
    (-1, 1, 0),
    (1, 0, 1),
    (-1, 0, -1),
    (1, 0, -1),
    (-1, 0, 1),
    (0, 1, 1),
    (0, -1, -1),
    (0, 1, -1),
    (0, -1, 1),
]
NF = 19
NS = 7
OPPOSITE = [FLOW_DIRS.index((-a, -b, -c)) for a, b, c in FLOW_DIRS]
SOLID = NF + NS
AUX = SOLID + 1
NA = 5
flow_omega = 1.25
solute_omega = 1.6
langmuir_rate = 0.05
VMEM_LIMIT = 24 << 20
F32 = jnp.float32
PAD = 8


class Plan:
    def __init__(self, steps, nx, ny, depth):
        self.steps, self.nx, self.ny, self.depth = steps, nx, ny, depth
        self.halo = w = steps
        self.chan = AUX + NA * steps
        self.sent = AUX + NA * (steps - 1)
        self.pitch = -(-(ny + 2 * w) // 8) * 8
        self.wide = nx + 2 * w
        self.height = self.wide * self.pitch + 2 * PAD
        self.tiles = list(range(self.pitch // 8))
        self.inside = [h for h in self.tiles if 8 * h > w and 8 * h + 8 < w + ny]
        self.outside = [h for h in self.tiles if h not in self.inside]
        self.count = {k: AUX + NA * (steps - k) for k in range(1, w)}
        self.base, at = {}, 0
        for k in range(1, w):
            self.base[k] = at
            at += self.count[k]
        self.base[w] = at
        self.slab = at + 7

    def last(self, axis, sign):
        flow = [i for i, c in enumerate(FLOW_DIRS) if c[axis] == sign]
        solute = [NF + i for i, c in enumerate(FLOW_DIRS[:NS]) if c[axis] == sign]
        return flow + solute + [SOLID]


def lanes(depth):
    return lax.broadcasted_iota(jnp.int32, (8, depth), 1)


def occupied(owner_ref):
    me = lax.axis_index("gz")
    count = jnp.int32(0)
    for j in range(owner_ref.shape[0]):
        count = count + jnp.where(owner_ref[j] == me, 1, 0).astype(jnp.int32)
    return count * BZC


def z_places(plan, length, ring):
    w, depth = plan.halo, plan.depth
    if ring == 2:
        first = lax.axis_index("gz") == 0
        return [(jnp.where(first, length - w, 0), jnp.where(first, length, depth - w))]
    return [(length - w, jnp.int32(depth - w)), (jnp.int32(0), length)]


def each(number, body, unroll=4):
    def several(i, carry):
        for u in range(unroll):
            body(i * unroll + u)
        return carry

    turns = number // unroll
    if turns > 1:
        lax.fori_loop(0, turns, several, 0)
    else:
        turns = 0
    for i in range(turns * unroll, number):
        body(i)


def tiles_of(plan):
    return [(y * (plan.nx // 8) + h, y, 8 * h) for y in range(plan.ny) for h in range(plan.nx // 8)]


def pack_kernel(plan, ring, parts, owner, flow, solute, density, velocity, level, solid, *refs):
    outs, (flow_out, solute_out, wide), (density_in, velocity_in, level_in, solid_in, sems) = (
        refs[:parts],
        refs[parts : parts + 3],
        refs[parts + 3 :],
    )
    w, depth, nx, ny = plan.halo, plan.depth, plan.nx, plan.ny
    cuts = [0, 7, 13, NF]
    flows = [pl.ds(a, b - a) for a, b in zip(cuts, cuts[1:])]
    pairs = [(flow.at[cut], flow_out.at[cut]) for cut in flows] + [
        (solute, solute_out),
        (solid, solid_in),
        (density, density_in),
        (level, level_in),
        (velocity, velocity_in),
    ]
    copies = [pltpu.make_async_copy(a, b, sems.at[i]) for i, (a, b) in enumerate(pairs)]
    for copy in copies:
        copy.start()

    length = occupied(owner)
    group = lanes(depth) // w
    places = z_places(plan, length, ring)
    shifts = [{n: (w * n + depth - start) & (depth - 1) for n, _, _ in tiles_of(plan)} for start, _ in places]

    def pack(at, first, number, ref):
        def one(i):
            packed = [None] * parts
            for n, y, x in tiles_of(plan):
                tile = ref[first + i, pl.ds(x * ny + y, 8, stride=ny), :]
                for p in range(parts):
                    moved = pltpu.roll(tile, shifts[p][n], 1)
                    packed[p] = moved if n == 0 else jnp.where(group == n, moved, packed[p])
            for p in range(parts):
                outs[p][at + first + i] = packed[p]

        each(number, one, 6)

    for copy, a, b in zip(copies, cuts, cuts[1:]):
        copy.wait()
        pack(0, a, b - a, flow_out)
    for copy in copies[3:]:
        copy.wait()
    pack(NF, 0, NS, solute_out)
    sources = [(solid_in, 0)]
    for s in range(plan.steps):
        t = plan.steps - 1 - s
        sources += [(density_in, t), (level_in, t)] + [(velocity_in, 3 * t + i) for i in range(3)]
    for c, (ref, i) in enumerate(sources):
        for x in range(nx):
            wide[c, x * ny : (x + 1) * ny, :] = ref[i, x * ny : (x + 1) * ny, :].astype(F32)
    pack(SOLID, 0, plan.sent - SOLID, wide)


def faces_kernel(plan, flow, solute, wide, packed, y_low, y_high):
    w, nx, ny = plan.halo, plan.nx, plan.ny
    for at, number, ref in ((0, NF, flow), (NF, NS, solute), (SOLID, plan.sent - SOLID, wide)):

        def row(c, y, ref=ref):
            return ref[c, pl.ds(y, nx, stride=ny), :]

        for k in range(1, w):

            def one(c, k=k, at=at, row=row):
                y_low[plan.base[k] + at + c] = row(c, k - 1)
                y_high[plan.base[k] + at + c] = row(c, ny - k)

            each(min(number, plan.count[k] - at), one)
        for out, sign, y in ((y_low, 1, w - 1), (y_high, -1, ny - w)):
            for j, c in enumerate(plan.last(1, sign)):
                if at <= c < at + number:
                    out[plan.base[w] + j] = row(c - at, y)


def column(plan, ring, owner, received):
    w, depth = plan.halo, plan.depth
    length = occupied(owner)
    lane = lanes(depth)
    live = lane < length
    places = [to for _, to in z_places(plan, length, ring)]
    halos = [((lane - to) & (depth - 1)) < w for to in places]
    shifts = [{n: (to + depth - w * n) & (depth - 1) for n, _, _ in tiles_of(plan)} for to in places]

    def put(tile, slabs, n):
        tile = jnp.where(live, tile, 0.0)
        for slab, halo, shift in zip(slabs, halos, shifts):
            tile = jnp.where(halo, pltpu.roll(slab, shift[n], 1), tile)
        return tile

    return put


def insert_kernel(plan, ring, parts, owner, low, high, *rest):
    received, (y_low, y_high) = rest[:parts], rest[parts:]
    put = column(plan, ring, owner, received)
    w, ny = plan.halo, plan.ny
    tall = plan.nx // 8

    def one(raw, out, j, c, y):
        slabs = [r[c] for r in received]
        for h in range(tall):
            out[j, 8 * h : 8 * h + 8, :] = put(raw[j, 8 * h : 8 * h + 8, :], slabs, y * tall + h)

    for k in range(1, w):

        def both(c, k=k):
            one(low, y_low, plan.base[k] + c, c, k - 1)
            one(high, y_high, plan.base[k] + c, c, ny - k)

        each(plan.count[k], both, 10)
    for raw, out, sign, y in ((low, y_low, 1, w - 1), (high, y_high, -1, ny - w)):
        for j, c in enumerate(plan.last(1, sign)):
            one(raw, out, plan.base[w] + j, c, y)


def inner_kernel(plan, ring, parts, owner, flow, solute, wide, *rest):
    received, (cells, fields, x_low, x_high) = rest[:parts], rest[parts:]
    w, nx, ny, pitch = plan.halo, plan.nx, plan.ny, plan.pitch
    put = column(plan, ring, owner, received)
    for at, number, ref, out, to in (
        (0, NF, flow, cells, 0),
        (NF, NS, solute, cells, NF),
        (SOLID, plan.chan - SOLID, wide, fields, 0),
    ):

        def one(i, sent=True, at=at, ref=ref, out=out, to=to):
            slabs = [r[at + i] for r in received] if sent else []
            for n, y, x in tiles_of(plan):
                tile = ref[i, pl.ds(x * ny + y, 8, stride=ny), :]
                out[to + i, pl.ds(PAD + (w + x) * pitch + w + y, 8, stride=pitch), :] = put(tile, slabs, n)

        within = min(number, plan.sent - at)
        each(within, one, 3)
        each(number - within, lambda i, one=one, within=within: one(within + i, False), 1)

    def row(ref, c, x):
        at = PAD + (w + x) * pitch + w
        return ref[c, at : at + ny, :]

    for k in range(1, w):

        def both(ref, c, j, k=k):
            x_low[plan.base[k] + j] = row(ref, c, k - 1)
            x_high[plan.base[k] + j] = row(ref, c, nx - k)

        channels(cells, fields, plan.count[k], both)
    for slab, sign, x in ((x_low, 1, w - 1), (x_high, -1, nx - w)):
        for j, c in enumerate(plan.last(0, sign)):
            ref, at = (cells, c) if c < SOLID else (fields, c - SOLID)
            slab[plan.base[w] + j] = row(ref, at, x)


def middle_kernel(plan, owner, cells, fields, other, masks):
    w, nx = plan.halo, plan.nx
    prepare(plan, owner, fields, masks, w, w + nx)
    sweep(plan, owner, cells, other, fields, masks, 0, w + 1, w + nx - 1, plan.inside)


def corners_kernel(plan, from_low, from_high, masks, low, high):
    w, nx, ny = plan.halo, plan.nx, plan.ny
    low[...] = jnp.zeros(low.shape, F32)
    high[...] = jnp.zeros(high.shape, F32)
    tall = 2 * w
    for out, sign in ((low, 1), (high, -1)):
        x_last = plan.last(0, sign)
        for k in range(1, w + 1):
            x = k - 1 if sign == 1 else nx - k
            for m in range(1, w + 1):
                for source, row, y_sign in ((from_low, w - m, -1), (from_high, w - 1 + m, 1)):
                    y_last = plan.last(1, y_sign)
                    if k < w and m < w:
                        number = min(plan.count[k], plan.count[m])
                        out[pl.ds(plan.base[k] * tall + row, number, stride=tall), :] = source[
                            pl.ds(plan.base[m] * nx + x, number, stride=nx), :
                        ]
                        continue
                    for c in range(AUX):
                        if (k == w and c not in x_last) or (m == w and c not in y_last):
                            continue
                        to = plan.base[k] + (x_last.index(c) if k == w else c)
                        at = plan.base[m] + (y_last.index(c) if m == w else c)
                        out[to * tall + row : to * tall + row + 1, :] = source[at * nx + x : at * nx + x + 1, :]


def channels(cells, fields, number, body):
    each(SOLID, lambda c: body(cells, c, c), 13)
    each(number - SOLID, lambda c: body(fields, c, SOLID + c))


def insert_layers(plan, cells, fields, axis, parts, put):
    w = plan.halo
    for k in range(1, w + 1):
        for part, sign in zip(parts, (-1, 1)):
            if k < w:
                channels(
                    cells,
                    fields,
                    plan.count[k],
                    lambda ref, c, j, k=k, part=part, sign=sign: put(ref, c, part, plan.base[k] + j, k, sign),
                )
                continue
            for j, c in enumerate(plan.last(axis, sign)):
                ref, at = (cells, c) if c < SOLID else (fields, c - SOLID)
                put(ref, at, part, plan.base[w] + j, k, sign)


def first_kernel(plan, owner, y_low, y_high, x_low, x_high, *refs):
    cells, fields, other, masks = refs[4:]
    w, nx, ny, pitch = plan.halo, plan.nx, plan.ny, plan.pitch

    def put_x(ref, c, part, j, k, sign):
        row = PAD + (w - k if sign < 0 else w + nx - 1 + k) * pitch + w
        ref[c, row : row + ny, :] = part[j]

    insert_layers(plan, cells, fields, 0, (x_low, x_high), put_x)

    def put_y(ref, c, part, j, m, sign):
        row = PAD + w * pitch + (w - m if sign < 0 else w + ny - 1 + m)
        ref[c, pl.ds(row, nx, stride=pitch), :] = part[j]

    insert_layers(plan, cells, fields, 1, (y_low, y_high), put_y)
    prepare(plan, owner, fields, masks, w, w + nx, plan.outside)
    prepare(plan, owner, fields, masks, 0, w)
    prepare(plan, owner, fields, masks, w + nx, plan.wide)
    edges(plan, owner, cells, other, fields, masks, 0, plan.inside)
    sweep(plan, owner, cells, other, fields, masks, 0, w + 1, w + nx - 1, plan.outside)
    buffers = [cells, other]
    for s in range(1, plan.steps - 1):
        sweep(plan, owner, buffers[s % 2], buffers[(s + 1) % 2], fields, masks, s, w + 1 + s, w + nx - 1 - s)


def steps_kernel(plan, owner, cells, fields, other, masks, c_low, c_high, flow_hbm, solute_hbm, flow_out, solute_out, sems):
    w, nx, ny, pitch = plan.halo, plan.nx, plan.ny, plan.pitch

    def put(ref, c, part, j, k, sign):
        row = PAD + (w - k if sign < 0 else w + nx - 1 + k) * pitch
        ref[c, row : row + w, :] = part[j, 0:w, :]
        ref[c, row + w + ny : row + w + ny + w, :] = part[j, w : 2 * w, :]

    insert_layers(plan, cells, fields, 0, (c_low, c_high), put)
    prepare(plan, owner, fields, masks, 0, w, plan.outside)
    prepare(plan, owner, fields, masks, w + nx, plan.wide, plan.outside)
    buffers = [cells, other]
    for s in range(plan.steps - 1):
        source, target = buffers[s % 2], buffers[(s + 1) % 2]
        edges(plan, owner, source, target, fields, masks, s, plan.outside if s == 0 else None)
    s = plan.steps - 1
    source = buffers[s % 2]

    def leave(x):
        return [
            pltpu.make_async_copy(ref.at[:, x], to.at[:, x], sems.at[n, x])
            for n, (ref, to) in enumerate(((flow_out, flow_hbm), (solute_out, solute_hbm)))
        ]

    def last(x):
        for h in range(ny // 8):
            row = PAD + (x + w) * pitch + w + 8 * h

            def write(c, value, h=h):
                if c < NF:
                    flow_out[c, x, 8 * h : 8 * h + 8, :] = value
                else:
                    solute_out[c - NF, x, 8 * h : 8 * h + 8, :] = value

            advance(plan, owner, source, fields, masks, s, row, write)
        for copy in leave(x):
            copy.start()

    each(nx, last, 4)
    for x in range(nx):
        for copy in leave(x):
            copy.wait()


def prepare(plan, owner, fields, masks, from_x, to_x, tiles=None):
    w, nx, ny, depth, pitch = plan.halo, plan.nx, plan.ny, plan.depth, plan.pitch
    length = occupied(owner)
    lane = lanes(depth)
    gx, gy, gz = (lax.axis_index(a) for a in ("gx", "gy", "gz"))
    last_x, last_y, last_z = (lax.axis_size(a) - 1 for a in ("gx", "gy", "gz"))
    above = jnp.where(gz < last_z, w, 0)
    below = jnp.where(gz > 0, w, 0)
    in_z = (lane < length + above) | (lane >= depth - below)
    y_first = jnp.where(gy > 0, 0, w)
    y_end = jnp.where(gy < last_y, ny + 2 * w, w + ny)
    x_first = jnp.where(gx > 0, 0, w)
    x_end = jnp.where(gx < last_x, nx + 2 * w, w + nx)
    sub = lax.broadcasted_iota(jnp.int32, (8, depth), 0)

    def one(i):
        x = from_x + i
        in_x = ((x >= x_first) & (x < x_end)).astype(F32)
        for h in tiles or plan.tiles:
            row = pl.multiple_of(PAD + x * pitch + 8 * h, 8)
            flags = fields[0, pl.ds(row, 8), :]
            y = sub + 8 * h
            masks[0, pl.ds(row, 8), :] = pltpu.roll(flags, depth - 1, 1)
            masks[1, pl.ds(row, 8), :] = pltpu.roll(flags, 1, 1)
            inside = in_z & (y >= y_first) & (y < y_end) & (flags == 0.0)
            masks[2, pl.ds(row, 8), :] = jnp.where(inside, in_x, 0.0)

    each(to_x - from_x, one)


def edges(plan, owner, source, target, fields, masks, s, tiles=None):
    sweep(plan, owner, source, target, fields, masks, s, 1 + s, plan.halo + 1 + s, tiles, plan.nx + plan.halo - 2 * s - 2)


def sweep(plan, owner, source, target, fields, masks, s, from_x, to_x, tiles=None, partner=None):
    pitch = plan.pitch

    def body(i):
        rows = [from_x + i] if partner is None else [from_x + i, from_x + i + partner]
        for x, h in [(x, h) for x in rows for h in tiles or plan.tiles]:
            row = pl.multiple_of(PAD + pitch * x + 8 * h, 8)

            def write(c, value, row=row):
                target[c, pl.ds(row, 8), :] = value

            advance(plan, owner, source, fields, masks, s, row, write)

    each(to_x - from_x, body, 2 if partner is None else 1)


def advance(plan, owner, source, fields, masks, s, row, write):
    depth, pitch = plan.depth, plan.pitch
    def field(ref, c, move=0):
        return ref[c, pl.ds(row + move, 8), :]

    blocked = {}

    def reads(first, number):
        result = []
        for i in range(number):
            sx, sy, sz = FLOW_DIRS[i]
            if i == 0:
                result.append(field(source, first))
                continue
            move = sx * pitch + sy
            near = field(source, first + i, move)
            if sz:
                near = pltpu.roll(near, (depth - sz) % depth, 1)
            if i not in blocked:
                flags = field(fields, 0, move) if sz == 0 else field(masks, 0 if sz == 1 else 1, move)
                blocked[i] = flags != 0.0
            result.append(jnp.where(blocked[i], field(source, first + OPPOSITE[i]), near))
        return result

    valid = field(masks, 2)
    if s == plan.steps - 1:
        valid = jnp.where(lanes(depth) < occupied(owner), valid, 0.0)
    aux = AUX - SOLID + NA * s
    density, level, ux, uy, uz = (field(fields, aux + n) for n in range(NA))

    h = reads(NF, NS)
    px, py, pz = h[1] - h[2], h[3] - h[4], h[5] - h[6]
    p0 = 0.25 * h[0] + 0.125 * ((h[1] + h[2]) + (h[3] + h[4]) + (h[5] + h[6]))
    grown = (1.0 + level) * (1.0 + level)
    density = jnp.maximum(density, 0.5)
    inverse = 1.0 / (grown * density)
    uptake = langmuir_rate * (density * inverse)
    common = valid * (
        (solute_omega - uptake) * p0 + (solute_omega * 0.5) * (px * ux + py * uy + pz * uz)
    )
    keep = (1.0 - solute_omega) * valid
    for i in range(NS):
        write(NF + i, keep * h[i] + common)
    factor = (0.5 * solute_omega) * level * (grown * inverse)
    fx, fy, fz = factor * px, factor * py, factor * pz

    g = reads(0, NF)
    a = {i: g[i] + g[i + 1] for i in range(1, NF, 2)}
    d = {i: g[i] - g[i + 1] for i in range(1, NF, 2)}
    m1x = (d[1] + d[1]) + (d[7] + d[9]) + (d[11] + d[13])
    m1y = (d[3] + d[3]) + (d[7] - d[9]) + (d[15] + d[17])
    m1z = (d[5] + d[5]) + (d[11] - d[13]) + (d[15] - d[17])
    exy, exz, eyz = a[7] + a[9], a[11] + a[13], a[15] + a[17]
    tx, ty, tz = a[1] + a[1], a[3] + a[3], a[5] + a[5]
    mxx, myy, mzz = tx + exy + exz, ty + exy + eyz, tz + exz + eyz
    mxy, mxz, myz = a[7] - a[9], a[11] - a[13], a[15] - a[17]
    m0 = 12.0 * g[0] + (tx + ty + tz) + (exy + exz + eyz)
    qx = mxx * ux + mxy * uy + mxz * uz
    qy = mxy * ux + myy * uy + myz * uz
    qz = mxz * ux + myz * uy + mzz * uz
    square = ux * ux + uy * uy + uz * uz
    scaled = flow_omega / 36.0
    zero = m0 * (scaled + (1.5 * scaled) * square) - (4.5 * scaled) * (qx * ux + qy * uy + qz * uz)
    zero = valid * (zero - (fx * ux + fy * uy + fz * uz))
    bx = valid * ((3.0 * scaled) * (m1x + 3.0 * qx - m0 * ux) + fx)
    by = valid * ((3.0 * scaled) * (m1y + 3.0 * qy - m0 * uy) + fy)
    bz = valid * ((3.0 * scaled) * (m1z + 3.0 * qz - m0 * uz) + fz)
    keep = (1.0 - flow_omega) * valid
    write(0, keep * g[0] + zero)
    moves = {1: bx, 3: by, 5: bz, 7: bx + by, 9: bx - by, 11: bx + bz, 13: bx - bz, 15: by + bz, 17: by - bz}
    for i, move in moves.items():
        write(i, keep * g[i] + (zero + move))
        write(i + 1, keep * g[i + 1] + (zero - move))


VMEM = pl.BlockSpec(memory_space=pltpu.VMEM)
SMEM = pl.BlockSpec(memory_space=pltpu.SMEM)
ANY = pl.BlockSpec(memory_space=pl.ANY)
HBM = pl.BlockSpec(memory_space=pltpu.HBM)


def call(kernel, ins, outs, name, cost, scratch=(), limit=VMEM_LIMIT, place=VMEM, aliases={}):
    return pl.pallas_call(
        kernel,
        in_specs=ins,
        out_shape=outs,
        out_specs=[place] * len(outs),
        input_output_aliases=aliases,
        scratch_shapes=list(scratch),
        name=name,
        cost_estimate=pl.CostEstimate(flops=cost, bytes_accessed=1 << 23, transcendentals=0),
        compiler_params=pltpu.CompilerParams(vmem_limit_bytes=limit),
    )


def per_device(flow_adjoint, solute_adjoint, flow_density, flow_velocity, solute_level, solid, owner):
    steps = flow_density.shape[0]
    nx, ny, depth = solid.shape
    plan = Plan(steps, nx, ny, depth)
    ring = lax.axis_size("gz")
    w = plan.halo
    arguments = (flow_adjoint, solute_adjoint, flow_density, flow_velocity, solute_level, solid)
    fields = [f.reshape(-1, nx * ny, depth) for f in arguments]
    owner, *fields = (pltpu.with_memory_space_constraint(f, pltpu.HBM) for f in (owner, *fields))

    def move(value, axis, by):
        size = lax.axis_size(axis)
        return lax.ppermute(value, axis, [(i, i + by) for i in range(size) if 0 <= i + by < size])

    parts = 1 if ring == 2 else 2

    def like(channels):
        return jax.ShapeDtypeStruct((channels, nx * ny, depth), F32)

    *packed, flow, solute, wide = call(
        functools.partial(pack_kernel, plan, ring, parts),
        [SMEM] + [HBM] * 6,
        [jax.ShapeDtypeStruct((plan.sent, 8, depth), F32)] * parts + [like(NF), like(NS), like(plan.chan - SOLID)],
        "pack_column",
        1 << 22,
        [pltpu.VMEM(f.shape, f.dtype) for f in fields[2:]] + [pltpu.SemaphoreType.DMA((8,))],
    )(owner, *fields)
    loaded = (flow, solute, wide)
    if ring == 2:
        received = [lax.ppermute(packed[0], "gz", [(0, 1), (1, 0)])]
    else:
        received = [move(packed[0], "gz", 1), move(packed[1], "gz", -1)]

    slab = [jax.ShapeDtypeStruct((plan.slab, nx, depth), F32)] * 2
    raw = call(functools.partial(faces_kernel, plan), [VMEM] * 3 + [ANY], slab, "faces", 1 << 24)(
        *loaded, packed[0]
    )
    y_low, y_high = call(
        functools.partial(insert_kernel, plan, ring, parts), [SMEM] + [VMEM] * (2 + parts), slab, "insert", 1 << 22, (), 24 << 20
    )(owner, *raw, *received)
    from_y_low = move(y_high, "gy", 1)
    from_y_high = move(y_low, "gy", -1)
    state = jax.ShapeDtypeStruct((SOLID, plan.height, depth), F32)
    saved = jax.ShapeDtypeStruct((plan.chan - SOLID, plan.height, depth), F32)
    flags = jax.ShapeDtypeStruct((3, plan.height, depth), F32)
    cells, kept, x_low, x_high = call(
        functools.partial(inner_kernel, plan, ring, parts),
        [SMEM] + [VMEM] * (3 + parts),
        [state, saved] + [jax.ShapeDtypeStruct((plan.slab, ny, depth), F32)] * 2,
        "inner",
        1 << 24,
    )(owner, *loaded, *received)
    from_x_low = move(x_high, "gx", 1)
    from_x_high = move(x_low, "gx", -1)
    other, masks = call(
        functools.partial(middle_kernel, plan), [SMEM] + [VMEM] * 2, [state, flags], "middle", 1 << 24, (), 8 << 20
    )(owner, cells, kept)

    def rows(value):
        return value.reshape(-1, depth)

    corner = jax.ShapeDtypeStruct((plan.slab * 2 * w, depth), F32)
    c_low, c_high = call(
        functools.partial(corners_kernel, plan), [VMEM] * 2 + [ANY], [corner, corner], "corners", 1 << 20
    )(rows(from_y_low), rows(from_y_high), masks)
    shape = (plan.slab, 2 * w, depth)
    from_c_low = move(c_high, "gx", 1).reshape(shape)
    from_c_high = move(c_low, "gx", -1).reshape(shape)
    assembled = [pltpu.with_memory_space_constraint(a, pltpu.VMEM) for a in (cells, kept, other, masks)]
    assembled = call(
        functools.partial(first_kernel, plan),
        [SMEM] + [VMEM] * 8,
        [state, saved, state, flags],
        "first",
        1 << 26,
        (),
        8 << 20,
        aliases={5: 0, 6: 1, 7: 2, 8: 3},
    )(owner, from_y_low, from_y_high, from_x_low, from_x_high, *assembled)
    flow, solute = call(
        functools.partial(steps_kernel, plan),
        [SMEM] + [VMEM] * 6,
        [jax.ShapeDtypeStruct(flow_adjoint.shape, F32), jax.ShapeDtypeStruct(solute_adjoint.shape, F32)],
        "steps",
        1 << 28,
        [
            pltpu.VMEM((NF, nx, ny, depth), F32),
            pltpu.VMEM((NS, nx, ny, depth), F32),
            pltpu.SemaphoreType.DMA((2, nx)),
        ],
        10 << 20,
        ANY,
    )(owner, *assembled, from_c_low, from_c_high)
    return (flow, solute)


def solution(mesh):
    in_specs = (
        P(None, "gx", "gy", "gz"),
        P(None, "gx", "gy", "gz"),
        P(None, "gx", "gy", "gz"),
        P(None, None, "gx", "gy", "gz"),
        P(None, "gx", "gy", "gz"),
        P("gx", "gy", "gz"),
        P(),
    )
    out_specs = (P(None, "gx", "gy", "gz"), P(None, "gx", "gy", "gz"))
    return jax.shard_map(
        per_device, mesh=mesh, in_specs=in_specs, out_specs=out_specs, check_vma=False
    )
```
